32 devices in a mesh: gx: 4 (over y, core), gy: 8 (over z, x).
Axes of the slice: x: 2, y: 2, z: 4, core: 2. Of those that a mesh axis runs over, the one named last changes fastest.
Arguments:
- patches: bfloat16 [1536, 49, 512], P(('gx', 'gy')), may hold values from -6 to 6
- regions: bfloat16 [1536, 512], P(('gx', 'gy')), may hold values from -6 to 6
- send_order: int32 [32, 48], replicated, may hold values from 0 to 47, each once within a row
- image_windows: int32 [48], replicated, may hold values from 1 to 768, 1536 in all
- attn_gain: float32 [512], replicated, may hold values from 0.1 to 1.9
- attn_shift: float32 [512], replicated, may hold values from -3 to 3
- w_qkv: bfloat16 [512, 1536], replicated, may hold values from -0.25 to 0.25
- w_out: bfloat16 [512, 512], replicated, may hold values from -1 to 1
- b_out: float32 [512], replicated, may hold values from -2 to 2
- mlp_gain: float32 [512], replicated, may hold values from 0.1 to 1.9
- mlp_shift: float32 [512], replicated, may hold values from -3 to 3
- w_up: bfloat16 [512, 2048], replicated, may hold values from -0.25 to 0.25
- b_up: float32 [2048], replicated, may hold values from -3 to 3
- w_down: bfloat16 [2048, 512], replicated, may hold values from -0.125 to 0.125
- b_down: float32 [512], replicated, may hold values from -2 to 2
- upstream_patches: bfloat16 [1536, 49, 512], P(('gx', 'gy')), may hold values from -6 to 6
- upstream_regions: bfloat16 [1536, 512], P(('gx', 'gy')), may hold values from -6 to 6
Outputs:
- out_patches: bfloat16 [1536, 49, 512], P(('gx', 'gy'))
- out_regions: bfloat16 [1536, 512], P(('gx', 'gy'))
- patch_grad: bfloat16 [1536, 49, 512], P(('gx', 'gy'))
- region_grad: bfloat16 [1536, 512], P(('gx', 'gy'))
- attn_gain_grad: float32 [512], replicated
- attn_shift_grad: float32 [512], replicated
- w_qkv_grad: float32 [512, 1536], replicated
- w_out_grad: float32 [512, 512], replicated
- b_out_grad: float32 [512], replicated
- mlp_gain_grad: float32 [512], replicated
- mlp_shift_grad: float32 [512], replicated
- w_up_grad: float32 [512, 2048], replicated
- b_up_grad: float32 [2048], replicated
- w_down_grad: float32 [2048, 512], replicated
- b_down_grad: float32 [512], replicated
The draws below stay inside these ranges and needn't reach their ends.
Inputs may be any that keep to these rules, and one draw needn't show every extreme that they name: `send_order`: each row is an ordering of its device's 48 arriving windows. `image_windows`: the sizes add up to 1536; the largest image has exactly 768 windows.
All inputs are finite; a program needn't handle non-finite values.
Results may differ from the reference program's by a relative error of at most 0.025.
Values may be sent and summed in bfloat16 or wider, within the bound.
A program may use at most 384 MiB of HBM per device.

```python
import math
import jax
import jax.numpy as jnp
import numpy as np
from jax import lax

D = 512
HEADS = 16
HEAD = 32
FF = 2048
WIN_TOK = 49
WIN_DEV = 48
WINDOWS = 1536
IMAGES = 48
N_GX = 4
N_GY = 8


def block_levels(stream_key, shape, cuts, low, largest):
    loudness = 1.0
    for dim, shards_of in cuts:
        heights = jax.random.uniform(jax.random.fold_in(jax.random.fold_in(stream_key, 6), dim), (shards_of,), jnp.float32, low / len(cuts), largest / len(cuts))
        loudness = loudness * jnp.repeat(jnp.exp(heights), shape[dim] // shards_of).reshape((-1,) + (1,) * (len(shape) - 1 - dim))
    return loudness


def profile(count, total, reach, skew):
    weights = [(1 << 20) // math.isqrt(grade ** skew) + 1 for grade in range(2, count + 1)]
    surplus, counts = total - reach - (count - 1), [1] * (count - 1)
    while surplus > 0:
        free = [i for i in range(count - 1) if counts[i] < reach]
        whole, budget = sum([weights[i] for i in free]), surplus
        for i in free:
            addition = min(reach - counts[i], max(1, budget * weights[i] // whole), surplus)
            counts[i] = counts[i] + addition
            surplus = surplus - addition
    return np.array([reach] + counts)


def uneven(stream_key, amount, total, bound, lean):
    if amount == 2:
        one = jax.random.randint(stream_key, (), max(1, total - bound), min(bound, total - 1) + 1)
        return jnp.stack([one, total - one])
    lengths = jnp.asarray(profile(amount, total, bound, lean), jnp.int32)
    couples = (amount - 1) // 2
    donor, sink = lengths[1:1 + 2 * couples:2], lengths[2:2 + 2 * couples:2]
    margin = jnp.minimum(donor - 1, bound - sink)
    passed = jax.random.randint(jax.random.fold_in(stream_key, 1), (couples,), 0, 1 << 20) % (margin + 1)
    lengths = lengths.at[1:1 + 2 * couples:2].set(donor - passed).at[2:2 + 2 * couples:2].set(sink + passed)
    return lengths[jax.random.permutation(jax.random.fold_in(stream_key, 2), amount)]


def centred(key, dims, spread, most, shards=(), held_as=jnp.bfloat16):
    values = spread * jax.random.normal(key, dims, jnp.float32)
    if shards:
        values = values * block_levels(key, dims, shards, -0.22, 0.18)
    return jnp.clip(values, -most, most).astype(held_as)


def setup_inputs(seed: int = 0) -> dict:
    splits = jax.random.split(jax.random.key(seed), 18)
    patches = centred(splits[0], (WINDOWS, WIN_TOK, D), 1.0, 6.0, ((0, 32),))
    regions = centred(splits[1], (WINDOWS, D), 1.0, 6.0, ((0, 32),))
    send_order = jax.vmap(lambda own: jax.random.permutation(own, WIN_DEV))(jax.random.split(splits[2], (N_GX * N_GY))).reshape((N_GX * N_GY, WIN_DEV)).astype(jnp.int32)
    image_windows = uneven(splits[3], IMAGES, WINDOWS, WINDOWS // 2, 2).astype(jnp.int32)
    attn_gain = jnp.clip(1.0 + 0.18 * jax.random.normal(splits[4], (D,), jnp.float32), 0.1, 1.9)
    attn_shift = centred(splits[5], (D,), 0.5, 3.0, (), jnp.float32)
    w_qkv = centred(splits[6], (D, 3 * D), D ** -0.5, 0.25)
    w_out = centred(splits[7], (D, D), (D // 16) ** -0.5, 1.0)
    b_out = centred(splits[8], (D,), 0.3, 2.0, (), jnp.float32)
    mlp_gain = jnp.clip(1.0 + 0.18 * jax.random.normal(splits[9], (D,), jnp.float32), 0.1, 1.9)
    mlp_shift = centred(splits[10], (D,), 0.5, 3.0, (), jnp.float32)
    w_up = centred(splits[11], (D, FF), D ** -0.5, 0.25)
    b_up = centred(splits[12], (FF,), 0.5, 3.0, (), jnp.float32)
    w_down = centred(splits[13], (FF, D), FF ** -0.5, 0.125)
    b_down = centred(splits[14], (D,), 0.3, 2.0, (), jnp.float32)
    upstream_patches = centred(splits[15], (WINDOWS, WIN_TOK, D), 1.0, 6.0, ((0, 32),))
    upstream_regions = centred(splits[16], (WINDOWS, D), 1.0, 6.0, ((0, 32),))
    return dict(patches=patches, regions=regions, send_order=send_order, image_windows=image_windows, attn_gain=attn_gain, attn_shift=attn_shift, w_qkv=w_qkv, w_out=w_out, b_out=b_out, mlp_gain=mlp_gain, mlp_shift=mlp_shift, w_up=w_up, b_up=b_up, w_down=w_down, b_down=b_down, upstream_patches=upstream_patches, upstream_regions=upstream_regions)


@jax.custom_vjp
def low(v):
    return lax.optimization_barrier(v.astype(jnp.bfloat16)).astype(jnp.float32)

@jax.custom_vjp
def low_back(v):
    return v

def low_keep(v):
    return (low(v), None)

def low_pass(kept, grad):
    return (grad,)

def back_keep(v):
    return (v, None)

def back_low(kept, grad):
    return (low(grad),)
low.defvjp(low_keep, low_pass)
low_back.defvjp(back_keep, back_low)
EPS = 1e-05
HIGH = lax.Precision.HIGHEST

def both_ways(values):
    return low_back(low(values))

def layer_norm(values, scales, offset):
    average = lax.optimization_barrier(jnp.mean(values, axis=-1, keepdims=True))
    centered = values - average
    variance = lax.optimization_barrier(jnp.mean(centered * centered, axis=-1, keepdims=True))
    return centered * lax.rsqrt(variance + EPS) * scales + offset

def source_rows(send_order):
    devices, per_dev = send_order.shape
    per_block = per_dev // N_GX
    target = jnp.arange(devices * per_dev, dtype=jnp.int32)
    dealt_dev = target // per_dev
    within = target % per_dev
    source_dev = within // per_block * N_GY + dealt_dev % N_GY
    local_slot = send_order[source_dev, dealt_dev // N_GY * per_block + within % per_block]
    return (source_dev * per_dev + local_slot).astype(jnp.int32)

def image_ids(image_windows, windows):
    bounds = jnp.cumsum(image_windows).astype(jnp.int32)
    places = jnp.arange(windows, dtype=jnp.int32)
    return lax.optimization_barrier(jnp.sum((places[:, None] >= bounds[None, :]).astype(jnp.int32), axis=1, dtype=jnp.int32))

def reference(patches, regions, send_order, image_windows, attn_gain, attn_shift, w_qkv, w_out, b_out, mlp_gain, mlp_shift, w_up, b_up, w_down, b_down, upstream_patches, upstream_regions):
    windows = regions.shape[0]
    seq_len = WIN_TOK + 1
    scaling = HEAD ** (-0.5)
    source = source_rows(send_order)
    image_of = jnp.take(image_ids(image_windows, windows), source)
    region_rows = math.gcd(windows, 512)
    window_rows = math.gcd(windows, 32)

    def forward(patch_f, region_f, attn_gain, attn_shift, w_qkv, w_out, b_out, mlp_gain, mlp_shift, w_up, b_up, w_down, b_down):
        tokens_in = jnp.take(patch_f, source, axis=0)
        region_in = jnp.take(region_f, source, axis=0)
        normed = low(layer_norm(region_in, attn_gain, attn_shift))
        qkv = both_ways(jnp.dot(normed, w_qkv, precision=HIGH))
        queries = qkv[:, :D].reshape(windows, HEADS, HEAD)
        keys_all = qkv[:, D:2 * D].reshape(windows, HEADS, HEAD)
        vals_all = qkv[:, 2 * D:].reshape(windows, HEADS, HEAD)

        def region_block(pieces):
            query_blk, image_blk = pieces
            scores = jnp.einsum('qhe,khe->hqk', query_blk, keys_all, precision=HIGH) * scaling
            scores = low_back(jnp.where(image_blk[None, :, None] == image_of[None, None, :], scores, -1e+30))
            probs = jax.nn.softmax(scores, axis=-1)
            return jnp.einsum('hqk,khe->qhe', low(probs), vals_all, precision=HIGH)
        blocks = windows // region_rows
        attended = lax.map(jax.checkpoint(region_block), (queries.reshape(blocks, region_rows, HEADS, HEAD), image_of.reshape(blocks, region_rows)))
        attended = both_ways(attended.reshape(windows, D))
        region_mid = region_in + low_back(jnp.dot(attended, w_out, precision=HIGH) + b_out)

        def window_block(pieces):
            patch_blk, region_blk = pieces
            count = patch_blk.shape[0]
            stacked = jnp.concatenate([region_blk[:, None, :], patch_blk], axis=1)
            normed_w = low(layer_norm(stacked, attn_gain, attn_shift))
            qkv_w = both_ways(jnp.einsum('wtd,df->wtf', normed_w, w_qkv, precision=HIGH))
            local_query = qkv_w[..., :D].reshape(count, seq_len, HEADS, HEAD)
            local_key = qkv_w[..., D:2 * D].reshape(count, seq_len, HEADS, HEAD)
            local_value = qkv_w[..., 2 * D:].reshape(count, seq_len, HEADS, HEAD)
            scores_w = low_back(jnp.einsum('wqhe,wkhe->whqk', local_query, local_key, precision=HIGH) * scaling)
            probs_w = jax.nn.softmax(scores_w, axis=-1)
            mixed_rows = both_ways(jnp.einsum('whqk,wkhe->wqhe', low(probs_w), local_value, precision=HIGH).reshape(count, seq_len, D))
            middle = stacked + low_back(jnp.einsum('wtd,df->wtf', mixed_rows, w_out, precision=HIGH) + b_out)
            normed_m = low(layer_norm(middle, mlp_gain, mlp_shift))
            hidden = low_back(jnp.einsum('wtd,df->wtf', normed_m, w_up, precision=HIGH) + b_up)
            active = low(jax.nn.gelu(hidden, approximate=False))
            return middle + low_back(jnp.einsum('wtf,fd->wtd', active, w_down, precision=HIGH) + b_down)
        nblocks = windows // window_rows
        result = lax.map(jax.checkpoint(window_block), (tokens_in.reshape(nblocks, window_rows, WIN_TOK, D), region_mid.reshape(nblocks, window_rows, D)))
        return result.reshape(windows, seq_len, D)
    floats = tuple((item.astype(jnp.float32) for item in (patches, regions, attn_gain, attn_shift, w_qkv, w_out, b_out, mlp_gain, mlp_shift, w_up, b_up, w_down, b_down)))
    result, pullback = jax.vjp(forward, *floats)
    upstream = jnp.concatenate([upstream_regions[:, None, :], upstream_patches], axis=1).astype(jnp.float32)
    grads = pullback(upstream)
    output = result.astype(jnp.bfloat16)
    return (output[:, 1:], output[:, 0], grads[0].astype(jnp.bfloat16), grads[1].astype(jnp.bfloat16), grads[2], grads[3], grads[4], grads[5], grads[6], grads[7], grads[8], grads[9], grads[10], grads[11], grads[12])
```

```python
import functools
import math

import jax
import jax.numpy as jnp
from jax import lax
from jax.experimental import pallas as pl
from jax.experimental.pallas import tpu as pltpu
from jax.sharding import PartitionSpec as P

HEADS = 16
EPS = 1e-05
F32 = jnp.float32
BF16 = jnp.bfloat16
LOG2E = 1.4426950408889634
VMEM_LIMIT = 60 * 1024 * 1024
HIGH = lax.Precision.HIGHEST
LANES = 128
SEG = 64


def mm(a, b):
    return lax.dot_general(a, b, (((1,), (0,)), ((), ())), preferred_element_type=F32)


def mm_nt(a, b):
    return lax.dot_general(a, b, (((1,), (1,)), ((), ())), preferred_element_type=F32)


def mm_tn(a, b):
    return lax.dot_general(a, b, (((0,), (0,)), ((), ())), preferred_element_type=F32)


def norm_stats(v):
    average = jnp.mean(v, axis=-1, keepdims=True)
    centered = v - average
    variance = jnp.mean(centered * centered, axis=-1, keepdims=True)
    rstd = lax.rsqrt(variance + EPS)
    return centered * rstd, rstd


def norm_back(hat, rstd, gain, dn):
    dhat = dn * gain
    m1 = jnp.mean(dhat, axis=-1, keepdims=True)
    m2 = jnp.mean(dhat * hat, axis=-1, keepdims=True)
    return rstd * (dhat - m1 - hat * m2)


def colsum(v):
    return jnp.sum(v, axis=0, keepdims=True)


def gelu_both(u):
    a = jnp.abs(u)
    d = 1.0 + (0.3275911 * 0.7071067811865476) * a
    r = pl.reciprocal(d, approx=True)
    t = r * (2.0 - d * r)
    e = jnp.exp2((u * u) * (-0.5 * LOG2E))
    poly = t * (
        0.127414796
        + t * (-0.142248368 + t * (0.7107068705 + t * (-0.7265760135 + t * 0.5307027145)))
    )
    tail = poly * e
    cdf = jnp.where(u >= 0.0, 1.0 - tail, tail)
    return u * cdf, cdf + u * (e * 0.3989422804014327)


def head_masks(rows, head_dim):
    lane = lax.broadcasted_iota(jnp.int32, (rows, LANES), 1)
    return [(lane // head_dim) == h for h in range(LANES // head_dim)]


def spread(v, masks):
    zero = jnp.zeros_like(v)
    return jnp.concatenate([jnp.where(m, v, zero) for m in masks], axis=0)


def unspread(full, rows, stride, masks):
    out = full[(len(masks) - 1) * stride : (len(masks) - 1) * stride + rows]
    for h in range(len(masks) - 2, -1, -1):
        out = jnp.where(masks[h][:rows], full[h * stride : h * stride + rows], out)
    return out


def one_hot(code_col, count):
    rows = code_col.shape[0]
    return (lax.broadcasted_iota(jnp.int32, (rows, count), 1) == code_col).astype(F32).astype(BF16)


def one_hot_t(code_row, count):
    rows = code_row.shape[1]
    return (lax.broadcasted_iota(jnp.int32, (count, rows), 0) == code_row).astype(F32).astype(BF16)


def whole(*shape):
    return pl.BlockSpec(shape, lambda *_: (0,) * len(shape))


class Sizes:
    def __init__(self, per_dev, patch_tokens, width, count_gx):
        self.w = per_dev
        self.tok = patch_tokens
        self.d = width
        self.nb = count_gx
        self.k = per_dev // count_gx
        step = 16 // math.gcd(16, self.k)
        self.pos = -(-(patch_tokens + 1) // step) * step
        self.gp = step
        while (self.gp * self.k) % 16:
            self.gp *= 2
        self.ng = self.pos // self.gp
        self.r = self.pos * self.k
        self.wide = 56 * self.k
        self.hd = width // HEADS
        self.groups = width // LANES
        self.per_group = LANES // self.hd
        self.chunk = self.r // 3 if self.r % 48 == 0 else self.r


def params(**kw):
    return pltpu.CompilerParams(vmem_limit_bytes=VMEM_LIMIT, **kw)


def pack_kernel(z, x_ref, first_ref, code_ref, out_ref):
    sel = one_hot(code_ref[...], z.gp * z.w)
    for g in range(z.ng):
        pack_group(z, g, sel, x_ref, first_ref, out_ref)


def pack_group(z, g, sel, x_ref, first_ref, out_ref):
    pieces = []
    for p in range(g * z.gp, (g + 1) * z.gp):
        if p == 0:
            pieces.append(jnp.zeros((z.w, z.d), BF16) if first_ref is None else first_ref[...])
        elif p <= z.tok:
            pieces.append(x_ref[p - 1])
        else:
            pieces.append(jnp.zeros((z.w, z.d), BF16))
    got = mm(sel, jnp.concatenate(pieces, axis=0)).astype(BF16)
    rows = z.gp * z.k
    for c in range(z.nb):
        out_ref[c, g * rows : (g + 1) * rows, :] = got[c * rows : (c + 1) * rows]


def unpack_group(z, g, sel_t, packed_ref, out_ref, first_ref):
    rows = z.gp * z.k
    src = jnp.concatenate([packed_ref[c, g * rows : (g + 1) * rows, :] for c in range(z.nb)], axis=0)
    got = mm(sel_t, src).astype(BF16)
    for i in range(z.gp):
        p = g * z.gp + i
        piece = got[i * z.w : (i + 1) * z.w]
        if p == 0:
            if first_ref is not None:
                first_ref[...] = piece
        elif p <= z.tok:
            out_ref[p - 1] = piece


def unpack_kernel(z, *refs):
    packed, code_ref, out_ref, first_ref = refs[: z.nb], refs[z.nb], refs[z.nb + 1], refs[z.nb + 2]
    sel_t = one_hot_t(code_ref[...], z.gp * z.w)
    rows = z.gp * z.k
    for g in range(z.ng):
        src = jnp.concatenate([packed[c][g * rows : (g + 1) * rows, :] for c in range(z.nb)], axis=0)
        got = mm(sel_t, src).astype(BF16)
        for i in range(z.gp):
            p = g * z.gp + i
            piece = got[i * z.w : (i + 1) * z.w]
            if p == 0:
                first_ref[...] = piece
            elif p <= z.tok:
                out_ref[p - 1] = piece


def qkv_kernel(z, x_ref, code_ref, gain_ref, shift_ref, w_ref, xp_ref, qkv_ref):
    sel = one_hot(code_ref[...], z.gp * z.w)
    for g in range(z.ng):
        pack_group(z, g, sel, x_ref, None, xp_ref)
    per = z.r // z.chunk

    def body(i, _):
        c, rows = i // per, pl.ds(pl.multiple_of((i % per) * z.chunk, 16), z.chunk)
        hat, _ = norm_stats(xp_ref[c, rows, :].astype(F32))
        nt = (hat * gain_ref[...] + shift_ref[...]).astype(BF16)
        qkv_ref[c, rows, :] = mm(nt, w_ref[...]).astype(BF16)
        return 0

    lax.fori_loop(0, z.nb * per, body, 0)


def region_fwd_kernel(
    z, kc, all_ref, own_ref, imgk_ref, imgq_ref, ord_ref, gain_ref, shift_ref, w_ref, wo_ref, bo_ref,
    r2_ref, p_ref, kv_ref, nr_ref, q_ref, o_ref, of_ref, nown_ref, s_ref,
):
    n = all_ref.shape[0]
    nq = HEADS * z.w
    hat, _ = norm_stats(own_ref[...].astype(F32))
    nown = (hat * gain_ref[...] + shift_ref[...]).astype(BF16)
    nown_ref[...] = nown
    q = mm(nown, w_ref[:, : z.d]).astype(BF16)
    q_ref[...] = q
    lane = lax.broadcasted_iota(jnp.int32, (z.w, z.d), 1) // z.hd
    zero = jnp.zeros_like(q)
    qbd = jnp.concatenate([jnp.where(lane == h, q, zero) for h in range(HEADS)], axis=0)
    scale = z.hd ** (-0.5) * LOG2E

    def scores(i, top):
        rows = pl.ds(pl.multiple_of(i * kc, kc), kc)
        hat, _ = norm_stats(all_ref[rows, :].astype(F32))
        nr = (hat * gain_ref[...] + shift_ref[...]).astype(BF16)
        nr_ref[rows, :] = nr
        kv = mm(nr, w_ref[:, z.d :]).astype(BF16)
        kv_ref[rows, :] = kv
        s = mm_nt(kv[:, : z.d], qbd) * scale
        s = jnp.where(imgk_ref[rows, :] == imgq_ref[...], s, -1e30)
        s_ref[rows, :] = s
        return jnp.maximum(top, jnp.max(s, axis=0, keepdims=True))

    top = lax.fori_loop(0, n // kc, scores, jnp.full((1, nq), -1e30, F32))

    def weigh(i, total):
        rows = pl.ds(pl.multiple_of(i * kc, kc), kc)
        p = jnp.exp2(s_ref[rows, :] - top)
        s_ref[rows, :] = p
        return total + jnp.sum(p, axis=0, keepdims=True)

    total = lax.fori_loop(0, n // kc, weigh, jnp.zeros((1, nq), F32))
    inverse = 1.0 / total

    def attend(i, acc):
        rows = pl.ds(pl.multiple_of(i * kc, kc), kc)
        p = (s_ref[rows, :] * inverse).astype(BF16)
        p_ref[rows, :] = p
        return acc + mm_tn(p, kv_ref[rows, z.d :])

    full = lax.fori_loop(0, n // kc, attend, jnp.zeros((nq, z.d), F32))
    o = full[(HEADS - 1) * z.w :]
    for h in range(HEADS - 2, -1, -1):
        o = jnp.where(lane == h, full[h * z.w : (h + 1) * z.w], o)
    of_ref[...] = o
    o = o.astype(BF16)
    o_ref[...] = o
    r2 = own_ref[...].astype(F32) + mm(o, wo_ref[...]) + bo_ref[...]
    sel = one_hot(ord_ref[...], z.w).astype(F32)
    r2 = jnp.dot(sel, r2, precision=HIGH, preferred_element_type=F32)
    for c in range(z.nb):
        r2_ref[c] = r2[c * z.k : (c + 1) * z.k]


def local_fwd_kernel(
    z, qkv_ref, xp_ref, r2_ref, gain_ref, shift_ref, w_ref, wo_ref, bo_ref,
    t2_ref, p_ref, qw_ref, o_ref, qs, os,
):
    tiles = 3 * z.groups
    for j in range(tiles):
        qs[j, : z.r, :] = qkv_ref[0, :, j * LANES : (j + 1) * LANES].astype(F32)
        if z.wide > z.r:
            qs[j, z.r :, :] = jnp.zeros((z.wide - z.r, LANES), F32)
    hat, _ = norm_stats(r2_ref[0])
    nt = (hat * gain_ref[...] + shift_ref[...]).astype(BF16)
    reg = mm(nt, w_ref[...]).astype(BF16).astype(F32)
    for j in range(tiles):
        qs[j, : z.k, :] = reg[:, j * LANES : (j + 1) * LANES]
    masks = head_masks(SEG, z.hd)
    pad = jnp.zeros((SEG - 56, LANES), F32)
    valid = lax.broadcasted_iota(jnp.int32, (56, z.per_group * SEG), 0) < z.tok + 1
    scale = z.hd ** (-0.5) * LOG2E

    def window(w, _):
        def load(j):
            rows = qs[j, pl.ds(w, 56, stride=z.k), :]
            got = jnp.concatenate([rows, pad], axis=0).astype(BF16)
            qw_ref[w, j] = got
            return got

        for g in range(z.groups):
            q, k, v = load(g), load(z.groups + g), load(2 * z.groups + g)
            s = mm_nt(k, spread(q, masks))[:56]
            s = jnp.where(valid, s, -1e30)
            p = jnp.exp2((s - jnp.max(s, axis=0, keepdims=True)) * scale)
            p = p * (1.0 / jnp.sum(p, axis=0, keepdims=True))
            p = jnp.concatenate([p, jnp.zeros((SEG - 56, z.per_group * SEG), F32)], axis=0).astype(BF16)
            p_ref[w, g] = p
            full = mm_tn(p, v)
            os[g, pl.ds(w, 56, stride=z.k), :] = unspread(full, 56, SEG, masks)
        return 0

    lax.fori_loop(0, z.k, window, 0)
    for i in range(z.r // z.chunk):
        rows = slice(i * z.chunk, (i + 1) * z.chunk)
        o = jnp.concatenate([os[g, rows, :] for g in range(z.groups)], axis=1).astype(BF16)
        o_ref[0, rows, :] = o
        t2_ref[0, rows, :] = xp_ref[0, rows, :].astype(F32) + mm(o, wo_ref[...]) + bo_ref[...]
    t2_ref[0, : z.k, :] = t2_ref[0, : z.k, :] + r2_ref[0]


def mlp_kernel(
    z, parts, t2_ref, e_ref, gain_ref, shift_ref, wu_ref, bu_ref, wd_ref, bd_ref,
    y_ref, gt_ref, gwu_ref, gwd_ref, small_ref, gbu_ref,
    n2_ref, h_ref, act_ref, gp_ref, yacc, dn, awu, awd,
):
    step = pl.program_id(0)
    steps = pl.num_programs(0)
    fc = wu_ref.shape[1] // parts

    @pl.when(step == 0)
    def _():
        awu[...] = jnp.zeros_like(awu)
        awd[...] = jnp.zeros_like(awd)
        small_ref[...] = jnp.zeros_like(small_ref)
        gbu_ref[...] = jnp.zeros_like(gbu_ref)

    sub = 48
    for i in range(z.r // sub):
        rows = slice(i * sub, (i + 1) * sub)
        hat, _ = norm_stats(t2_ref[0, rows, :])
        n2_ref[rows, :] = (hat * gain_ref[...] + shift_ref[...]).astype(BF16)

    def part(f, _):
        cols = pl.ds(pl.multiple_of(f * fc, fc), fc)
        h_ref[...] = mm(n2_ref[...], wu_ref[:, cols])
        bias = bu_ref[:, cols]
        for i in range(z.r // 16):
            rows = slice(i * 16, (i + 1) * 16)
            act, gp = gelu_both(h_ref[rows, :] + bias)
            act_ref[rows, :] = act.astype(BF16)
            gp_ref[rows, :] = gp
        e = e_ref[0]
        yacc[...] = jnp.where(f == 0, 0.0, yacc[...]) + mm(act_ref[...], wd_ref[cols, :])
        awd[cols, :] += mm_tn(act_ref[...], e)
        h_ref[...] = mm_nt(e, wd_ref[cols, :])
        total = jnp.zeros((1, fc), F32)
        for i in range(z.r // 16):
            rows = slice(i * 16, (i + 1) * 16)
            dh = (h_ref[rows, :] * gp_ref[rows, :]).astype(BF16)
            act_ref[rows, :] = dh
            total = total + colsum(dh.astype(F32))
        gbu_ref[:, cols] += total
        awu[:, cols] += mm_tn(n2_ref[...], act_ref[...])
        dn[...] = jnp.where(f == 0, 0.0, dn[...]) + mm_nt(act_ref[...], wu_ref[:, cols])
        return 0

    lax.fori_loop(0, parts, part, 0)
    sums = [jnp.zeros((1, z.d), F32) for _ in range(4)]
    for i in range(z.r // sub):
        rows = slice(i * sub, (i + 1) * sub)
        t2 = t2_ref[0, rows, :]
        e = e_ref[0, rows, :].astype(F32)
        y_ref[0, rows, :] = (t2 + yacc[rows, :] + bd_ref[...]).astype(BF16)
        hat, rstd = norm_stats(t2)
        d = dn[rows, :]
        gt = (e + norm_back(hat, rstd, gain_ref[...], d)).astype(BF16)
        gt_ref[0, rows, :] = gt
        sums = [
            sums[0] + colsum(d * hat),
            sums[1] + colsum(d),
            sums[2] + colsum(e),
            sums[3] + colsum(gt.astype(F32)),
        ]
    for i in range(4):
        small_ref[i : i + 1, :] += sums[i]

    @pl.when(step == steps - 1)
    def _():
        gwu_ref[...] = awu[...].astype(BF16)
        gwd_ref[...] = awd[...].astype(BF16)


def local_bwd_kernel(
    z, gt_ref, xp_ref, r2_ref, o_ref, p_ref, qw_ref, code_ref, gain_ref, shift_ref, w_ref, wo_ref,
    pg_ref, dt0_ref, gwq_ref, gwo_ref, small_ref,
    ds_, dq_, dqkv, dtp, hat_s,
):
    step = pl.program_id(0)
    steps = pl.num_programs(0)

    @pl.when(step == 0)
    def _():
        gwq_ref[...] = jnp.zeros_like(gwq_ref)
        gwo_ref[...] = jnp.zeros_like(gwo_ref)
        small_ref[...] = jnp.zeros_like(small_ref)

    gt = gt_ref[0]
    dot = mm_nt(gt, wo_ref[...])
    for j in range(z.groups):
        ds_[j, : z.r, :] = dot[:, j * LANES : (j + 1) * LANES]
        if z.wide > z.r:
            ds_[j, z.r :, :] = jnp.zeros((z.wide - z.r, LANES), F32)
    gwo_ref[...] += mm_tn(o_ref[0], gt)
    masks = head_masks(SEG, z.hd)
    pad = jnp.zeros((SEG - 56, LANES), F32)
    scale = z.hd ** (-0.5)

    def window(w, _):
        for g in range(z.groups):
            q, k, v = qw_ref[w, g], qw_ref[w, z.groups + g], qw_ref[w, 2 * z.groups + g]
            do = jnp.concatenate([ds_[g, pl.ds(w, 56, stride=z.k), :], pad], axis=0).astype(BF16)
            p = p_ref[w, g]
            dobd = spread(do, masks)
            dp = mm_nt(v, dobd)
            pf = p.astype(F32)
            t = pf * dp
            ds = (t - pf * jnp.sum(t, axis=0, keepdims=True)).astype(BF16)
            dv = mm(p, dobd)
            dk = mm(ds, spread(q, masks)) * scale
            dq = unspread(mm_tn(ds, k), 56, SEG, masks) * scale
            dq_[g, pl.ds(w, 56, stride=z.k), :] = dq
            dq_[z.groups + g, pl.ds(w, 56, stride=z.k), :] = dk[:56]
            dq_[2 * z.groups + g, pl.ds(w, 56, stride=z.k), :] = dv[:56]
        return 0

    lax.fori_loop(0, z.k, window, 0)
    for j in range(3 * z.groups):
        dqkv[:, j * LANES : (j + 1) * LANES] = dq_[j, : z.r, :].astype(BF16)
    dn = mm_nt(dqkv[...], w_ref[...])
    ds_flat = hat_s
    t = xp_ref[0].astype(F32)
    t = jnp.concatenate([r2_ref[0], t[z.k :]], axis=0)
    hat, rstd = norm_stats(t)
    nt = (hat * gain_ref[...] + shift_ref[...]).astype(BF16)
    gwq_ref[...] += mm_tn(nt, dqkv[...])
    dt = gt.astype(F32) + norm_back(hat, rstd, gain_ref[...], dn)
    dt0_ref[0] = dt[: z.k]
    dtp[step] = dt.astype(BF16)
    small_ref[0:1, :] += colsum(dn * hat)
    small_ref[1:2, :] += colsum(dn)

    @pl.when(step == steps - 1)
    def _():
        sel_t = one_hot_t(code_ref[...], z.gp * z.w)
        for g in range(z.ng):
            unpack_group(z, g, sel_t, dtp, pg_ref, None)


def region_bwd_kernel(
    z, kc, dt0_ref, all_ref, o_ref, of_ref, p_ref, kv_ref, nr_ref, q_ref, nown_ref, own_ref, ord_ref, gain_ref,
    w_ref, wo_ref,
    dnr_ref, dt0a_ref, dnown_ref, gwq_ref, gwo_ref, small_ref,
):
    n = all_ref.shape[0]
    nq = HEADS * z.w
    dt0 = jnp.concatenate([dt0_ref[c] for c in range(z.nb)], axis=0)
    sel_t = one_hot_t(ord_ref[...], z.w).astype(F32)
    dt0 = jnp.dot(sel_t, dt0, precision=HIGH, preferred_element_type=F32)
    dt0a_ref[...] = dt0
    gr = dt0.astype(BF16)
    gwo_ref[...] = mm_tn(o_ref[...], gr)
    do = mm_nt(gr, wo_ref[...]).astype(BF16)
    lane = lax.broadcasted_iota(jnp.int32, (z.w, z.d), 1) // z.hd
    zero = jnp.zeros_like(do)
    dobd = jnp.concatenate([jnp.where(lane == h, do, zero) for h in range(HEADS)], axis=0)
    q = q_ref[...]
    qbd = jnp.concatenate([jnp.where(lane == h, q, zero) for h in range(HEADS)], axis=0)
    scale = z.hd ** (-0.5)

    prod = do.astype(F32) * of_ref[...]
    spread_prod = jnp.concatenate([jnp.where(lane == h, prod, 0.0) for h in range(HEADS)], axis=0)
    delta = lax.dot_general(
        jnp.ones((8, z.d), F32), spread_prod, (((1,), (1,)), ((), ())), precision=HIGH,
        preferred_element_type=F32,
    )[0:1]
    small_ref[...] = jnp.zeros_like(small_ref)
    gwq_ref[...] = jnp.zeros_like(gwq_ref)

    def second(i, acc):
        rows = pl.ds(pl.multiple_of(i * kc, kc), kc)
        p = p_ref[rows, :]
        ds = (p.astype(F32) * (mm_nt(kv_ref[rows, z.d :], dobd) - delta)).astype(BF16)
        dv = mm(p, dobd).astype(BF16)
        dk = (mm(ds, qbd) * scale).astype(BF16)
        dkv = jnp.concatenate([dk, dv], axis=1)
        gwq_ref[:, z.d :] += mm_tn(nr_ref[rows, :], dkv)
        dn = mm_nt(dkv, w_ref[:, z.d :])
        dnr_ref[rows, :] = dn.astype(BF16)
        hat, _ = norm_stats(all_ref[rows, :].astype(F32))
        small_ref[0:1, :] += colsum(dn * hat)
        small_ref[1:2, :] += colsum(dn)
        return acc + mm_tn(ds, kv_ref[rows, : z.d])

    full = lax.fori_loop(0, n // kc, second, jnp.zeros((nq, z.d), F32))
    dq = full[(HEADS - 1) * z.w :]
    for h in range(HEADS - 2, -1, -1):
        dq = jnp.where(lane == h, full[h * z.w : (h + 1) * z.w], dq)
    dq = (dq * scale).astype(BF16)
    gwq_ref[:, : z.d] = mm_tn(nown_ref[...], dq)
    dn = mm_nt(dq, w_ref[:, : z.d])
    dnown_ref[...] = dn
    hat, _ = norm_stats(own_ref[...].astype(F32))
    small_ref[0:1, :] += colsum(dn * hat)
    small_ref[1:2, :] += colsum(dn)
    small_ref[2:3, :] = colsum(gr.astype(F32))


def local(
    patches, regions, send_order, image_windows, attn_gain, attn_shift, w_qkv, w_out, b_out,
    mlp_gain, mlp_shift, w_up, b_up, w_down, b_down, upstream_patches, upstream_regions,
):
    axes = ("gx", "gy")
    nx, ny = lax.axis_size("gx"), lax.axis_size("gy")
    z = Sizes(patches.shape[0], patches.shape[1], patches.shape[2], nx)
    ff = w_up.shape[1]
    n = z.w * nx * ny
    gx = lax.axis_index("gx")
    dev = gx * ny + lax.axis_index("gy")
    sds = jax.ShapeDtypeStruct

    order = lax.dynamic_slice_in_dim(send_order, dev, 1, 0)[0].reshape(nx, z.k)
    tile = jnp.arange(nx, dtype=jnp.int32)
    order_t = jnp.take(order, (gx - tile) % nx, axis=0)
    place = jnp.arange(z.gp, dtype=jnp.int32) * z.w
    code_x = (order_t[:, None, :] + place[None, :, None]).reshape(-1)
    block = ((gx + tile) % nx)[:, None] * z.k + jnp.arange(z.k, dtype=jnp.int32)[None, :]
    code_e = (block[:, None, :] + place[None, :, None]).reshape(-1)
    order_t = order_t.reshape(-1)
    bounds = jnp.cumsum(image_windows)
    image = jnp.sum(
        (jnp.arange(n, dtype=jnp.int32)[:, None] >= bounds[None, :]).astype(jnp.int32), axis=1
    )
    image_own = lax.dynamic_slice_in_dim(image, dev * z.w, z.w)
    gain, shift = attn_gain[None], attn_shift[None]

    x_t = jnp.transpose(patches, (1, 0, 2))
    e_t = jnp.transpose(upstream_patches, (1, 0, 2))

    packed = pl.pallas_call(
        functools.partial(pack_kernel, z),
        out_shape=sds((z.nb, z.r, z.d), BF16),
        compiler_params=params(),
        name="pack",
    )(e_t, upstream_regions, code_e[:, None])

    def exchange(blocks, sign):
        out = [blocks[0]]
        for o in range(1, nx):
            out.append(
                lax.ppermute(blocks[o], "gx", [(i, (i + sign * o) % nx) for i in range(nx)])
            )
        return out

    e_in = jnp.stack(exchange([packed[o] for o in range(nx)], 1))

    regions_all = lax.all_gather(regions, axes, axis=0, tiled=True)

    xp, qkv = pl.pallas_call(
        functools.partial(qkv_kernel, z),
        out_shape=(sds((z.nb, z.r, z.d), BF16), sds((z.nb, z.r, 3 * z.d), BF16)),
        compiler_params=params(),
        name="qkv",
    )(x_t, code_x[:, None], gain, shift, w_qkv)

    kc = 256
    nq = HEADS * z.w
    r2, p_r, kv_all, nr_all, q_r, o_r, o_f, n_own = pl.pallas_call(
        functools.partial(region_fwd_kernel, z, kc),
        out_shape=(
            sds((z.nb, z.k, z.d), F32),
            sds((n, nq), BF16),
            sds((n, 2 * z.d), BF16),
            sds((n, z.d), BF16),
            sds((z.w, z.d), BF16),
            sds((z.w, z.d), BF16),
            sds((z.w, z.d), F32),
            sds((z.w, z.d), BF16),
        ),
        scratch_shapes=[pltpu.VMEM((n, nq), F32)],
        compiler_params=params(),
        name="region_fwd",
    )(
        regions_all, regions, image[:, None], jnp.tile(image_own, HEADS)[None], order_t[:, None],
        gain, shift, w_qkv, w_out, b_out[None],
    )

    def tiled(*shape):
        return pl.BlockSpec((1,) + shape, lambda i: (i,) + (0,) * len(shape))

    def grouped(*shape):
        return pl.BlockSpec((z.k,) + shape, lambda i: (i,) + (0,) * len(shape))

    cols = z.per_group * SEG
    t2, p_w, qw, o_w = pl.pallas_call(
        functools.partial(local_fwd_kernel, z),
        grid=(z.nb,),
        in_specs=[
            tiled(z.r, 3 * z.d), tiled(z.r, z.d), tiled(z.k, z.d), whole(1, z.d), whole(1, z.d),
            whole(z.d, 3 * z.d), whole(z.d, z.d), whole(1, z.d),
        ],
        out_specs=[
            tiled(z.r, z.d), grouped(z.groups, SEG, cols), grouped(3 * z.groups, SEG, LANES),
            tiled(z.r, z.d),
        ],
        out_shape=(
            sds((z.nb, z.r, z.d), F32),
            sds((z.w, z.groups, SEG, cols), BF16),
            sds((z.w, 3 * z.groups, SEG, LANES), BF16),
            sds((z.nb, z.r, z.d), BF16),
        ),
        scratch_shapes=[
            pltpu.VMEM((3 * z.groups, z.wide, LANES), F32),
            pltpu.VMEM((z.groups, z.wide, LANES), F32),
        ],
        compiler_params=params(),
        name="local_fwd",
    )(qkv, xp, r2, gain, shift, w_qkv, w_out, b_out[None])

    parts = 4
    fc = ff // parts
    y, gt, gwu, gwd, small_m, gbu = pl.pallas_call(
        functools.partial(mlp_kernel, z, parts),
        grid=(z.nb,),
        in_specs=[
            tiled(z.r, z.d), tiled(z.r, z.d), whole(1, z.d), whole(1, z.d), whole(z.d, ff),
            whole(1, ff), whole(ff, z.d), whole(1, z.d),
        ],
        out_specs=[
            tiled(z.r, z.d), tiled(z.r, z.d), whole(z.d, ff), whole(ff, z.d), whole(8, z.d),
            whole(1, ff),
        ],
        out_shape=(
            sds((z.nb, z.r, z.d), BF16),
            sds((z.nb, z.r, z.d), BF16),
            sds((z.d, ff), BF16),
            sds((ff, z.d), BF16),
            sds((8, z.d), F32),
            sds((1, ff), F32),
        ),
        scratch_shapes=[
            pltpu.VMEM((z.r, z.d), BF16),
            pltpu.VMEM((z.r, fc), F32),
            pltpu.VMEM((z.r, fc), BF16),
            pltpu.VMEM((z.r, fc), F32),
            pltpu.VMEM((z.r, z.d), F32),
            pltpu.VMEM((z.r, z.d), F32),
            pltpu.VMEM((z.d, ff), F32),
            pltpu.VMEM((ff, z.d), F32),
        ],
        compiler_params=params(),
        name="mlp",
    )(t2, e_in, mlp_gain[None], mlp_shift[None], w_up, b_up[None], w_down, b_down[None])

    y_in = exchange([y[o] for o in range(nx)], -1)
    out_p, out_r = pl.pallas_call(
        functools.partial(unpack_kernel, z),
        out_shape=(sds((z.tok, z.w, z.d), BF16), sds((z.w, z.d), BF16)),
        compiler_params=params(),
        name="unpack",
    )(*y_in, code_e[None])

    patch_grad, dt0, gwq, gwo, small_a = pl.pallas_call(
        functools.partial(local_bwd_kernel, z),
        grid=(z.nb,),
        in_specs=[
            tiled(z.r, z.d), tiled(z.r, z.d), tiled(z.k, z.d), tiled(z.r, z.d),
            grouped(z.groups, SEG, cols), grouped(3 * z.groups, SEG, LANES),
            whole(1, z.nb * z.gp * z.k), whole(1, z.d), whole(1, z.d), whole(z.d, 3 * z.d),
            whole(z.d, z.d),
        ],
        out_specs=[
            whole(z.tok, z.w, z.d), tiled(z.k, z.d), whole(z.d, 3 * z.d), whole(z.d, z.d),
            whole(8, z.d),
        ],
        out_shape=(
            sds((z.tok, z.w, z.d), BF16),
            sds((z.nb, z.k, z.d), F32),
            sds((z.d, 3 * z.d), F32),
            sds((z.d, z.d), F32),
            sds((8, z.d), F32),
        ),
        scratch_shapes=[
            pltpu.VMEM((z.groups, z.wide, LANES), F32),
            pltpu.VMEM((3 * z.groups, z.wide, LANES), F32),
            pltpu.VMEM((z.r, 3 * z.d), BF16),
            pltpu.VMEM((z.nb, z.r, z.d), BF16),
            pltpu.VMEM((8, LANES), F32),
        ],
        compiler_params=params(),
        name="local_bwd",
    )(gt, xp, r2, o_w, p_w, qw, code_x[None], gain, shift, w_qkv, w_out)

    dnr, dt0a, dn_own, gwq_r, gwo_r, small_r = pl.pallas_call(
        functools.partial(region_bwd_kernel, z, kc),
        out_shape=(
            sds((n, z.d), BF16),
            sds((z.w, z.d), F32),
            sds((z.w, z.d), F32),
            sds((z.d, 3 * z.d), F32),
            sds((z.d, z.d), F32),
            sds((8, z.d), F32),
        ),
        compiler_params=params(),
        name="region_bwd",
    )(
        dt0, regions_all, o_r, o_f, p_r, kv_all, nr_all, q_r, n_own, regions, order_t[None], gain, w_qkv,
        w_out,
    )

    dnr_own = lax.psum_scatter(dnr, axes, scatter_dimension=0, tiled=True).astype(F32) + dn_own
    hat, rstd = norm_stats(regions.astype(F32))
    region_grad = (dt0a + norm_back(hat, rstd, gain, dnr_own)).astype(BF16)

    gwq = (gwq + gwq_r).astype(BF16)
    gwo = (gwo + gwo_r).astype(BF16)
    small_a = small_a + small_r
    gwu, gwd, gwq, gwo = lax.psum((gwu, gwd, gwq, gwo), axes)
    g_again, g_ashift, g_bout, g_mgain, g_mshift, g_bdown, g_bup = lax.psum(
        (small_a[0], small_a[1], small_a[2] + small_m[3], small_m[0], small_m[1], small_m[2], gbu[0]),
        axes,
    )
    return (
        jnp.transpose(out_p, (1, 0, 2)),
        out_r,
        jnp.transpose(patch_grad, (1, 0, 2)),
        region_grad,
        g_again,
        g_ashift,
        gwq.astype(F32),
        gwo.astype(F32),
        g_bout,
        g_mgain,
        g_mshift,
        gwu.astype(F32),
        g_bup,
        gwd.astype(F32),
        g_bdown,
    )


def solution(mesh):
    split = ("gx", "gy")
    rows3, rows2, full = P(split, None, None), P(split, None), P()
    in_specs = (rows3, rows2) + (full,) * 13 + (rows3, rows2)
    out_specs = (rows3, rows2, rows3, rows2) + (full,) * 11
    return jax.shard_map(local, mesh=mesh, in_specs=in_specs, out_specs=out_specs, check_vma=False)
```

```python
import functools
import math

import jax
import jax.numpy as jnp
from jax import lax
from jax.experimental import pallas as pl
from jax.experimental.pallas import tpu as pltpu
from jax.sharding import PartitionSpec as P

HEADS = 16
EPS = 1e-05
F32 = jnp.float32
BF16 = jnp.bfloat16
LOG2E = 1.4426950408889634
VMEM_LIMIT = 60 * 1024 * 1024
HIGH = lax.Precision.HIGHEST
LANES = 128
MLP_PARTS = 4
BWD_TICKS = 3
MLP_US = 60.0
BWD_US = 36.0
LATENCY_US = 3.0
SLACK_US = 2.5
SEG = 64


def mm(a, b):
    return lax.dot_general(a, b, (((1,), (0,)), ((), ())), preferred_element_type=F32)


def mm_nt(a, b):
    return lax.dot_general(a, b, (((1,), (1,)), ((), ())), preferred_element_type=F32)


def mm_tn(a, b):
    return lax.dot_general(a, b, (((0,), (0,)), ((), ())), preferred_element_type=F32)


def norm_stats(v):
    average = jnp.mean(v, axis=-1, keepdims=True)
    centered = v - average
    variance = jnp.mean(centered * centered, axis=-1, keepdims=True)
    rstd = lax.rsqrt(variance + EPS)
    return centered * rstd, rstd


def norm_back(hat, rstd, gain, dn):
    dhat = dn * gain
    m1 = jnp.mean(dhat, axis=-1, keepdims=True)
    m2 = jnp.mean(dhat * hat, axis=-1, keepdims=True)
    return rstd * (dhat - m1 - hat * m2)


def colsum(v):
    return jnp.sum(v, axis=0, keepdims=True)


def gelu_both(u):
    a = jnp.abs(u)
    d = 1.0 + (0.3275911 * 0.7071067811865476) * a
    r = pl.reciprocal(d, approx=True)
    t = r * (2.0 - d * r)
    e = jnp.exp2((u * u) * (-0.5 * LOG2E))
    poly = t * (
        0.127414796
        + t * (-0.142248368 + t * (0.7107068705 + t * (-0.7265760135 + t * 0.5307027145)))
    )
    tail = poly * e
    cdf = jnp.where(u >= 0.0, 1.0 - tail, tail)
    return u * cdf, cdf + u * (e * 0.3989422804014327)


def head_masks(rows, head_dim):
    lane = lax.broadcasted_iota(jnp.int32, (rows, LANES), 1)
    return [(lane // head_dim) == h for h in range(LANES // head_dim)]


def spread(v, masks):
    zero = jnp.zeros_like(v)
    return jnp.concatenate([jnp.where(m, v, zero) for m in masks], axis=0)


def unspread(full, rows, stride, masks):
    out = full[(len(masks) - 1) * stride : (len(masks) - 1) * stride + rows]
    for h in range(len(masks) - 2, -1, -1):
        out = jnp.where(masks[h][:rows], full[h * stride : h * stride + rows], out)
    return out


def one_hot(code_col, count):
    rows = code_col.shape[0]
    return (lax.broadcasted_iota(jnp.int32, (rows, count), 1) == code_col).astype(F32).astype(BF16)


def one_hot_t(code_row, count):
    rows = code_row.shape[1]
    return (lax.broadcasted_iota(jnp.int32, (count, rows), 0) == code_row).astype(F32).astype(BF16)


def whole(*shape):
    return pl.BlockSpec(shape, lambda *_: (0,) * len(shape))


class Sizes:
    def __init__(self, per_dev, patch_tokens, width, count_gx):
        self.w = per_dev
        self.tok = patch_tokens
        self.d = width
        self.nb = count_gx
        self.k = per_dev // count_gx
        step = 16 // math.gcd(16, self.k)
        self.pos = -(-(patch_tokens + 1) // step) * step
        self.gp = step
        while (self.gp * self.k) % 16:
            self.gp *= 2
        self.ng = self.pos // self.gp
        self.early = self.ng // 2 * self.gp * self.k
        self.r = self.pos * self.k
        self.wide = 56 * self.k
        self.hd = width // HEADS
        self.groups = width // LANES
        self.per_group = LANES // self.hd
        self.chunk = self.r // 3 if self.r % 48 == 0 else self.r
        self.kp = -(-self.k // 16) * 16
        self.side = max(j for j in range(1, 5) if self.k % j == 0)
        self.t = self.nb * self.r
        self.tp = -(-self.t // 256) * 256
        self.m = max(m for m in range(16, 833, 16) if self.t % m == 0 and self.t <= 4 * m)


def params(**kw):
    return pltpu.CompilerParams(vmem_limit_bytes=VMEM_LIMIT, **kw)


def pack_group(z, g, sel_t, x_ref, first_ref, outs):
    pieces = []
    for p in range(g * z.gp, (g + 1) * z.gp):
        if p == 0:
            pieces.append(jnp.zeros((z.w, z.d), BF16) if first_ref is None else first_ref[...])
        elif p <= z.tok:
            pieces.append(x_ref[p - 1])
        else:
            pieces.append(jnp.zeros((z.w, z.d), BF16))
    got = mm_tn(sel_t, jnp.concatenate(pieces, axis=0)).astype(BF16)
    rows = z.gp * z.k
    for c in range(z.nb):
        outs[c][g * rows : (g + 1) * rows, :] = got[c * rows : (c + 1) * rows]


def unpack_group(z, g, sel_t, packed_ref, out_ref, first_ref, at=None):
    rows = z.gp * z.k
    here = slice((g if at is None else at) * rows, ((g if at is None else at) + 1) * rows)
    src = jnp.concatenate([packed_ref[c, here, :] for c in range(z.nb)], axis=0)
    got = mm(sel_t, src).astype(BF16)
    for i in range(z.gp):
        p = g * z.gp + i
        piece = got[i * z.w : (i + 1) * z.w]
        if p == 0:
            if first_ref is not None:
                first_ref[...] = piece
        elif p <= z.tok:
            out_ref[p - 1] = piece


def start_kernel(
    z, nx, ny, x_ref, e_ref, first_ref, codex_ref, codee_ref, gain_ref, shift_ref, w_ref, own_ref, *refs
):
    packed, refs = refs[: z.nb], refs[z.nb :]
    xp_ref, qkv_ref, all_ref, xs, es, qs, nt, buf, sems, load_sems, out_sems = refs
    loads = [
        pltpu.make_async_copy(src, dst, load_sems.at[i])
        for i, (src, dst) in enumerate(((e_ref, es), (x_ref, xs)))
    ]
    for x in loads:
        x.start()
    mesh = Mesh2(nx, ny)
    rounds = routes_of(nx, ny)[0]
    gather = Gather(mesh, buf, z.w, rounds, sems, 0)
    mesh.barrier(rounds)
    buf[pl.ds(*gather.held(0)), :] = own_ref[...]
    gather.start(0)

    def pack(src, code_ref, first, outs):
        sel_t = one_hot_t(code_ref[...], z.gp * z.w)
        for g in range(z.ng):
            pack_group(z, g, sel_t, src, first, outs)

    outs = [pltpu.make_async_copy(qs.at[c], qkv_ref.at[c], out_sems.at[c]) for c in range(z.nb)]

    def project(c):
        hat, _ = norm_stats(xp_ref[c].astype(F32))
        nt[...] = (hat * gain_ref[...] + shift_ref[...]).astype(BF16)
        qs[c] = mm(nt[...], w_ref[...]).astype(BF16)
        outs[c].start()

    stages = gather.stages
    loads[0].wait()
    pack(es, codee_ref, first_ref, packed)
    loads[1].wait()
    pack(xs, codex_ref, None, [xp_ref.at[c] for c in range(z.nb)])
    for s in range(1, stages + 1):
        gather.finish(s - 1)
        if s < stages:
            gather.start(s)
            for c in range(z.nb * (s - 1) // (stages - 1), z.nb * s // (stages - 1)):
                project(c)
    n = nx * ny
    order = flat(rounds)
    for dev in range(n):
        p = place_of(order, nx, ny, dev)
        all_ref[dev * z.w : (dev + 1) * z.w, :] = buf[p * z.w : (p + 1) * z.w, :]
    for x in outs:
        x.wait()


def region_fwd_kernel(
    z, kc, ny, all_ref, own_ref, bounds_ref, ord_ref, gain_ref, shift_ref, w_ref, wo_ref, bo_ref,
    r2_ref, p_ref, kv_ref, nr_ref, q_ref, o_ref, of_ref, nown_ref, s_ref,
):
    n = all_ref.shape[0]
    nq = HEADS * z.w
    hat, _ = norm_stats(own_ref[...].astype(F32))
    nown = (hat * gain_ref[...] + shift_ref[...]).astype(BF16)
    nown_ref[...] = nown
    q = mm(nown, w_ref[:, : z.d]).astype(BF16)
    q_ref[...] = q
    lane = lax.broadcasted_iota(jnp.int32, (z.w, z.d), 1) // z.hd
    zero = jnp.zeros_like(q)
    qbd = jnp.concatenate([jnp.where(lane == h, q, zero) for h in range(HEADS)], axis=0)
    scale = z.hd ** (-0.5) * LOG2E
    dev = lax.axis_index("gx") * ny + lax.axis_index("gy")
    window = dev * z.w + lax.broadcasted_iota(jnp.int32, (1, nq), 1) % z.w

    def image(j, span):
        low, high = span
        bound = bounds_ref[j]
        return jnp.where(bound <= window, bound, low), jnp.where(bound > window, jnp.minimum(high, bound), high)

    low, high = lax.fori_loop(
        0, bounds_ref.shape[0], image,
        (jnp.zeros((1, nq), jnp.int32), jnp.full((1, nq), n, jnp.int32)),
    )
    key = lax.broadcasted_iota(jnp.int32, (kc, nq), 0)

    def scores(i, top):
        rows = pl.ds(pl.multiple_of(i * kc, kc), kc)
        hat, _ = norm_stats(all_ref[rows, :].astype(F32))
        nr = (hat * gain_ref[...] + shift_ref[...]).astype(BF16)
        nr_ref[rows, :] = nr
        kv = mm(nr, w_ref[:, z.d :]).astype(BF16)
        kv_ref[rows, :] = kv
        s = mm_nt(kv[:, : z.d], qbd) * scale
        s = jnp.where((key >= low - i * kc) & (key < high - i * kc), s, -1e30)
        s_ref[rows, :] = s
        return jnp.maximum(top, jnp.max(s, axis=0, keepdims=True))

    top = lax.fori_loop(0, n // kc, scores, jnp.full((1, nq), -1e30, F32))

    def weigh(i, total):
        rows = pl.ds(pl.multiple_of(i * kc, kc), kc)
        p = jnp.exp2(s_ref[rows, :] - top)
        s_ref[rows, :] = p
        return total + jnp.sum(p, axis=0, keepdims=True)

    total = lax.fori_loop(0, n // kc, weigh, jnp.zeros((1, nq), F32))
    inverse = 1.0 / total

    def attend(i, acc):
        rows = pl.ds(pl.multiple_of(i * kc, kc), kc)
        p = (s_ref[rows, :] * inverse).astype(BF16)
        p_ref[rows, :] = p
        return acc + mm_tn(p, kv_ref[rows, z.d :])

    full = lax.fori_loop(0, n // kc, attend, jnp.zeros((nq, z.d), F32))
    o = full[(HEADS - 1) * z.w :]
    for h in range(HEADS - 2, -1, -1):
        o = jnp.where(lane == h, full[h * z.w : (h + 1) * z.w], o)
    of_ref[...] = o
    o = o.astype(BF16)
    o_ref[...] = o
    r2 = own_ref[...].astype(F32) + mm(o, wo_ref[...]) + bo_ref[...]
    sel_t = one_hot_t(ord_ref[...], z.w).astype(F32)
    r2 = lax.dot_general(
        sel_t, r2, (((0,), (0,)), ((), ())), precision=HIGH, preferred_element_type=F32
    )
    for c in range(z.nb):
        r2_ref[c, : z.k, :] = r2[c * z.k : (c + 1) * z.k]
        r2_ref[c, z.k :, :] = jnp.zeros((z.kp - z.k, z.d), F32)


def local_fwd_kernel(
    z, qkv_ref, xp_ref, r2_ref, gain_ref, shift_ref, w_ref, wo_ref, bo_ref,
    t2_ref, p_ref, qw_ref, o_ref, qs, os,
):
    tiles = 3 * z.groups
    for j in range(tiles):
        qs[j, : z.r, :] = qkv_ref[0, :, j * LANES : (j + 1) * LANES].astype(F32)
        if z.wide > z.r:
            qs[j, z.r :, :] = jnp.zeros((z.wide - z.r, LANES), F32)
    hat, _ = norm_stats(r2_ref[0])
    nt = (hat * gain_ref[...] + shift_ref[...]).astype(BF16)
    reg = mm(nt, w_ref[...]).astype(BF16).astype(F32)
    for j in range(tiles):
        qs[j, : z.k, :] = reg[: z.k, j * LANES : (j + 1) * LANES]
    masks = head_masks(SEG, z.hd)
    pad = jnp.zeros((SEG - 56, LANES), F32)
    valid = lax.broadcasted_iota(jnp.int32, (56, z.per_group * SEG), 0) < z.tok + 1
    scale = z.hd ** (-0.5) * LOG2E
    tail = jnp.zeros((SEG - 56, z.per_group * SEG), F32)

    def windows(i, _):
        jobs = [(i * z.side + j, g) for j in range(z.side) for g in range(z.groups)]

        def load(w, j):
            rows = qs[j, pl.ds(w, 56, stride=z.k), :]
            got = jnp.concatenate([rows, pad], axis=0).astype(BF16)
            qw_ref[w, j] = got
            return got

        q = [load(w, g) for w, g in jobs]
        k = [load(w, z.groups + g) for w, g in jobs]
        v = [load(w, 2 * z.groups + g) for w, g in jobs]
        s = [mm_nt(kk, spread(qq, masks))[:56] for qq, kk in zip(q, k)]
        s = [jnp.where(valid, x, -1e30) for x in s]
        p = [jnp.exp2((x - jnp.max(x, axis=0, keepdims=True)) * scale) for x in s]
        p = [x * (1.0 / jnp.sum(x, axis=0, keepdims=True)) for x in p]
        p = [jnp.concatenate([x, tail], axis=0).astype(BF16) for x in p]
        for (w, g), x in zip(jobs, p):
            p_ref[w, g] = x
        full = [mm_tn(x, vv) for x, vv in zip(p, v)]
        for (w, g), x in zip(jobs, full):
            os[g, pl.ds(w, 56, stride=z.k), :] = unspread(x, 56, SEG, masks)
        return 0

    lax.fori_loop(0, z.k // z.side, windows, 0)
    for i in range(z.r // z.chunk):
        rows = slice(i * z.chunk, (i + 1) * z.chunk)
        o = jnp.concatenate([os[g, rows, :] for g in range(z.groups)], axis=1).astype(BF16)
        o_ref[0, rows, :] = o
        t2_ref[0, rows, :] = xp_ref[0, rows, :].astype(F32) + mm(o, wo_ref[...]) + bo_ref[...]
    t2_ref[0, : z.k, :] = t2_ref[0, : z.k, :] + r2_ref[0, : z.k, :]


def tiles_dot(lhs, w, acc, transposed=False):
    side = 256
    for k in range(w.shape[0] // side):
        for j in range(len(acc)):
            ks, js = slice(k * side, (k + 1) * side), slice(j * side, (j + 1) * side)
            pltpu.matmul_push_rhs(w[js, ks] if transposed else w[ks, js], k % 2, j, transpose=transposed)
            pltpu.matmul_acc_lhs(acc[j], lhs(k), load_staged_rhs=k % 2)


def mlp_kernel(z, nx, ny, acts, done, *refs):
    (t2_ref, *e_refs), refs = refs[: 1 + z.nb], refs[1 + z.nb :]
    (
        gain_ref, shift_ref, wu_ref, bu_ref, wd_ref, bd_ref,
        y_ref, gt_ref, buf_ref, small_ref, gbu_ref,
        n2, e, n2_t, e_t, h0, h1, d0, d1, active, dh, yacc, dn, buf, recv, full, sems, copy_sem,
    ) = refs
    f = pl.program_id(0)
    parts = pl.num_programs(0)
    mesh = Mesh2(nx, ny)
    sums = mlp_sums(mesh, z, buf, recv, full, sems)
    per = len(acts) // MLP_PARTS
    sub, side = math.gcd(z.m, 64), 256
    fc = wu_ref.shape[1]
    m = h0.shape[0]
    chunks = z.t // m

    def rows_of(c):
        return slice(c * m, (c + 1) * m)

    def tick(p):
        for step in range(len(acts) // per):
            if acts[step * per + p]:

                @pl.when(f == step)
                def _():
                    act(sums, acts[step * per + p])

    @pl.when(f == 0)
    def _():
        fetch = [
            pltpu.make_async_copy(e_refs[c], e.at[c * z.r : (c + 1) * z.r, :], copy_sem.at[c])
            for c in range(z.nb)
        ]
        begin = [
            pltpu.make_async_copy(t2_ref.at[rows_of(c), :], yacc.at[rows_of(c), :], copy_sem.at[z.nb + c])
            for c in range(chunks)
        ]
        for x in begin + fetch:
            x.start()
        mesh.barrier(all_rounds(nx, ny))

        def prepare(i, _):
            rows = pl.ds(pl.multiple_of(i * sub, 16), sub)
            hat, _ = norm_stats(yacc[rows, :])
            n2[rows, :] = (hat * gain_ref[...] + shift_ref[...]).astype(BF16)
            dn[rows, :] = jnp.zeros((sub, z.d), F32)
            return 0

        for c in range(chunks):
            begin[c].wait()
            lax.fori_loop(c * (m // sub), (c + 1) * (m // sub), prepare, 0, unroll=13)
        for x in fetch:
            x.wait()
        if z.tp > z.t:
            for x in (n2, e, active, dh):
                x[z.t :, :] = jnp.zeros((z.tp - z.t, x.shape[1]), BF16)

        def turn(i, _):
            span = pl.ds(pl.multiple_of(i * side, side), side)
            n2_t[: z.d, span] = n2[span, :].T
            e_t[: z.d, span] = e[span, :].T
            n2_t[z.d :, span] = jnp.ones((16, side), BF16)
            e_t[z.d :, span] = jnp.zeros((16, side), BF16)
            return 0

        lax.fori_loop(0, z.tp // side, turn, 0)

    results = [
        [
            pltpu.make_async_copy(n2.at[rows_of(c), :], y_ref.at[rows_of(c), :], copy_sem.at[8 + 2 * c]),
            pltpu.make_async_copy(e.at[rows_of(c), :], gt_ref.at[rows_of(c), :], copy_sem.at[9 + 2 * c]),
        ]
        for c in range(chunks)
    ]
    slots = (h0, h1, d0, d1)
    again = [
        pltpu.make_async_copy(t2_ref.at[rows_of(c), :], slots[c], copy_sem.at[c]) for c in range(chunks)
    ]
    tick(0)
    bias = bu_ref[...]

    def stream(acc0, acc1):
        acc = (acc0, acc1)
        h, d = (h0, h1), (d0, d1)

        def rows(c):
            return slice(c * m, (c + 1) * m)

        def up(c):
            tiles_dot(lambda k: n2[rows(c), k * side : (k + 1) * side], wu_ref, acc)
            for j in range(2):
                h[c % 2][:, j * side : (j + 1) * side] = pltpu.matmul_pop(acc[j])
            tiles_dot(lambda k: e[rows(c), k * side : (k + 1) * side], wd_ref, acc, True)
            for j in range(2):
                d[c % 2][:, j * side : (j + 1) * side] = pltpu.matmul_pop(acc[j])

        def down(c):
            tiles_dot(lambda k: active[rows(c), k * side : (k + 1) * side], wd_ref, acc)
            for j in range(2):
                yacc[rows(c), j * side : (j + 1) * side] += pltpu.matmul_pop(acc[j])
            tiles_dot(lambda k: dh[rows(c), k * side : (k + 1) * side], wu_ref, acc, True)
            for j in range(2):
                dn[rows(c), j * side : (j + 1) * side] += pltpu.matmul_pop(acc[j])

        def middle(c):
            for i in range(m // 16):
                r, o = slice(i * 16, (i + 1) * 16), slice(c * m + i * 16, c * m + (i + 1) * 16)
                value, slope = gelu_both(h[c % 2][r, :] + bias)
                active[o, :] = value.astype(BF16)
                got = (d[c % 2][r, :] * slope).astype(BF16)
                dh[o, :] = got

        up(0)
        for c in range(chunks):
            if c + 1 < chunks:
                up(c + 1)
            middle(c)
            if c < 3:
                tick(1 + 2 * c)
            if c:
                down(c - 1)
            if c < 3:
                tick(2 + 2 * c)
        down(chunks - 1)

    pl.run_scoped(
        stream, pltpu.ACC(mxu_id=0)((m, side), F32), pltpu.ACC(mxu_id=1)((m, side), F32)
    )
    @pl.when(f == parts - 1)
    def _():
        for x in again:
            x.start()

    tick(7)
    here = pl.multiple_of(f * (2 * fc), 16)

    def gradients(acc0, acc1):
        acc = (acc0, acc1)
        halves = [slice(j * side, (j + 1) * side) for j in range(2)]

        def over_tokens(left, right):
            for i in range(z.tp // side):
                span = slice(i * side, (i + 1) * side)
                for j in range(2):
                    pltpu.matmul_push_rhs(right[span, halves[j]], i % 2, j)
                    pltpu.matmul_acc_lhs(acc[j], left[:, span], load_staged_rhs=i % 2)

        over_tokens(e_t, active)
        for j in range(2):
            rows = pl.ds(pl.multiple_of(here + j * side, 16), side)
            buf[rows, :] = pltpu.matmul_pop(acc[j])[: z.d].T.astype(BF16)
        tick(8)
        over_tokens(n2_t, dh)
        for j in range(2):
            got = pltpu.matmul_pop(acc[j])
            buf[pl.ds(pl.multiple_of(here + fc, 16), z.d), halves[j]] = got[: z.d].astype(BF16)
            gbu_ref[0, :, halves[j]] = got[z.d : z.d + 1]

    pl.run_scoped(
        gradients, pltpu.ACC(mxu_id=0)((z.d + 16, side), F32), pltpu.ACC(mxu_id=1)((z.d + 16, side), F32)
    )
    tick(9)

    @pl.when(f == parts - 1)
    def _():
        zero = jnp.zeros((1, z.d), F32)
        got = (zero,) * 4
        for c in range(chunks):
            again[c].wait()

            def close(i, sums, c=c):
                here = pl.ds(pl.multiple_of(i * sub, 16), sub)
                rows = pl.ds(pl.multiple_of(c * m + i * sub, 16), sub)
                up = e[rows, :].astype(F32)
                n2[rows, :] = (yacc[rows, :] + bd_ref[...]).astype(BF16)
                hat, rstd = norm_stats(slots[c][here, :])
                d = dn[rows, :]
                gt = (up + norm_back(hat, rstd, gain_ref[...], d)).astype(BF16)
                e[rows, :] = gt
                return (
                    sums[0] + colsum(d * hat), sums[1] + colsum(d), sums[2] + colsum(up),
                    sums[3] + colsum(gt.astype(F32)),
                )

            got = lax.fori_loop(0, m // sub, close, got, unroll=13)
            for x in results[c]:
                x.start()
        small_ref[...] = jnp.zeros_like(small_ref)
        for i in range(4):
            small_ref[i : i + 1, :] = got[i]

    tick(10)

    @pl.when(f == parts - 1)
    def _():
        out = carry(sums, done, buf_ref, copy_sem, True)
        for x in out:
            x.start()
        for x in out + sum(results, []):
            x.wait()


def mlp_count(nx, ny, rows):
    count = 2 * MLP_PARTS
    while rows // count % (16 * nx * ny):
        count //= 2
    return count


def mlp_ready(i, count, head, part_us):
    unit = (i + 1) * (2 * MLP_PARTS // count) - 1
    return head + part_us * (unit // 2 + (0.9 if unit % 2 == 0 else 1.0))


def mlp_sums(mesh, z, buf, recv, full, sems):
    nx, ny = mesh.n["gx"], mesh.n["gy"]
    count = mlp_count(nx, ny, buf.shape[0])
    rows = buf.shape[0] // count
    sem0, out = 0, []
    for i in range(count):
        rounds = mlp_route(nx, ny, i, count)
        out.append(Sum(mesh, buf, i * rows, rows, rounds, recv, i * rows, sems, sem0, full))
        sem0 += 2 * sems_of(rounds)
    return out


def mlp_route(nx, ny, i, count):
    first, other = routes_of(nx, ny)
    if i == count - 1:
        return other
    return long_first(first) if i in (3, 6) else first


def long_first(rounds):
    return rounds[:1] + rounds[-1:] + rounds[1:-1]


def local_bwd_kernel(
    z, nx, ny, acts, before, done, gt_ref, xp_ref, r2_ref, o_ref, p_ref, qw_ref, code_ref, gain_ref, shift_ref, w_ref,
    wo_ref, part_ref, y_ref,
    pg_ref, dt0_ref, gwq_ref, gwo_ref, small_ref, buf_ref, yin_ref,
    ds_, dq_, dqkv, dtp, buf, recv, full, sems, ysems, copy_sem,
):
    step = pl.program_id(0)
    steps = pl.num_programs(0)
    mesh = Mesh2(nx, ny)
    sums = mlp_sums(mesh, z, buf, recv, full, sems)
    per = len(acts) // z.nb

    def tick(p):
        for i in range(z.nb):
            if acts[i * per + p]:

                @pl.when(step == i)
                def _():
                    act(sums, acts[i * per + p])

    units = z.early // 16

    def send(o, i):
        rows = pl.ds(units * i // z.nb * 16, (units * (i + 1) // z.nb - units * i // z.nb) * 16)
        return pltpu.make_async_remote_copy(
            src_ref=y_ref.at[o, rows], dst_ref=yin_ref.at[o, rows], send_sem=ysems.at[0, o * z.nb + i],
            recv_sem=ysems.at[1, o * z.nb + i], device_id=mesh.beside(nx - o),
            device_id_type=pl.DeviceIdType.MESH,
        )

    own_y = pltpu.make_async_copy(y_ref.at[0, : z.early], yin_ref.at[0], ysems.at[0, 0])

    @pl.when(step == 0)
    def _():
        gwq_ref[...] = jnp.zeros_like(gwq_ref)
        gwo_ref[...] = jnp.zeros_like(gwo_ref)
        small_ref[...] = jnp.zeros_like(small_ref)
        fetch = carry(sums, before, part_ref, copy_sem, False)
        for x in fetch:
            x.start()
        mesh.barrier(all_rounds(nx, ny), row=True)
        own_y.start()
        for x in fetch:
            x.wait()

    tick(0)
    for i in range(z.nb):

        @pl.when(step == i)
        def _(i=i):
            for o in range(1, nx):
                send(o, i).start()

    gt = gt_ref[0]
    dot = mm_nt(gt, wo_ref[...])
    for j in range(z.groups):
        ds_[j, : z.r, :] = dot[:, j * LANES : (j + 1) * LANES]
        if z.wide > z.r:
            ds_[j, z.r :, :] = jnp.zeros((z.wide - z.r, LANES), F32)
    gwo_ref[...] += mm_tn(o_ref[0], gt)
    masks = head_masks(SEG, z.hd)
    pad = jnp.zeros((SEG - 56, LANES), F32)
    scale = z.hd ** (-0.5)

    def windows(i, _):
        jobs = [(i * z.side + j, g) for j in range(z.side) for g in range(z.groups)]
        do = [
            jnp.concatenate([ds_[g, pl.ds(w, 56, stride=z.k), :], pad], axis=0).astype(BF16)
            for w, g in jobs
        ]
        dobd = [spread(x, masks) for x in do]
        dp = [mm_nt(qw_ref[w, 2 * z.groups + g], x) for (w, g), x in zip(jobs, dobd)]
        dv = [mm(p_ref[w, g], x) for (w, g), x in zip(jobs, dobd)]
        for (w, g), x in zip(jobs, dv):
            dq_[2 * z.groups + g, pl.ds(w, 56, stride=z.k), :] = x[:56]
        ds = []
        for (w, g), x in zip(jobs, dp):
            pf = p_ref[w, g].astype(F32)
            t = pf * x
            ds.append((t - pf * jnp.sum(t, axis=0, keepdims=True)).astype(BF16))
        dk = [mm(x, spread(qw_ref[w, g], masks)) for (w, g), x in zip(jobs, ds)]
        for (w, g), x in zip(jobs, dk):
            dq_[z.groups + g, pl.ds(w, 56, stride=z.k), :] = x[:56] * scale
        full = [mm_tn(x, qw_ref[w, z.groups + g]) for (w, g), x in zip(jobs, ds)]
        for (w, g), x in zip(jobs, full):
            dq_[g, pl.ds(w, 56, stride=z.k), :] = unspread(x, 56, SEG, masks) * scale
        return 0

    rounds = z.k // z.side
    for i in range(BWD_TICKS):
        lax.fori_loop(rounds * i // BWD_TICKS, rounds * (i + 1) // BWD_TICKS, windows, 0)
        tick(1 + i)
    for j in range(3 * z.groups):
        dqkv[:, j * LANES : (j + 1) * LANES] = dq_[j, : z.r, :].astype(BF16)
    dn = mm_nt(dqkv[...], w_ref[...])
    t = xp_ref[0].astype(F32)
    t = jnp.concatenate([r2_ref[0, : z.k, :], t[z.k :]], axis=0)
    hat, rstd = norm_stats(t)
    nt = (hat * gain_ref[...] + shift_ref[...]).astype(BF16)
    gwq_ref[...] += mm_tn(nt, dqkv[...])
    dt = gt.astype(F32) + norm_back(hat, rstd, gain_ref[...], dn)
    dt0_ref[0, : z.k, :] = dt[: z.k]
    dt0_ref[0, z.k :, :] = jnp.zeros((z.kp - z.k, z.d), F32)
    dtp[step] = dt.astype(BF16)
    small_ref[0:1, :] += colsum(dn * hat)
    small_ref[1:2, :] += colsum(dn)
    tick(1 + BWD_TICKS)

    @pl.when(step == steps - 1)
    def _():
        sel_t = one_hot_t(code_ref[...], z.gp * z.w)
        for g in range(z.ng):
            unpack_group(z, g, sel_t, dtp, pg_ref, None)

    tick(2 + BWD_TICKS)

    @pl.when(step == steps - 1)
    def _():
        out = carry(sums, done, buf_ref, copy_sem, True)
        for x in out:
            x.start()
        own_y.wait()
        for o in range(1, nx):
            for i in range(z.nb):
                send(o, i).wait()
        for x in out:
            x.wait()


def bit_list(count, axis):
    return [(axis, b) for b in range(count.bit_length() - 1)]


def n_bits(count):
    return count.bit_length() - 1


def stage_costs(nx, ny, rounds, size):
    xs = n_bits(ny) // 2
    costs, share = [], size
    for group in rounds:
        share /= 1 << len(group)
        wire = {}
        if group == (("gx", 0),):
            costs.append((2.5, wire))
            continue
        for axis, b in group:
            name, far = ("y", b > 1) if axis == "gx" else ("x", b > 0) if b < xs else ("z", b > xs)
            wire[name] = max(wire.get(name, 0.0), (8 if far else 4) * share / 85e3)
        costs.append((LATENCY_US, wire))
    return costs + costs[::-1]


class Mesh2:
    def __init__(self, nx, ny):
        self.n = {"gx": nx, "gy": ny}
        self.at = {"gx": lax.axis_index("gx"), "gy": lax.axis_index("gy")}

    def bit(self, which):
        axis, b = which
        return lax.rem(self.at[axis] // (1 << b), 2)

    def flips(self, group):
        return [
            [which for i, which in enumerate(group) if m >> (len(group) - 1 - i) & 1]
            for m in range(1, 1 << len(group))
        ]

    def partner(self, flipped):
        at = dict(self.at)
        for axis, b in flipped:
            at[axis] = at[axis] + (1 - 2 * self.bit((axis, b))) * (1 << b)
        return (at["gx"], at["gy"])

    def share(self, group, flipped=()):
        index = 0
        for which in group:
            bit = self.bit(which)
            index = 2 * index + (1 - bit if which in flipped else bit)
        return index

    def beside(self, o):
        return (lax.rem(self.at["gx"] + o, self.n["gx"]), self.at["gy"])

    def barrier(self, rounds, row=False):
        sem = pltpu.get_barrier_semaphore()
        sets = []
        for group in rounds:
            sets += [x for x in self.flips(group) if sorted(x) not in [sorted(y) for y in sets]]
        if row:
            sets = [x for x in sets if any(axis == "gy" for axis, _ in x)]
        others = [self.partner(x) for x in sets]
        if row:
            others += [self.beside(o) for o in range(1, self.n["gx"])]
        for other in others:
            pl.semaphore_signal(sem, inc=1, device_id=other, device_id_type=pl.DeviceIdType.MESH)
        pl.semaphore_wait(sem, len(others))


def routes_of(nx, ny):
    core, ys, g = [("gx", 0)], bit_list(nx, "gx")[1:], bit_list(ny, "gy")
    xs, zs = g[: len(g) // 2], g[len(g) // 2 :]
    if len(g) == 3:
        xs, zs = g[:1], g[1:]
    plane = [tuple(x) for x in zip(ys, xs)]
    line = [tuple(zs)]
    first = [tuple(core)] + plane + line
    other = [tuple(core)] + [tuple(x) for x in zip(xs, zs)]
    left = [x for x in ys + g if not any(x in group for group in other)]
    while left:
        other.append(tuple(left[:2]))
        left = left[2:]
    return first, other


def all_rounds(nx, ny):
    first, other = routes_of(nx, ny)
    return first + other


def place_of(order, nx, ny, dev):
    gx, gy = dev // ny, dev % ny
    p = 0
    for axis, b in order:
        p = 2 * p + (((gx if axis == "gx" else gy) >> b) & 1)
    return p


def flat(rounds):
    return [which for group in rounds for which in group]


def remote(mesh, src, dst, sems, i, flipped):
    return pltpu.make_async_remote_copy(
        src_ref=src, dst_ref=dst, send_sem=sems.at[0, i], recv_sem=sems.at[1, i],
        device_id=mesh.partner(flipped), device_id_type=pl.DeviceIdType.MESH,
    )


def sems_of(rounds):
    return sum((1 << len(group)) - 1 for group in rounds)


class Sum:
    def __init__(self, mesh, buf, start, rows, rounds, recv, recv_start, sems, sem0, full=None):
        self.mesh, self.buf, self.rounds, self.sems, self.sem0 = mesh, buf, rounds, sems, sem0
        self.recv, self.recv0, self.first, self.total = recv, recv_start, start, rows
        self.full = full
        self.n = len(rounds)
        self.stages = self.n * (2 if full is not None else 1)

    def held(self, s):
        off, rows = self.first, self.total
        for group in self.rounds[:s]:
            rows //= 1 << len(group)
            off = off + self.mesh.share(group) * rows
        return off, rows

    def recv_base(self, s):
        rows, base = self.total, self.recv0
        for group in self.rounds[:s]:
            part = rows >> len(group)
            base += rows - part
            rows = part
        return base

    def copies(self, s):
        back = s >= self.n
        r = 2 * self.n - 1 - s if back else s
        group = self.rounds[r]
        sem = self.sem0 + (sems_of(self.rounds) if back else 0) + sems_of(self.rounds[:r])
        off, rows = self.held(r)
        part = rows >> len(group)
        out = []
        for i, flipped in enumerate(self.mesh.flips(group)):
            if back:
                mine = pl.multiple_of(off + self.mesh.share(group) * part, 16)
                src = dst = self.full.at[pl.ds(mine, part)]
            else:
                theirs = pl.multiple_of(off + self.mesh.share(group, flipped) * part, 16)
                src = self.buf.at[pl.ds(theirs, part)]
                dst = self.recv.at[pl.ds(self.recv_base(r) + i * part, part)]
            out.append(remote(self.mesh, src, dst, self.sems, sem + i, flipped))
        return out

    def start(self, s):
        for x in self.copies(s):
            x.start()

    def finish(self, s):
        for x in self.copies(s):
            x.wait()
        if s < self.n:
            off, part = self.held(s + 1)
            base = self.recv_base(s)
            count = (1 << len(self.rounds[s])) - 1
            step = math.gcd(part, 64)
            into = self.full if s == self.n - 1 and self.full is not None else self.buf

            def add(i, _):
                mine = pl.ds(pl.multiple_of(off + i * step, 16), step)
                total = self.buf[mine, :].astype(F32)
                for j in range(count):
                    theirs = pl.ds(pl.multiple_of(base + j * part + i * step, 16), step)
                    total = total + self.recv[theirs, :].astype(F32)
                into[mine, :] = total.astype(BF16)
                return 0

            lax.fori_loop(0, part // step, add, 0)


def carry(sums, done, where, sem, out):
    copies = []
    for x, s in zip(sums, done):
        off, rows = x.held(min(s, 2 * x.n - s))
        rows = pl.ds(pl.multiple_of(off, 16), rows)
        mine = (x.buf if s < x.n else x.full).at[rows]
        src, dst = (mine, where.at[rows]) if out else (where.at[rows], mine)
        copies.append(pltpu.make_async_copy(src, dst, sem.at[len(copies)]))
    return copies


def plan(ready, done, stages, cost, slots, end, share=1.0):
    acts = [[] for _ in slots]
    done = list(done)
    running = [None] * len(done)
    free = {"x": 0.0, "y": 0.0, "z": 0.0}
    rate = {"x": 1.0, "y": share, "z": 1.0}
    for i, now in enumerate(slots):
        last = i == len(slots) - 1
        for j in range(len(done)):
            if ready[j] > now:
                continue
            stop = None
            if running[j] is not None:
                if now < running[j] and not last:
                    continue
                stop = done[j]
                done[j] += 1
                running[j] = None
            go = None
            if done[j] < stages and not last:
                latency, wire = cost[j][done[j]]
                over = max([now] + [max(free[c], now) + wire[c] / rate[c] for c in wire]) + latency
                if over <= end + SLACK_US:
                    go = done[j]
                    running[j] = over
                    for c in wire:
                        free[c] = max(free[c], now) + wire[c] / rate[c]
            if stop is not None or go is not None:
                acts[i].append((j, stop, go))
    return acts, done


def act(sums, acts):
    for j, stop, go in acts:
        if stop is not None:
            sums[j].finish(stop)
        if go is not None:
            sums[j].start(go)


class Gather:
    def __init__(self, mesh, buf, rows, rounds, sems, sem0):
        self.mesh, self.buf, self.rounds, self.sems, self.sem0 = mesh, buf, rounds, sems, sem0
        self.block = rows
        self.stages = len(rounds)

    def held(self, s):
        off, rows = 0, self.block << len(flat(self.rounds))
        for group in self.rounds[: self.stages - s]:
            rows >>= len(group)
            off = off + self.mesh.share(group) * rows
        return pl.multiple_of(off, 16), rows

    def copies(self, s):
        group = self.rounds[self.stages - 1 - s]
        here = self.buf.at[pl.ds(*self.held(s))]
        sem = self.sem0 + sems_of(self.rounds[: self.stages - 1 - s])
        return [
            remote(self.mesh, here, here, self.sems, sem + i, flipped)
            for i, flipped in enumerate(self.mesh.flips(group))
        ]

    def start(self, s):
        for x in self.copies(s):
            x.start()

    def finish(self, s):
        for x in self.copies(s):
            x.wait()


def region_bwd_kernel(
    z, nx, ny, done,
    dt0_ref, all_ref, o_ref, of_ref, p_ref, kv_ref, nr_ref, q_ref, nown_ref, own_ref, ord_ref, gain_ref,
    w_ref, wo_ref, gwq_ref, gwo_ref, smalla_ref, smallm_ref, gbu_ref, part_ref, y_ref,
    mlp_ref, att_ref, vec_ref, dnr_ref, dt0a_ref, dnown_ref, yin_ref,
    dobd, qbd, delta, acc, gacc, small, buf, recv, full, abuf, arecv, afull, vbuf, dbuf, drecv,
    sems, asems, ysems, copy_sem,
):
    step = pl.program_id(0)
    steps = pl.num_programs(0)
    mesh = Mesh2(nx, ny)
    d = z.d
    kc = all_ref.shape[0]
    nq = HEADS * z.w
    n = nx * ny
    scale = z.hd ** (-0.5)
    rest = mlp_sums(mesh, z, buf, recv, full, sems)
    first, other = routes_of(nx, ny)
    last = long_first(first)
    order_d = flat(last)
    bits = len(order_d)
    lane = lax.broadcasted_iota(jnp.int32, (z.w, d), 1) // z.hd

    late = pl.ds(z.early, z.r - z.early)

    def send(o):
        return pltpu.make_async_remote_copy(
            src_ref=y_ref.at[o, late], dst_ref=yin_ref.at[o], send_sem=ysems.at[0, o],
            recv_sem=ysems.at[1, o], device_id=mesh.beside(nx - o),
            device_id_type=pl.DeviceIdType.MESH,
        )

    own_y = pltpu.make_async_copy(y_ref.at[0, late], yin_ref.at[0], ysems.at[0, 0])

    @pl.when(step == 0)
    def _():
        fetch = carry(rest, done, part_ref, copy_sem, False)
        for x in fetch:
            x.start()
        mesh.barrier(all_rounds(nx, ny), row=True)
        for x in fetch:
            x.wait()
        for x, s in zip(rest, done):
            if s < x.stages:
                x.start(s)
        for o in range(1, nx):
            send(o).start()
        own_y.start()
        dt0 = jnp.concatenate([dt0_ref[c, : z.k, :] for c in range(z.nb)], axis=0)
        sel_t = one_hot_t(ord_ref[...], z.w).astype(F32)
        dt0 = jnp.dot(sel_t, dt0, precision=HIGH, preferred_element_type=F32)
        dt0a_ref[...] = dt0
        gr = dt0.astype(BF16)
        abuf[3 * d :, :] = (gwo_ref[...] + mm_tn(o_ref[...], gr)).astype(BF16)
        do = mm_nt(gr, wo_ref[...]).astype(BF16)
        zero = jnp.zeros_like(do)
        q = q_ref[...]
        for h in range(HEADS):
            dobd[h * z.w : (h + 1) * z.w, :] = jnp.where(lane == h, do, zero)
            qbd[h * z.w : (h + 1) * z.w, :] = jnp.where(lane == h, q, zero)
        prod = do.astype(F32) * of_ref[...]
        spread_prod = jnp.concatenate([jnp.where(lane == h, prod, 0.0) for h in range(HEADS)], axis=0)
        delta[...] = lax.dot_general(
            jnp.ones((8, d), F32), spread_prod, (((1,), (1,)), ((), ())), precision=HIGH,
            preferred_element_type=F32,
        )
        small[...] = jnp.zeros_like(small)
        small[2:3, :] = colsum(gr.astype(F32))
        acc[...] = jnp.zeros_like(acc)
        gacc[...] = gwq_ref[...]

    for i in range(1, n // (kc // z.w)):

        @pl.when(step == i)
        def _(i=i):
            for x, s in zip(rest, done):
                if s + i - 1 < x.stages:
                    x.finish(s + i - 1)
                if s + i < x.stages:
                    x.start(s + i)

    p = p_ref[...]
    ds = (p.astype(F32) * (mm_nt(kv_ref[:, d:], dobd[...]) - delta[0:1, :])).astype(BF16)
    dv = mm(p, dobd[...]).astype(BF16)
    dk = (mm(ds, qbd[...]) * scale).astype(BF16)
    dkv = jnp.concatenate([dk, dv], axis=1)
    gacc[:, d:] += mm_tn(nr_ref[...], dkv)
    dn = mm_nt(dkv, w_ref[:, d:])
    acc[...] += mm_tn(ds, kv_ref[:, :d])
    hat, _ = norm_stats(all_ref[...].astype(F32))
    small[0:1, :] += colsum(dn * hat)
    small[1:2, :] += colsum(dn)
    per = kc // z.w
    for j in range(per):
        dev = step * per + j
        at = {"gx": dev // ny, "gy": lax.rem(dev, ny)}
        place = 0
        for axis, b in order_d:
            place = 2 * place + lax.rem(at[axis] // (1 << b), 2)
        dbuf[pl.ds(pl.multiple_of(place * z.w, 16), z.w), :] = dn[j * z.w : (j + 1) * z.w].astype(BF16)

    @pl.when(step == steps - 1)
    def _():
        dq = acc[(HEADS - 1) * z.w :, :]
        for h in range(HEADS - 2, -1, -1):
            dq = jnp.where(lane == h, acc[h * z.w : (h + 1) * z.w, :], dq)
        dq = (dq * scale).astype(BF16)
        abuf[:d, :] = (gacc[:, :d] + mm_tn(nown_ref[...], dq)).astype(BF16)
        for f in range(1, 3):
            abuf[f * d : (f + 1) * d, :] = gacc[:, f * d : (f + 1) * d].astype(BF16)
        sums = []
        sem0 = bits
        split = max(x for x in (1, 2, 4) if (4 * d // x) % (16 * n) == 0 or x == 1)
        for i in range(split):
            rows = 4 * d // split
            rounds = first if i < 3 else last
            sums.append(Sum(mesh, abuf, i * rows, rows, rounds, arecv, i * rows, asems, sem0, afull))
            sem0 += 2 * sems_of(rounds)
        sums.append(Sum(mesh, dbuf, 0, n * z.w, last, drecv, 0, asems, sem0))
        for x in sums[:split]:
            x.start(0)
        dnown = mm_nt(dq, w_ref[:, :d])
        dnown_ref[...] = dnown
        hat, _ = norm_stats(own_ref[...].astype(F32))
        vbuf[0] = jnp.zeros_like(vbuf[0])
        vbuf[0, 0:1, :] = smalla_ref[0:1, :] + small[0:1, :] + colsum(dnown * hat)
        vbuf[0, 1:2, :] = smalla_ref[1:2, :] + small[1:2, :] + colsum(dnown)
        vbuf[0, 2:3, :] = smallm_ref[3:4, :] + small[2:3, :]
        vbuf[0, 3:6, :] = smallm_ref[0:3, :]
        row = 6
        for f in range(MLP_PARTS):
            for i in range(gbu_ref.shape[2] // d):
                vbuf[0, row : row + 1, :] = gbu_ref[f, :, i * d : (i + 1) * d]
                row += 1
        past = n // (kc // z.w) - 1
        queue = [(x, 0) for x in sums] + [(x, s + past) for x, s in zip(rest, done) if s + past < x.stages]
        started = [True] * split + [False] + [True] * (len(queue) - split - 1)
        vec = None
        for s in range(max(bits, 2 * len(first)) + 1):
            for i, (x, s0) in enumerate(queue):
                if s and s0 + s - 1 < x.stages:
                    x.finish(s0 + s - 1)
                if s0 + s < x.stages and (s or not started[i]):
                    x.start(s0 + s)
            if s <= bits:
                if s:
                    vec.wait()
                    vbuf[2 * s] = vbuf[2 * s - 2] + vbuf[2 * s - 1]
                if s < bits:
                    vec = remote(mesh, vbuf.at[2 * s], vbuf.at[2 * s + 1], asems, s, [order_d[s]])
                    vec.start()
        vec_ref[...] = vbuf[2 * bits]
        dnr_ref[...] = dbuf[pl.ds(pl.multiple_of(sums[split].held(len(last))[0], 16), z.w), :]
        outs = [
            pltpu.make_async_copy(full, mlp_ref, copy_sem.at[0]),
            pltpu.make_async_copy(afull, att_ref, copy_sem.at[1]),
        ]
        for x in outs:
            x.start()
        own_y.wait()
        for o in range(1, nx):
            send(o).wait()
        for x in outs:
            x.wait()


def finish_kernel(
    z, mlp_ref, att_ref, vec_ref, early_ref, late_ref, code_ref, own_ref, dnr_ref, dnown_ref, dt0a_ref, gain_ref,
    out_ref, first_ref, rg_ref, gwu_ref, gwd_ref, gwq_ref, gwo_ref, gbu_ref, *rows,
):
    f = pl.program_id(0)
    fc = gwd_ref.shape[0]
    d = z.d
    gwd_ref[...] = mlp_ref[:fc, :].astype(F32)
    for i in range(fc // d):
        gwu_ref[:, i * d : (i + 1) * d] = mlp_ref[fc + i * d : fc + (i + 1) * d, :].astype(F32)

    @pl.when(f < 3)
    def _():
        gwq_ref[...] = att_ref[...].astype(F32)

    @pl.when(f == 3)
    def _():
        gwo_ref[...] = att_ref[...].astype(F32)

    @pl.when(f == 0)
    def _():
        for i, row in enumerate(rows):
            row[...] = vec_ref[i : i + 1, :]
        gbu_ref[...] = vec_ref[6 : 6 + gbu_ref.shape[0], :]
        hat, rstd = norm_stats(own_ref[...].astype(F32))
        dn = dnr_ref[...].astype(F32) + dnown_ref[...]
        rg_ref[...] = (dt0a_ref[...] + norm_back(hat, rstd, gain_ref[...], dn)).astype(BF16)

    for step in range(MLP_PARTS):

        @pl.when(f == step)
        def _():
            sel_t = one_hot_t(code_ref[...], z.gp * z.w)
            for g in range(z.ng * step // MLP_PARTS, z.ng * (step + 1) // MLP_PARTS):
                rows = z.gp * z.k
                at = z.early // rows
                src, i = (early_ref, g) if g < at else (late_ref, g - at)
                unpack_group(z, g, sel_t, src, out_ref, first_ref, i)


def local(
    patches, regions, send_order, image_windows, attn_gain, attn_shift, w_qkv, w_out, b_out,
    mlp_gain, mlp_shift, w_up, b_up, w_down, b_down, upstream_patches, upstream_regions,
):
    nx, ny = lax.axis_size("gx"), lax.axis_size("gy")
    z = Sizes(patches.shape[0], patches.shape[1], patches.shape[2], nx)
    ff = w_up.shape[1]
    n = z.w * nx * ny
    gx = lax.axis_index("gx")
    dev = gx * ny + lax.axis_index("gy")
    sds = jax.ShapeDtypeStruct

    order = lax.dynamic_slice_in_dim(send_order, dev, 1, 0)[0].reshape(nx, z.k)
    tile = jnp.arange(nx, dtype=jnp.int32)
    order_t = jnp.take(order, (gx - tile) % nx, axis=0)
    place = jnp.arange(z.gp, dtype=jnp.int32) * z.w
    code_x = (order_t[:, None, :] + place[None, :, None]).reshape(-1)
    block = ((gx + tile) % nx)[:, None] * z.k + jnp.arange(z.k, dtype=jnp.int32)[None, :]
    code_e = (block[:, None, :] + place[None, :, None]).reshape(-1)
    order_t = order_t.reshape(-1)
    bounds = jnp.cumsum(image_windows)
    gain, shift = attn_gain[None], attn_shift[None]

    x_t = jnp.transpose(patches, (1, 0, 2))
    e_t = jnp.transpose(upstream_patches, (1, 0, 2))

    bits = n_bits(nx * ny)
    anywhere = pl.BlockSpec(memory_space=pl.ANY)
    vmem = pl.BlockSpec(memory_space=pltpu.VMEM)
    *packed, xp, qkv, regions_all = pl.pallas_call(
        functools.partial(start_kernel, z, nx, ny),
        in_specs=[anywhere, anywhere] + [vmem] * 7,
        out_specs=[vmem] * (z.nb + 1) + [anywhere, vmem],
        out_shape=[sds((z.r, z.d), BF16)] * z.nb + [
            sds((z.nb, z.r, z.d), BF16),
            sds((z.nb, z.r, 3 * z.d), BF16),
            sds((n, z.d), BF16),
        ],
        scratch_shapes=[
            pltpu.VMEM((z.tok, z.w, z.d), BF16),
            pltpu.VMEM((z.tok, z.w, z.d), BF16),
            pltpu.VMEM((z.nb, z.r, 3 * z.d), BF16),
            pltpu.VMEM((z.r, z.d), BF16),
            pltpu.VMEM((n, z.d), BF16),
            pltpu.SemaphoreType.DMA((2, sems_of(routes_of(nx, ny)[0]))),
            pltpu.SemaphoreType.DMA((2,)),
            pltpu.SemaphoreType.DMA((z.nb,)),
        ],
        compiler_params=params(collective_id=0, has_side_effects=True),
        name="start",
    )(x_t, e_t, upstream_regions, code_x[None], code_e[None], gain, shift, w_qkv, regions)

    e_in = [packed[0]]
    for o in range(1, nx):
        e_in.append(lax.ppermute(packed[o], "gx", [(i, (i + o) % nx) for i in range(nx)]))

    kc = 8 * z.w
    nq = HEADS * z.w
    r2, p_r, kv_all, nr_all, q_r, o_r, o_f, n_own = pl.pallas_call(
        functools.partial(region_fwd_kernel, z, kc, ny),
        in_specs=[vmem, vmem, pl.BlockSpec(memory_space=pltpu.SMEM)] + [vmem] * 6,
        out_shape=(
            sds((z.nb, z.kp, z.d), F32),
            sds((n, nq), BF16),
            sds((n, 2 * z.d), BF16),
            sds((n, z.d), BF16),
            sds((z.w, z.d), BF16),
            sds((z.w, z.d), BF16),
            sds((z.w, z.d), F32),
            sds((z.w, z.d), BF16),
        ),
        scratch_shapes=[pltpu.VMEM((n, nq), F32)],
        compiler_params=params(),
        name="region_fwd",
    )(
        regions_all, regions, bounds, order_t[None], gain, shift, w_qkv, w_out, b_out[None],
    )

    def tiled(*shape):
        return pl.BlockSpec((1,) + shape, lambda i: (i,) + (0,) * len(shape))

    def grouped(*shape):
        return pl.BlockSpec((z.k,) + shape, lambda i: (i,) + (0,) * len(shape))

    cols = z.per_group * SEG
    t2, p_w, qw, o_w = pl.pallas_call(
        functools.partial(local_fwd_kernel, z),
        grid=(z.nb,),
        in_specs=[
            tiled(z.r, 3 * z.d), tiled(z.r, z.d), tiled(z.kp, z.d), whole(1, z.d), whole(1, z.d),
            whole(z.d, 3 * z.d), whole(z.d, z.d), whole(1, z.d),
        ],
        out_specs=[
            tiled(z.r, z.d), grouped(z.groups, SEG, cols), grouped(3 * z.groups, SEG, LANES),
            tiled(z.r, z.d),
        ],
        out_shape=(
            sds((z.nb, z.r, z.d), F32),
            sds((z.w, z.groups, SEG, cols), BF16),
            sds((z.w, 3 * z.groups, SEG, LANES), BF16),
            sds((z.nb, z.r, z.d), BF16),
        ),
        scratch_shapes=[
            pltpu.VMEM((3 * z.groups, z.wide, LANES), F32),
            pltpu.VMEM((z.groups, z.wide, LANES), F32),
        ],
        compiler_params=params(),
        name="local_fwd",
    )(qkv, xp, r2, gain, shift, w_qkv, w_out, b_out[None])

    parts = MLP_PARTS
    fc = ff // parts
    total = 2 * ff
    first, other = routes_of(nx, ny)
    stages = 2 * len(first)
    n_sums = mlp_count(nx, ny, total)
    cost = [stage_costs(nx, ny, mlp_route(nx, ny, i, n_sums), total // n_sums * z.d * 2) for i in range(n_sums)]
    n_sems = sum(2 * sems_of(mlp_route(nx, ny, i, n_sums)) for i in range(n_sums))
    head, part_us, tail_us = 11.0, MLP_US / parts, 7.0
    slots = []
    for i in range(parts):
        base = head + part_us * i
        slots += [base + part_us * x for x in (0.0, 0.26, 0.32, 0.47, 0.55, 0.63, 0.71, 0.8, 0.9, 1.0)]
        slots.append(base + part_us + (tail_us if i == parts - 1 else 0.0))
    acts_m, done_m = plan(
        [mlp_ready(i, n_sums, head, part_us) - 0.05 for i in range(n_sums)], [0] * n_sums, stages, cost,
        slots, slots[-1],
    )
    keep = dict(pipeline_mode=pl.Buffered(1))

    def once(*shape):
        return pl.BlockSpec(shape, lambda *_: (0,) * len(shape), **keep)

    y, gt, part_sums, small_m, gbu = pl.pallas_call(
        functools.partial(mlp_kernel, z, nx, ny, acts_m, tuple(done_m)),
        grid=(parts,),
        in_specs=[pl.BlockSpec(memory_space=pl.ANY)] * (1 + z.nb) + [
            once(1, z.d), once(1, z.d), pl.BlockSpec((z.d, fc), lambda f: (0, f)),
            pl.BlockSpec((1, fc), lambda f: (0, f)), pl.BlockSpec((fc, z.d), lambda f: (f, 0)),
            once(1, z.d),
        ],
        out_specs=[
            anywhere, anywhere, anywhere, once(8, z.d),
            pl.BlockSpec((1, 1, fc), lambda f: (f, 0, 0)),
        ],
        out_shape=(
            sds((z.t, z.d), BF16),
            sds((z.t, z.d), BF16),
            sds((total, z.d), BF16),
            sds((8, z.d), F32),
            sds((parts, 1, fc), F32),
        ),
        scratch_shapes=[
            pltpu.VMEM((z.tp, z.d), BF16),
            pltpu.VMEM((z.tp, z.d), BF16),
            pltpu.VMEM((z.d + 16, z.tp), BF16),
            pltpu.VMEM((z.d + 16, z.tp), BF16),
            pltpu.VMEM((z.m, fc), F32),
            pltpu.VMEM((z.m, fc), F32),
            pltpu.VMEM((z.m, fc), F32),
            pltpu.VMEM((z.m, fc), F32),
            pltpu.VMEM((z.tp, fc), BF16),
            pltpu.VMEM((z.tp, fc), BF16),
            pltpu.VMEM((z.t, z.d), F32),
            pltpu.VMEM((z.t, z.d), F32),
            pltpu.VMEM((total, z.d), BF16),
            pltpu.VMEM((total, z.d), BF16),
            pltpu.VMEM((total, z.d), BF16),
            pltpu.SemaphoreType.DMA((2, n_sems)),
            pltpu.SemaphoreType.DMA((z.nb + 16,)),
        ],
        compiler_params=params(collective_id=1, has_side_effects=True),
        name="mlp",
    )(
        t2.reshape(z.t, z.d), *e_in, mlp_gain[None], mlp_shift[None], w_up, b_up[None], w_down,
        b_down[None],
    )
    y, gt = y.reshape(z.nb, z.r, z.d), gt.reshape(z.nb, z.r, z.d)

    head, part_us, tail_us = 2.0, BWD_US / z.nb, 2.0
    slots = []
    for i in range(z.nb):
        base = head + part_us * i
        slots += [base + part_us * x for x in (0.0, 0.3, 0.5, 0.7, 1.0)]
        slots.append(base + part_us + (tail_us if i == z.nb - 1 else 0.0))
    acts_b, done = plan([0.0] * n_sums, done_m, stages, cost, slots, slots[-1], 0.6)
    patch_grad, dt0, gwq, gwo, small_a, part_sums, y_early = pl.pallas_call(
        functools.partial(local_bwd_kernel, z, nx, ny, acts_b, tuple(done_m), tuple(done)),
        grid=(z.nb,),
        in_specs=[
            tiled(z.r, z.d), tiled(z.r, z.d), tiled(z.kp, z.d), tiled(z.r, z.d),
            grouped(z.groups, SEG, cols), grouped(3 * z.groups, SEG, LANES),
            whole(1, z.nb * z.gp * z.k), whole(1, z.d), whole(1, z.d), whole(z.d, 3 * z.d),
            whole(z.d, z.d), anywhere, anywhere,
        ],
        out_specs=[
            once(z.tok, z.w, z.d), tiled(z.kp, z.d), once(z.d, 3 * z.d), once(z.d, z.d),
            once(8, z.d), anywhere, anywhere,
        ],
        out_shape=(
            sds((z.tok, z.w, z.d), BF16),
            sds((z.nb, z.kp, z.d), F32),
            sds((z.d, 3 * z.d), F32),
            sds((z.d, z.d), F32),
            sds((8, z.d), F32),
            sds((total, z.d), BF16),
            sds((z.nb, z.early, z.d), BF16),
        ),
        scratch_shapes=[
            pltpu.VMEM((z.groups, z.wide, LANES), F32),
            pltpu.VMEM((3 * z.groups, z.wide, LANES), F32),
            pltpu.VMEM((z.r, 3 * z.d), BF16),
            pltpu.VMEM((z.nb, z.r, z.d), BF16),
            pltpu.VMEM((total, z.d), BF16),
            pltpu.VMEM((total, z.d), BF16),
            pltpu.VMEM((total, z.d), BF16),
            pltpu.SemaphoreType.DMA((2, n_sems)),
            pltpu.SemaphoreType.DMA((2, nx * z.nb)),
            pltpu.SemaphoreType.DMA((n_sums,)),
        ],
        compiler_params=params(collective_id=2, has_side_effects=True),
        name="local_bwd",
    )(gt, xp, r2, o_w, p_w, qw, code_x[None], gain, shift, w_qkv, w_out, part_sums, y)

    def keys(*shape):
        return pl.BlockSpec((kc,) + shape, lambda i: (i,) + (0,) * len(shape))

    mlp_total, att_total, vec, dnr, dt0a, dn_own, y_late = pl.pallas_call(
        functools.partial(region_bwd_kernel, z, nx, ny, tuple(done)),
        grid=(n // kc,),
        in_specs=[
            once(z.nb, z.kp, z.d), keys(z.d), once(z.w, z.d), once(z.w, z.d), keys(nq), keys(2 * z.d),
            keys(z.d), once(z.w, z.d), once(z.w, z.d), once(z.w, z.d), once(1, z.w), once(1, z.d),
            once(z.d, 3 * z.d), once(z.d, z.d), once(z.d, 3 * z.d), once(z.d, z.d), once(8, z.d),
            once(8, z.d), once(parts, 1, fc), anywhere, anywhere,
        ],
        out_specs=[
            anywhere, anywhere, once(16, z.d), once(z.w, z.d), once(z.w, z.d), once(z.w, z.d), anywhere,
        ],
        out_shape=(
            sds((total, z.d), BF16),
            sds((4 * z.d, z.d), BF16),
            sds((16, z.d), F32),
            sds((z.w, z.d), BF16),
            sds((z.w, z.d), F32),
            sds((z.w, z.d), F32),
            sds((z.nb, z.r - z.early, z.d), BF16),
        ),
        scratch_shapes=[
            pltpu.VMEM((nq, z.d), BF16),
            pltpu.VMEM((nq, z.d), BF16),
            pltpu.VMEM((8, nq), F32),
            pltpu.VMEM((nq, z.d), F32),
            pltpu.VMEM((z.d, 3 * z.d), F32),
            pltpu.VMEM((8, z.d), F32),
            pltpu.VMEM((total, z.d), BF16),
            pltpu.VMEM((total, z.d), BF16),
            pltpu.VMEM((total, z.d), BF16),
            pltpu.VMEM((4 * z.d, z.d), BF16),
            pltpu.VMEM((4 * z.d, z.d), BF16),
            pltpu.VMEM((4 * z.d, z.d), BF16),
            pltpu.VMEM((2 * bits + 1, 16, z.d), F32),
            pltpu.VMEM((n, z.d), BF16),
            pltpu.VMEM((n, z.d), BF16),
            pltpu.SemaphoreType.DMA((2, n_sems)),
            pltpu.SemaphoreType.DMA((2, bits + 9 * sems_of(first))),
            pltpu.SemaphoreType.DMA((2, nx)),
            pltpu.SemaphoreType.DMA((max(n_sums, 2),)),
        ],
        compiler_params=params(collective_id=3, has_side_effects=True),
        name="region_bwd",
    )(
        dt0, regions_all, o_r, o_f, p_r, kv_all, nr_all, q_r, n_own, regions, order_t[None], gain, w_qkv,
        w_out, gwq, gwo, small_a, small_m, gbu, part_sums, y,
    )

    out_p, out_r, region_grad, gwu, gwd, gwq, gwo, gbu, *rows = pl.pallas_call(
        functools.partial(finish_kernel, z),
        grid=(parts,),
        in_specs=[
            pl.BlockSpec((2 * fc, z.d), lambda f: (f, 0)), pl.BlockSpec((z.d, z.d), lambda f: (f, 0)),
            once(16, z.d), once(z.nb, z.early, z.d), once(z.nb, z.r - z.early, z.d), once(1, z.nb * z.gp * z.k), once(z.w, z.d),
            once(z.w, z.d), once(z.w, z.d), once(z.w, z.d), once(1, z.d),
        ],
        out_specs=[
            once(z.tok, z.w, z.d), once(z.w, z.d), once(z.w, z.d),
            pl.BlockSpec((z.d, fc), lambda f: (0, f)), pl.BlockSpec((fc, z.d), lambda f: (f, 0)),
            pl.BlockSpec((z.d, z.d), lambda f: (0, jnp.minimum(f, 2))), once(z.d, z.d),
            once(ff // z.d, z.d),
        ] + [once(1, z.d)] * 6,
        out_shape=[
            sds((z.tok, z.w, z.d), BF16), sds((z.w, z.d), BF16), sds((z.w, z.d), BF16),
            sds((z.d, ff), F32), sds((ff, z.d), F32), sds((z.d, 3 * z.d), F32), sds((z.d, z.d), F32),
            sds((ff // z.d, z.d), F32),
        ] + [sds((1, z.d), F32)] * 6,
        compiler_params=params(),
        name="finish",
    )(mlp_total, att_total, vec, y_early, y_late, code_e[None], regions, dnr, dn_own, dt0a, gain)
    rows = [x[0] for x in rows]
    return (
        jnp.transpose(out_p, (1, 0, 2)),
        out_r,
        jnp.transpose(patch_grad, (1, 0, 2)),
        region_grad,
        rows[0],
        rows[1],
        gwq,
        gwo,
        rows[2],
        rows[3],
        rows[4],
        gwu,
        gbu.reshape(ff),
        gwd,
        rows[5],
    )


def solution(mesh):
    split = ("gx", "gy")
    rows3, rows2, full = P(split, None, None), P(split, None), P()
    in_specs = (rows3, rows2) + (full,) * 13 + (rows3, rows2)
    out_specs = (rows3, rows2, rows3, rows2) + (full,) * 11
    return jax.shard_map(local, mesh=mesh, in_specs=in_specs, out_specs=out_specs, check_vma=False)
```

```python
import functools
import math

import jax
import jax.numpy as jnp
from jax import lax
from jax.experimental import pallas as pl
from jax.experimental.pallas import tpu as pltpu
from jax.sharding import PartitionSpec as P

HEADS = 16
EPS = 1e-05
F32 = jnp.float32
BF16 = jnp.bfloat16
LOG2E = 1.4426950408889634
VMEM_LIMIT = 60 * 1024 * 1024
HIGH = lax.Precision.HIGHEST
LANES = 128
MLP_PARTS = 4
BWD_TICKS = 3
MLP_US = 60.0
BWD_US = 36.0
LATENCY_US = 3.0
SLACK_US = 2.5
SEG = 64


def mm(a, b):
    return lax.dot_general(a, b, (((1,), (0,)), ((), ())), preferred_element_type=F32)


def mm_nt(a, b):
    return lax.dot_general(a, b, (((1,), (1,)), ((), ())), preferred_element_type=F32)


def mm_tn(a, b):
    return lax.dot_general(a, b, (((0,), (0,)), ((), ())), preferred_element_type=F32)


def norm_stats(v):
    average = jnp.mean(v, axis=-1, keepdims=True)
    centered = v - average
    variance = jnp.mean(centered * centered, axis=-1, keepdims=True)
    rstd = lax.rsqrt(variance + EPS)
    return centered * rstd, rstd


def norm_back(hat, rstd, gain, dn):
    dhat = dn * gain
    m1 = jnp.mean(dhat, axis=-1, keepdims=True)
    m2 = jnp.mean(dhat * hat, axis=-1, keepdims=True)
    return rstd * (dhat - m1 - hat * m2)


def colsum(v):
    return jnp.sum(v, axis=0, keepdims=True)


def gelu_both(u):
    a = jnp.abs(u)
    d = 1.0 + (0.3275911 * 0.7071067811865476) * a
    r = pl.reciprocal(d, approx=True)
    t = r * (2.0 - d * r)
    e = jnp.exp2((u * u) * (-0.5 * LOG2E))
    poly = t * (
        0.127414796
        + t * (-0.142248368 + t * (0.7107068705 + t * (-0.7265760135 + t * 0.5307027145)))
    )
    tail = poly * e
    cdf = jnp.where(u >= 0.0, 1.0 - tail, tail)
    return u * cdf, cdf + u * (e * 0.3989422804014327)


def head_masks(rows, head_dim):
    lane = lax.broadcasted_iota(jnp.int32, (rows, LANES), 1)
    return [(lane // head_dim) == h for h in range(LANES // head_dim)]


def spread(v, masks):
    zero = jnp.zeros_like(v)
    return jnp.concatenate([jnp.where(m, v, zero) for m in masks], axis=0)


def unspread(full, rows, stride, masks):
    out = full[(len(masks) - 1) * stride : (len(masks) - 1) * stride + rows]
    for h in range(len(masks) - 2, -1, -1):
        out = jnp.where(masks[h][:rows], full[h * stride : h * stride + rows], out)
    return out


def one_hot(code_col, count):
    rows = code_col.shape[0]
    return (lax.broadcasted_iota(jnp.int32, (rows, count), 1) == code_col).astype(F32).astype(BF16)


def one_hot_t(code_row, count):
    rows = code_row.shape[1]
    return (lax.broadcasted_iota(jnp.int32, (count, rows), 0) == code_row).astype(F32).astype(BF16)


def whole(*shape):
    return pl.BlockSpec(shape, lambda *_: (0,) * len(shape))


class Sizes:
    def __init__(self, per_dev, patch_tokens, width, count_gx):
        self.w = per_dev
        self.tok = patch_tokens
        self.d = width
        self.nb = count_gx
        self.k = per_dev // count_gx
        step = 16 // math.gcd(16, self.k)
        self.pos = -(-(patch_tokens + 1) // step) * step
        self.gp = step
        while (self.gp * self.k) % 16:
            self.gp *= 2
        self.ng = self.pos // self.gp
        self.early = self.ng // 2 * self.gp * self.k
        self.r = self.pos * self.k
        self.wide = 56 * self.k
        self.hd = width // HEADS
        self.groups = width // LANES
        self.per_group = LANES // self.hd
        self.chunk = self.r // 3 if self.r % 48 == 0 else self.r
        self.kp = -(-self.k // 16) * 16
        self.side = max(j for j in range(1, 5) if self.k % j == 0)
        self.t = self.nb * self.r
        self.tp = -(-self.t // 512) * 512
        self.m = max(m for m in range(16, 449, 16) if self.t % (2 * m) == 0)


def params(**kw):
    return pltpu.CompilerParams(vmem_limit_bytes=VMEM_LIMIT, **kw)


def pack_group(z, g, sel_t, x_ref, first_ref, outs):
    pieces = []
    for p in range(g * z.gp, (g + 1) * z.gp):
        if p == 0:
            pieces.append(jnp.zeros((z.w, z.d), BF16) if first_ref is None else first_ref[...])
        elif p <= z.tok:
            pieces.append(x_ref[p - 1])
        else:
            pieces.append(jnp.zeros((z.w, z.d), BF16))
    got = mm_tn(sel_t, jnp.concatenate(pieces, axis=0)).astype(BF16)
    rows = z.gp * z.k
    for c in range(z.nb):
        outs[c][g * rows : (g + 1) * rows, :] = got[c * rows : (c + 1) * rows]


def unpack_group(z, g, sel_t, packed_ref, out_ref, first_ref, at=None):
    rows = z.gp * z.k
    here = slice((g if at is None else at) * rows, ((g if at is None else at) + 1) * rows)
    src = jnp.concatenate([packed_ref[c, here, :] for c in range(z.nb)], axis=0)
    got = mm(sel_t, src).astype(BF16)
    for i in range(z.gp):
        p = g * z.gp + i
        piece = got[i * z.w : (i + 1) * z.w]
        if p == 0:
            if first_ref is not None:
                first_ref[...] = piece
        elif p <= z.tok:
            out_ref[p - 1] = piece


def start_kernel(
    z, nx, ny, x_ref, e_ref, first_ref, codex_ref, codee_ref, gain_ref, shift_ref, w_ref, own_ref, *refs
):
    packed, refs = refs[: z.nb], refs[z.nb :]
    xp_ref, qkv_ref, all_ref, xs, es, qs, nt, buf, sems, load_sems, out_sems = refs
    loads = [
        pltpu.make_async_copy(src, dst, load_sems.at[i])
        for i, (src, dst) in enumerate(((e_ref, es), (x_ref, xs)))
    ]
    for x in loads:
        x.start()
    mesh = Mesh2(nx, ny)
    rounds = routes_of(nx, ny)[0]
    gather = Gather(mesh, buf, z.w, rounds, sems, 0)
    mesh.barrier(rounds)
    buf[pl.ds(*gather.held(0)), :] = own_ref[...]
    gather.start(0)

    def pack(src, code_ref, first, outs):
        sel_t = one_hot_t(code_ref[...], z.gp * z.w)
        for g in range(z.ng):
            pack_group(z, g, sel_t, src, first, outs)

    outs = [pltpu.make_async_copy(qs.at[c], qkv_ref.at[c], out_sems.at[c]) for c in range(z.nb)]

    def project(c):
        hat, _ = norm_stats(xp_ref[c].astype(F32))
        nt[...] = (hat * gain_ref[...] + shift_ref[...]).astype(BF16)
        qs[c] = mm(nt[...], w_ref[...]).astype(BF16)
        outs[c].start()

    stages = gather.stages
    loads[0].wait()
    pack(es, codee_ref, first_ref, packed)
    loads[1].wait()
    pack(xs, codex_ref, None, [xp_ref.at[c] for c in range(z.nb)])
    for s in range(1, stages + 1):
        gather.finish(s - 1)
        if s < stages:
            gather.start(s)
            for c in range(z.nb * (s - 1) // (stages - 1), z.nb * s // (stages - 1)):
                project(c)
    n = nx * ny
    order = flat(rounds)
    for dev in range(n):
        p = place_of(order, nx, ny, dev)
        all_ref[dev * z.w : (dev + 1) * z.w, :] = buf[p * z.w : (p + 1) * z.w, :]
    for x in outs:
        x.wait()


def region_fwd_kernel(
    z, kc, ny, all_ref, own_ref, bounds_ref, ord_ref, gain_ref, shift_ref, w_ref, wo_ref, bo_ref,
    r2_ref, p_ref, kv_ref, nr_ref, q_ref, o_ref, of_ref, nown_ref, s_ref,
):
    n = all_ref.shape[0]
    nq = HEADS * z.w
    hat, _ = norm_stats(own_ref[...].astype(F32))
    nown = (hat * gain_ref[...] + shift_ref[...]).astype(BF16)
    nown_ref[...] = nown
    q = mm(nown, w_ref[:, : z.d]).astype(BF16)
    q_ref[...] = q
    lane = lax.broadcasted_iota(jnp.int32, (z.w, z.d), 1) // z.hd
    zero = jnp.zeros_like(q)
    qbd = jnp.concatenate([jnp.where(lane == h, q, zero) for h in range(HEADS)], axis=0)
    scale = z.hd ** (-0.5) * LOG2E
    dev = lax.axis_index("gx") * ny + lax.axis_index("gy")
    window = dev * z.w + lax.broadcasted_iota(jnp.int32, (1, nq), 1) % z.w

    def image(j, span):
        low, high = span
        bound = bounds_ref[j]
        return jnp.where(bound <= window, bound, low), jnp.where(bound > window, jnp.minimum(high, bound), high)

    low, high = lax.fori_loop(
        0, bounds_ref.shape[0], image,
        (jnp.zeros((1, nq), jnp.int32), jnp.full((1, nq), n, jnp.int32)),
    )
    key = lax.broadcasted_iota(jnp.int32, (kc, nq), 0)

    def reach(j, span):
        bound = bounds_ref[j]
        return (
            jnp.where(bound <= dev * z.w, bound, span[0]),
            jnp.where(bound > dev * z.w + z.w - 1, jnp.minimum(span[1], bound), span[1]),
        )

    begin, end = lax.fori_loop(0, bounds_ref.shape[0], reach, (jnp.int32(0), jnp.int32(n)))
    begin, end = begin // kc, (end + kc - 1) // kc

    def blank(i, _):
        rows = pl.ds(pl.multiple_of(i * kc, kc), kc)
        nr_ref[rows, :] = jnp.zeros((kc, z.d), BF16)
        kv_ref[rows, :] = jnp.zeros((kc, 2 * z.d), BF16)
        p_ref[rows, :] = jnp.zeros((kc, nq), BF16)
        return 0

    lax.fori_loop(0, begin, blank, 0)
    lax.fori_loop(end, n // kc, blank, 0)

    def scores(i, top):
        rows = pl.ds(pl.multiple_of(i * kc, kc), kc)
        hat, _ = norm_stats(all_ref[rows, :].astype(F32))
        nr = (hat * gain_ref[...] + shift_ref[...]).astype(BF16)
        nr_ref[rows, :] = nr
        kv = mm(nr, w_ref[:, z.d :]).astype(BF16)
        kv_ref[rows, :] = kv
        s = mm_nt(kv[:, : z.d], qbd) * scale
        s = jnp.where((key >= low - i * kc) & (key < high - i * kc), s, -1e30)
        s_ref[rows, :] = s
        return jnp.maximum(top, jnp.max(s, axis=0, keepdims=True))

    top = lax.fori_loop(begin, end, scores, jnp.full((1, nq), -1e30, F32))

    def weigh(i, total):
        rows = pl.ds(pl.multiple_of(i * kc, kc), kc)
        p = jnp.exp2(s_ref[rows, :] - top)
        s_ref[rows, :] = p
        return total + jnp.sum(p, axis=0, keepdims=True)

    total = lax.fori_loop(begin, end, weigh, jnp.zeros((1, nq), F32))
    inverse = 1.0 / total

    def attend(i, acc):
        rows = pl.ds(pl.multiple_of(i * kc, kc), kc)
        p = (s_ref[rows, :] * inverse).astype(BF16)
        p_ref[rows, :] = p
        return acc + mm_tn(p, kv_ref[rows, z.d :])

    full = lax.fori_loop(begin, end, attend, jnp.zeros((nq, z.d), F32))
    o = full[(HEADS - 1) * z.w :]
    for h in range(HEADS - 2, -1, -1):
        o = jnp.where(lane == h, full[h * z.w : (h + 1) * z.w], o)
    of_ref[...] = o
    o = o.astype(BF16)
    o_ref[...] = o
    r2 = own_ref[...].astype(F32) + mm(o, wo_ref[...]) + bo_ref[...]
    sel_t = one_hot_t(ord_ref[...], z.w).astype(F32)
    r2 = lax.dot_general(
        sel_t, r2, (((0,), (0,)), ((), ())), precision=HIGH, preferred_element_type=F32
    )
    for c in range(z.nb):
        r2_ref[c, : z.k, :] = r2[c * z.k : (c + 1) * z.k]
        r2_ref[c, z.k :, :] = jnp.zeros((z.kp - z.k, z.d), F32)


def local_fwd_kernel(
    z, qkv_ref, xp_ref, r2_ref, gain_ref, shift_ref, w_ref, wo_ref, bo_ref,
    t2_ref, p_ref, qw_ref, o_ref, qs, os,
):
    tiles = 3 * z.groups
    for j in range(tiles):
        qs[j, : z.r, :] = qkv_ref[0, :, j * LANES : (j + 1) * LANES].astype(F32)
        if z.wide > z.r:
            qs[j, z.r :, :] = jnp.zeros((z.wide - z.r, LANES), F32)
    hat, _ = norm_stats(r2_ref[0])
    nt = (hat * gain_ref[...] + shift_ref[...]).astype(BF16)
    reg = mm(nt, w_ref[...]).astype(BF16).astype(F32)
    for j in range(tiles):
        qs[j, : z.k, :] = reg[: z.k, j * LANES : (j + 1) * LANES]
    masks = head_masks(SEG, z.hd)
    pad = jnp.zeros((SEG - 56, LANES), F32)
    valid = lax.broadcasted_iota(jnp.int32, (56, z.per_group * SEG), 0) < z.tok + 1
    scale = z.hd ** (-0.5) * LOG2E
    tail = jnp.zeros((SEG - 56, z.per_group * SEG), F32)

    def windows(i, _):
        jobs = [(i * z.side + j, g) for j in range(z.side) for g in range(z.groups)]

        def load(w, j):
            rows = qs[j, pl.ds(w, 56, stride=z.k), :]
            got = jnp.concatenate([rows, pad], axis=0).astype(BF16)
            qw_ref[w, j] = got
            return got

        q = [load(w, g) for w, g in jobs]
        k = [load(w, z.groups + g) for w, g in jobs]
        v = [load(w, 2 * z.groups + g) for w, g in jobs]
        s = [mm_nt(kk, spread(qq, masks))[:56] for qq, kk in zip(q, k)]
        s = [jnp.where(valid, x, -1e30) for x in s]
        p = [jnp.exp2((x - jnp.max(x, axis=0, keepdims=True)) * scale) for x in s]
        p = [x * (1.0 / jnp.sum(x, axis=0, keepdims=True)) for x in p]
        p = [jnp.concatenate([x, tail], axis=0).astype(BF16) for x in p]
        for (w, g), x in zip(jobs, p):
            p_ref[w, g] = x
        full = [mm_tn(x, vv) for x, vv in zip(p, v)]
        for (w, g), x in zip(jobs, full):
            os[g, pl.ds(w, 56, stride=z.k), :] = unspread(x, 56, SEG, masks)
        return 0

    lax.fori_loop(0, z.k // z.side, windows, 0)
    for i in range(z.r // z.chunk):
        rows = slice(i * z.chunk, (i + 1) * z.chunk)
        o = jnp.concatenate([os[g, rows, :] for g in range(z.groups)], axis=1).astype(BF16)
        o_ref[0, rows, :] = o
        t2_ref[0, rows, :] = xp_ref[0, rows, :].astype(F32) + mm(o, wo_ref[...]) + bo_ref[...]
    t2_ref[0, : z.k, :] = t2_ref[0, : z.k, :] + r2_ref[0, : z.k, :]


def tiles_dot(lhs, w, acc, transposed=False):
    side = 256
    for k in range(w.shape[0] // side):
        for j in range(len(acc)):
            ks, js = slice(k * side, (k + 1) * side), slice(j * side, (j + 1) * side)
            pltpu.matmul_push_rhs(w[js, ks] if transposed else w[ks, js], k % 2, j, transpose=transposed)
            pltpu.matmul_acc_lhs(acc[j], lhs(k), load_staged_rhs=k % 2)


def mlp_kernel(z, nx, ny, acts, done, *refs):
    (t2_ref, *e_refs), refs = refs[: 1 + z.nb], refs[1 + z.nb :]
    (
        gain_ref, shift_ref, wu_ref, bu_ref, wd_ref, bd_ref,
        y_ref, gt_ref, buf_ref, small_ref, gbu_ref,
        n2, e, n2_t, e_t, h0, h1, d0, d1, active, dh, yacc, dn, buf, recv, full, sems, copy_sem,
    ) = refs
    f = pl.program_id(0)
    parts = pl.num_programs(0)
    mesh = Mesh2(nx, ny)
    sums = mlp_sums(mesh, z, buf, recv, full, sems)
    per = len(acts) // MLP_PARTS
    sub, side = math.gcd(z.m, 32), 256
    fc = wu_ref.shape[1]
    m = h0.shape[0]
    chunks = z.t // m

    def rows_of(c):
        return slice(c * m, (c + 1) * m)

    def tick(p):
        for step in range(len(acts) // per):
            if acts[step * per + p]:

                @pl.when(f == step)
                def _():
                    act(sums, acts[step * per + p])

    @pl.when(f == 0)
    def _():
        fetch = [
            pltpu.make_async_copy(e_refs[c], e.at[c * z.r : (c + 1) * z.r, :], copy_sem.at[c])
            for c in range(z.nb)
        ]
        begin = [
            pltpu.make_async_copy(t2_ref.at[rows_of(c), :], yacc.at[rows_of(c), :], copy_sem.at[8 + c])
            for c in range(chunks)
        ]
        for x in begin + fetch:
            x.start()
        mesh.barrier(all_rounds(nx, ny))

        def prepare(i, _):
            rows = pl.ds(pl.multiple_of(i * sub, 16), sub)
            hat, _ = norm_stats(yacc[rows, :])
            n2[rows, :] = (hat * gain_ref[...] + shift_ref[...]).astype(BF16)
            dn[rows, :] = jnp.zeros((sub, z.d), F32)
            return 0

        for c in range(chunks):
            begin[c].wait()
            lax.fori_loop(c * (m // sub), (c + 1) * (m // sub), prepare, 0, unroll=13)
        for x in fetch:
            x.wait()
        if z.tp > z.t:
            for x in (n2, e, active, dh):
                x[z.t :, :] = jnp.zeros((z.tp - z.t, x.shape[1]), BF16)

        def turn(i, _):
            span = pl.ds(pl.multiple_of(i * side, side), side)
            n2_t[: z.d, span] = n2[span, :].T
            e_t[: z.d, span] = e[span, :].T
            n2_t[z.d :, span] = jnp.ones((16, side), BF16)
            e_t[z.d :, span] = jnp.zeros((16, side), BF16)
            return 0

        lax.fori_loop(0, z.tp // side, turn, 0)

    results = [
        [
            pltpu.make_async_copy(n2.at[rows_of(c), :], y_ref.at[rows_of(c), :], copy_sem.at[8 + 2 * (c % 8)]),
            pltpu.make_async_copy(e.at[rows_of(c), :], gt_ref.at[rows_of(c), :], copy_sem.at[9 + 2 * (c % 8)]),
        ]
        for c in range(chunks)
    ]
    slots = (h0, h1, d0, d1)
    again = [
        pltpu.make_async_copy(t2_ref.at[rows_of(c), :], slots[c % 4], copy_sem.at[c % 4])
        for c in range(chunks)
    ]
    tick(0)
    bias = bu_ref[...]

    def stream(*accs):
        one, two = accs[:2], accs[2:]
        h, d = (h0, h1), (d0, d1)

        def rows(c):
            return pl.ds(pl.multiple_of(c * m, 16), m)

        def up(c, slot):
            tiles_dot(lambda k: n2[rows(c), k * side : (k + 1) * side], wu_ref, one)
            for j in range(2):
                h[slot][:, j * side : (j + 1) * side] = pltpu.matmul_pop(one[j])
            tiles_dot(lambda k: e[rows(c), k * side : (k + 1) * side], wd_ref, two, True)
            for j in range(2):
                d[slot][:, j * side : (j + 1) * side] = pltpu.matmul_pop(two[j])

        def down(c):
            tiles_dot(lambda k: active[rows(c), k * side : (k + 1) * side], wd_ref, one)
            for j in range(2):
                yacc[rows(c), j * side : (j + 1) * side] += pltpu.matmul_pop(one[j])
            tiles_dot(lambda k: dh[rows(c), k * side : (k + 1) * side], wu_ref, two, True)
            for j in range(2):
                dn[rows(c), j * side : (j + 1) * side] += pltpu.matmul_pop(two[j])

        def middle(c, slot):
            for i in range(m // 16):
                r, o = slice(i * 16, (i + 1) * 16), pl.ds(pl.multiple_of(c * m + i * 16, 16), 16)
                value, slope = gelu_both(h[slot][r, :] + bias)
                active[o, :] = value.astype(BF16)
                dh[o, :] = (d[slot][r, :] * slope).astype(BF16)

        def pair(i, _):
            for slot in range(2):
                c = 2 * i + slot
                up(jnp.minimum(c + 1, chunks - 1), 1 - slot)
                middle(c, slot)
                down(c)
            return 0

        up(0, 0)
        for i in range(3):
            lax.fori_loop(chunks // 2 * i // 3, chunks // 2 * (i + 1) // 3, pair, 0)
            tick(1 + i)

    pl.run_scoped(stream, *[pltpu.ACC(mxu_id=i)((m, side), F32) for i in (0, 1, 0, 1)])
    @pl.when(f == parts - 1)
    def _():
        for x in again[:4]:
            x.start()

    tick(4)
    here = pl.multiple_of(f * (2 * fc), 16)

    def gradients(acc0, acc1):
        acc = (acc0, acc1)
        halves = [slice(j * side, (j + 1) * side) for j in range(2)]

        def over_tokens(left, right):
            def two(i, _):
                for k in range(2):
                    span = pl.ds(pl.multiple_of((2 * i + k) * side, side), side)
                    for j in range(2):
                        pltpu.matmul_push_rhs(right[span, halves[j]], k, j)
                        pltpu.matmul_acc_lhs(acc[j], left[:, span], load_staged_rhs=k)
                return 0

            lax.fori_loop(0, z.tp // (2 * side), two, 0)

        over_tokens(e_t, active)
        for j in range(2):
            rows = pl.ds(pl.multiple_of(here + j * side, 16), side)
            buf[rows, :] = pltpu.matmul_pop(acc[j])[: z.d].T.astype(BF16)
        tick(5)
        over_tokens(n2_t, dh)
        for j in range(2):
            got = pltpu.matmul_pop(acc[j])
            buf[pl.ds(pl.multiple_of(here + fc, 16), z.d), halves[j]] = got[: z.d].astype(BF16)
            gbu_ref[0, :, halves[j]] = got[z.d : z.d + 1]

    pl.run_scoped(
        gradients, pltpu.ACC(mxu_id=0)((z.d + 16, side), F32), pltpu.ACC(mxu_id=1)((z.d + 16, side), F32)
    )
    tick(6)

    @pl.when(f == parts - 1)
    def _():
        zero = jnp.zeros((1, z.d), F32)
        got = (zero,) * 4
        for c in range(chunks):
            again[c].wait()

            def close(i, sums, c=c):
                here = pl.ds(pl.multiple_of(i * sub, 16), sub)
                rows = pl.ds(pl.multiple_of(c * m + i * sub, 16), sub)
                up = e[rows, :].astype(F32)
                n2[rows, :] = (yacc[rows, :] + bd_ref[...]).astype(BF16)
                hat, rstd = norm_stats(slots[c % 4][here, :])
                d = dn[rows, :]
                gt = (up + norm_back(hat, rstd, gain_ref[...], d)).astype(BF16)
                e[rows, :] = gt
                return (
                    sums[0] + colsum(d * hat), sums[1] + colsum(d), sums[2] + colsum(up),
                    sums[3] + colsum(gt.astype(F32)),
                )

            got = lax.fori_loop(0, m // sub, close, got, unroll=13)
            for x in results[c] + again[c + 4 : c + 5]:
                x.start()
        small_ref[...] = jnp.zeros_like(small_ref)
        for i in range(4):
            small_ref[i : i + 1, :] = got[i]

    tick(7)

    @pl.when(f == parts - 1)
    def _():
        out = carry(sums, done, buf_ref, copy_sem, True)
        for x in out:
            x.start()
        for x in out + sum(results, []):
            x.wait()


def mlp_count(nx, ny, rows):
    count = 2 * MLP_PARTS
    while rows // count % (16 * nx * ny):
        count //= 2
    return count


def mlp_ready(i, count, head, part_us):
    unit = (i + 1) * (2 * MLP_PARTS // count) - 1
    return head + part_us * (unit // 2 + (0.9 if unit % 2 == 0 else 1.0))


def mlp_sums(mesh, z, buf, recv, full, sems):
    nx, ny = mesh.n["gx"], mesh.n["gy"]
    count = mlp_count(nx, ny, buf.shape[0])
    rows = buf.shape[0] // count
    sem0, out = 0, []
    for i in range(count):
        rounds = mlp_route(nx, ny, i, count)
        out.append(Sum(mesh, buf, i * rows, rows, rounds, recv, i * rows, sems, sem0, full))
        sem0 += 2 * sems_of(rounds)
    return out


def mlp_route(nx, ny, i, count):
    first, other = routes_of(nx, ny)
    if i == count - 1:
        return other
    return long_first(first) if i in (3, 6) else first


def long_first(rounds):
    return rounds[:1] + rounds[-1:] + rounds[1:-1]


def local_bwd_kernel(
    z, nx, ny, acts, before, done, gt_ref, xp_ref, r2_ref, o_ref, p_ref, qw_ref, code_ref, gain_ref, shift_ref, w_ref,
    wo_ref, part_ref, y_ref,
    pg_ref, dt0_ref, gwq_ref, gwo_ref, small_ref, buf_ref, yin_ref,
    ds_, dq_, dqkv, dtp, buf, recv, full, sems, ysems, copy_sem,
):
    step = pl.program_id(0)
    steps = pl.num_programs(0)
    mesh = Mesh2(nx, ny)
    sums = mlp_sums(mesh, z, buf, recv, full, sems)
    per = len(acts) // z.nb

    def tick(p):
        for i in range(z.nb):
            if acts[i * per + p]:

                @pl.when(step == i)
                def _():
                    act(sums, acts[i * per + p])

    units = z.early // 16

    def send(o, i):
        rows = pl.ds(units * i // z.nb * 16, (units * (i + 1) // z.nb - units * i // z.nb) * 16)
        return pltpu.make_async_remote_copy(
            src_ref=y_ref.at[o, rows], dst_ref=yin_ref.at[o, rows], send_sem=ysems.at[0, o * z.nb + i],
            recv_sem=ysems.at[1, o * z.nb + i], device_id=mesh.beside(nx - o),
            device_id_type=pl.DeviceIdType.MESH,
        )

    own_y = pltpu.make_async_copy(y_ref.at[0, : z.early], yin_ref.at[0], ysems.at[0, 0])

    @pl.when(step == 0)
    def _():
        gwq_ref[...] = jnp.zeros_like(gwq_ref)
        gwo_ref[...] = jnp.zeros_like(gwo_ref)
        small_ref[...] = jnp.zeros_like(small_ref)
        fetch = carry(sums, before, part_ref, copy_sem, False)
        for x in fetch:
            x.start()
        mesh.barrier(all_rounds(nx, ny), row=True)
        own_y.start()
        for x in fetch:
            x.wait()

    tick(0)
    for i in range(z.nb):

        @pl.when(step == i)
        def _(i=i):
            for o in range(1, nx):
                send(o, i).start()

    gt = gt_ref[0]
    dot = mm_nt(gt, wo_ref[...])
    for j in range(z.groups):
        ds_[j, : z.r, :] = dot[:, j * LANES : (j + 1) * LANES]
        if z.wide > z.r:
            ds_[j, z.r :, :] = jnp.zeros((z.wide - z.r, LANES), F32)
    gwo_ref[...] += mm_tn(o_ref[0], gt)
    masks = head_masks(SEG, z.hd)
    pad = jnp.zeros((SEG - 56, LANES), F32)
    scale = z.hd ** (-0.5)

    def windows(i, _):
        jobs = [(i * z.side + j, g) for j in range(z.side) for g in range(z.groups)]
        do = [
            jnp.concatenate([ds_[g, pl.ds(w, 56, stride=z.k), :], pad], axis=0).astype(BF16)
            for w, g in jobs
        ]
        dobd = [spread(x, masks) for x in do]
        dp = [mm_nt(qw_ref[w, 2 * z.groups + g], x) for (w, g), x in zip(jobs, dobd)]
        dv = [mm(p_ref[w, g], x) for (w, g), x in zip(jobs, dobd)]
        for (w, g), x in zip(jobs, dv):
            dq_[2 * z.groups + g, pl.ds(w, 56, stride=z.k), :] = x[:56]
        ds = []
        for (w, g), x in zip(jobs, dp):
            pf = p_ref[w, g].astype(F32)
            t = pf * x
            ds.append((t - pf * jnp.sum(t, axis=0, keepdims=True)).astype(BF16))
        dk = [mm(x, spread(qw_ref[w, g], masks)) for (w, g), x in zip(jobs, ds)]
        for (w, g), x in zip(jobs, dk):
            dq_[z.groups + g, pl.ds(w, 56, stride=z.k), :] = x[:56] * scale
        full = [mm_tn(x, qw_ref[w, z.groups + g]) for (w, g), x in zip(jobs, ds)]
        for (w, g), x in zip(jobs, full):
            dq_[g, pl.ds(w, 56, stride=z.k), :] = unspread(x, 56, SEG, masks) * scale
        return 0

    rounds = z.k // z.side
    for i in range(BWD_TICKS):
        lax.fori_loop(rounds * i // BWD_TICKS, rounds * (i + 1) // BWD_TICKS, windows, 0)
        tick(1 + i)
    for j in range(3 * z.groups):
        dqkv[:, j * LANES : (j + 1) * LANES] = dq_[j, : z.r, :].astype(BF16)
    dn = mm_nt(dqkv[...], w_ref[...])
    t = xp_ref[0].astype(F32)
    t = jnp.concatenate([r2_ref[0, : z.k, :], t[z.k :]], axis=0)
    hat, rstd = norm_stats(t)
    nt = (hat * gain_ref[...] + shift_ref[...]).astype(BF16)
    gwq_ref[...] += mm_tn(nt, dqkv[...])
    dt = gt.astype(F32) + norm_back(hat, rstd, gain_ref[...], dn)
    dt0_ref[0, : z.k, :] = dt[: z.k]
    dt0_ref[0, z.k :, :] = jnp.zeros((z.kp - z.k, z.d), F32)
    dtp[step] = dt.astype(BF16)
    small_ref[0:1, :] += colsum(dn * hat)
    small_ref[1:2, :] += colsum(dn)
    tick(1 + BWD_TICKS)

    @pl.when(step == steps - 1)
    def _():
        sel_t = one_hot_t(code_ref[...], z.gp * z.w)
        for g in range(z.ng):
            unpack_group(z, g, sel_t, dtp, pg_ref, None)

    tick(2 + BWD_TICKS)

    @pl.when(step == steps - 1)
    def _():
        out = carry(sums, done, buf_ref, copy_sem, True)
        for x in out:
            x.start()
        own_y.wait()
        for o in range(1, nx):
            for i in range(z.nb):
                send(o, i).wait()
        for x in out:
            x.wait()


def bit_list(count, axis):
    return [(axis, b) for b in range(count.bit_length() - 1)]


def n_bits(count):
    return count.bit_length() - 1


def stage_costs(nx, ny, rounds, size):
    xs = n_bits(ny) // 2
    costs, share = [], size
    for group in rounds:
        share /= 1 << len(group)
        wire = {}
        if group == (("gx", 0),):
            costs.append((2.5, wire))
            continue
        for axis, b in group:
            name, far = ("y", b > 1) if axis == "gx" else ("x", b > 0) if b < xs else ("z", b > xs)
            wire[name] = max(wire.get(name, 0.0), (8 if far else 4) * share / 85e3)
        costs.append((LATENCY_US, wire))
    return costs + costs[::-1]


class Mesh2:
    def __init__(self, nx, ny):
        self.n = {"gx": nx, "gy": ny}
        self.at = {"gx": lax.axis_index("gx"), "gy": lax.axis_index("gy")}

    def bit(self, which):
        axis, b = which
        return lax.rem(self.at[axis] // (1 << b), 2)

    def flips(self, group):
        return [
            [which for i, which in enumerate(group) if m >> (len(group) - 1 - i) & 1]
            for m in range(1, 1 << len(group))
        ]

    def partner(self, flipped):
        at = dict(self.at)
        for axis, b in flipped:
            at[axis] = at[axis] + (1 - 2 * self.bit((axis, b))) * (1 << b)
        return (at["gx"], at["gy"])

    def share(self, group, flipped=()):
        index = 0
        for which in group:
            bit = self.bit(which)
            index = 2 * index + (1 - bit if which in flipped else bit)
        return index

    def beside(self, o):
        return (lax.rem(self.at["gx"] + o, self.n["gx"]), self.at["gy"])

    def barrier(self, rounds, row=False):
        sem = pltpu.get_barrier_semaphore()
        sets = []
        for group in rounds:
            sets += [x for x in self.flips(group) if sorted(x) not in [sorted(y) for y in sets]]
        if row:
            sets = [x for x in sets if any(axis == "gy" for axis, _ in x)]
        others = [self.partner(x) for x in sets]
        if row:
            others += [self.beside(o) for o in range(1, self.n["gx"])]
        for other in others:
            pl.semaphore_signal(sem, inc=1, device_id=other, device_id_type=pl.DeviceIdType.MESH)
        pl.semaphore_wait(sem, len(others))


def routes_of(nx, ny):
    core, ys, g = [("gx", 0)], bit_list(nx, "gx")[1:], bit_list(ny, "gy")
    xs, zs = g[: len(g) // 2], g[len(g) // 2 :]
    if len(g) == 3:
        xs, zs = g[:1], g[1:]
    plane = [tuple(x) for x in zip(ys, xs)]
    line = [tuple(zs)]
    first = [tuple(core)] + plane + line
    other = [tuple(core)] + [tuple(x) for x in zip(xs, zs)]
    left = [x for x in ys + g if not any(x in group for group in other)]
    while left:
        other.append(tuple(left[:2]))
        left = left[2:]
    return first, other


def all_rounds(nx, ny):
    first, other = routes_of(nx, ny)
    return first + other


def place_of(order, nx, ny, dev):
    gx, gy = dev // ny, dev % ny
    p = 0
    for axis, b in order:
        p = 2 * p + (((gx if axis == "gx" else gy) >> b) & 1)
    return p


def flat(rounds):
    return [which for group in rounds for which in group]


def remote(mesh, src, dst, sems, i, flipped):
    return pltpu.make_async_remote_copy(
        src_ref=src, dst_ref=dst, send_sem=sems.at[0, i], recv_sem=sems.at[1, i],
        device_id=mesh.partner(flipped), device_id_type=pl.DeviceIdType.MESH,
    )


def sems_of(rounds):
    return sum((1 << len(group)) - 1 for group in rounds)


class Sum:
    def __init__(self, mesh, buf, start, rows, rounds, recv, recv_start, sems, sem0, full=None):
        self.mesh, self.buf, self.rounds, self.sems, self.sem0 = mesh, buf, rounds, sems, sem0
        self.recv, self.recv0, self.first, self.total = recv, recv_start, start, rows
        self.full = full
        self.n = len(rounds)
        self.stages = self.n * (2 if full is not None else 1)

    def held(self, s):
        off, rows = self.first, self.total
        for group in self.rounds[:s]:
            rows //= 1 << len(group)
            off = off + self.mesh.share(group) * rows
        return off, rows

    def recv_base(self, s):
        rows, base = self.total, self.recv0
        for group in self.rounds[:s]:
            part = rows >> len(group)
            base += rows - part
            rows = part
        return base

    def copies(self, s):
        back = s >= self.n
        r = 2 * self.n - 1 - s if back else s
        group = self.rounds[r]
        sem = self.sem0 + (sems_of(self.rounds) if back else 0) + sems_of(self.rounds[:r])
        off, rows = self.held(r)
        part = rows >> len(group)
        out = []
        for i, flipped in enumerate(self.mesh.flips(group)):
            if back:
                mine = pl.multiple_of(off + self.mesh.share(group) * part, 16)
                src = dst = self.full.at[pl.ds(mine, part)]
            else:
                theirs = pl.multiple_of(off + self.mesh.share(group, flipped) * part, 16)
                src = self.buf.at[pl.ds(theirs, part)]
                dst = self.recv.at[pl.ds(self.recv_base(r) + i * part, part)]
            out.append(remote(self.mesh, src, dst, self.sems, sem + i, flipped))
        return out

    def start(self, s):
        for x in self.copies(s):
            x.start()

    def finish(self, s):
        for x in self.copies(s):
            x.wait()
        if s < self.n:
            off, part = self.held(s + 1)
            base = self.recv_base(s)
            count = (1 << len(self.rounds[s])) - 1
            step = math.gcd(part, 64)
            into = self.full if s == self.n - 1 and self.full is not None else self.buf

            def add(i, _):
                mine = pl.ds(pl.multiple_of(off + i * step, 16), step)
                total = self.buf[mine, :].astype(F32)
                for j in range(count):
                    theirs = pl.ds(pl.multiple_of(base + j * part + i * step, 16), step)
                    total = total + self.recv[theirs, :].astype(F32)
                into[mine, :] = total.astype(BF16)
                return 0

            lax.fori_loop(0, part // step, add, 0)


def carry(sums, done, where, sem, out):
    copies = []
    for x, s in zip(sums, done):
        off, rows = x.held(min(s, 2 * x.n - s))
        rows = pl.ds(pl.multiple_of(off, 16), rows)
        mine = (x.buf if s < x.n else x.full).at[rows]
        src, dst = (mine, where.at[rows]) if out else (where.at[rows], mine)
        copies.append(pltpu.make_async_copy(src, dst, sem.at[len(copies)]))
    return copies


def plan(ready, done, stages, cost, slots, end, share=1.0):
    acts = [[] for _ in slots]
    done = list(done)
    running = [None] * len(done)
    free = {"x": 0.0, "y": 0.0, "z": 0.0}
    rate = {"x": 1.0, "y": share, "z": 1.0}
    for i, now in enumerate(slots):
        last = i == len(slots) - 1
        for j in range(len(done)):
            if ready[j] > now:
                continue
            stop = None
            if running[j] is not None:
                if now < running[j] and not last:
                    continue
                stop = done[j]
                done[j] += 1
                running[j] = None
            go = None
            if done[j] < stages and not last:
                latency, wire = cost[j][done[j]]
                over = max([now] + [max(free[c], now) + wire[c] / rate[c] for c in wire]) + latency
                if over <= end + SLACK_US:
                    go = done[j]
                    running[j] = over
                    for c in wire:
                        free[c] = max(free[c], now) + wire[c] / rate[c]
            if stop is not None or go is not None:
                acts[i].append((j, stop, go))
    return acts, done


def act(sums, acts):
    for j, stop, go in acts:
        if stop is not None:
            sums[j].finish(stop)
        if go is not None:
            sums[j].start(go)


class Gather:
    def __init__(self, mesh, buf, rows, rounds, sems, sem0):
        self.mesh, self.buf, self.rounds, self.sems, self.sem0 = mesh, buf, rounds, sems, sem0
        self.block = rows
        self.stages = len(rounds)

    def held(self, s):
        off, rows = 0, self.block << len(flat(self.rounds))
        for group in self.rounds[: self.stages - s]:
            rows >>= len(group)
            off = off + self.mesh.share(group) * rows
        return pl.multiple_of(off, 16), rows

    def copies(self, s):
        group = self.rounds[self.stages - 1 - s]
        here = self.buf.at[pl.ds(*self.held(s))]
        sem = self.sem0 + sems_of(self.rounds[: self.stages - 1 - s])
        return [
            remote(self.mesh, here, here, self.sems, sem + i, flipped)
            for i, flipped in enumerate(self.mesh.flips(group))
        ]

    def start(self, s):
        for x in self.copies(s):
            x.start()

    def finish(self, s):
        for x in self.copies(s):
            x.wait()


def region_bwd_kernel(
    z, nx, ny, done,
    dt0_ref, all_ref, o_ref, of_ref, p_ref, kv_ref, nr_ref, q_ref, nown_ref, own_ref, ord_ref, gain_ref,
    w_ref, wo_ref, gwq_ref, gwo_ref, smalla_ref, smallm_ref, gbu_ref, part_ref, y_ref,
    mlp_ref, att_ref, vec_ref, dnr_ref, dt0a_ref, dnown_ref, yin_ref,
    dobd, qbd, delta, acc, gacc, small, buf, recv, full, abuf, arecv, afull, vbuf, dbuf, drecv,
    sems, asems, ysems, copy_sem,
):
    step = pl.program_id(0)
    steps = pl.num_programs(0)
    mesh = Mesh2(nx, ny)
    d = z.d
    kc = all_ref.shape[0]
    nq = HEADS * z.w
    n = nx * ny
    scale = z.hd ** (-0.5)
    rest = mlp_sums(mesh, z, buf, recv, full, sems)
    first, other = routes_of(nx, ny)
    last = long_first(first)
    order_d = flat(first)
    bits = len(order_d)
    lane = lax.broadcasted_iota(jnp.int32, (z.w, d), 1) // z.hd

    late = pl.ds(z.early, z.r - z.early)

    def send(o):
        return pltpu.make_async_remote_copy(
            src_ref=y_ref.at[o, late], dst_ref=yin_ref.at[o], send_sem=ysems.at[0, o],
            recv_sem=ysems.at[1, o], device_id=mesh.beside(nx - o),
            device_id_type=pl.DeviceIdType.MESH,
        )

    own_y = pltpu.make_async_copy(y_ref.at[0, late], yin_ref.at[0], ysems.at[0, 0])

    sums, sem0 = [], bits
    split = max(x for x in (1, 2, 4) if (4 * d // x) % (16 * n) == 0 or x == 1)
    for i in range(split):
        rows = 4 * d // split
        rounds = first if i < 3 else last
        sums.append(Sum(mesh, abuf, i * rows, rows, rounds, arecv, i * rows, asems, sem0, afull))
        sem0 += 2 * sems_of(rounds)
    sums.append(Sum(mesh, dbuf, 0, n * z.w, first, drecv, 0, asems, sem0))

    @pl.when(step == 0)
    def _():
        fetch = carry(rest, done, part_ref, copy_sem, False)
        for x in fetch:
            x.start()
        mesh.barrier(all_rounds(nx, ny), row=True)
        for x in fetch:
            x.wait()
        for x, s in zip(rest, done):
            if s < x.stages:
                x.start(s)
        for o in range(1, nx):
            send(o).start()
        own_y.start()
        dt0 = jnp.concatenate([dt0_ref[c, : z.k, :] for c in range(z.nb)], axis=0)
        sel_t = one_hot_t(ord_ref[...], z.w).astype(F32)
        dt0 = jnp.dot(sel_t, dt0, precision=HIGH, preferred_element_type=F32)
        dt0a_ref[...] = dt0
        gr = dt0.astype(BF16)
        abuf[3 * d :, :] = (gwo_ref[...] + mm_tn(o_ref[...], gr)).astype(BF16)
        do = mm_nt(gr, wo_ref[...]).astype(BF16)
        zero = jnp.zeros_like(do)
        q = q_ref[...]
        for h in range(HEADS):
            dobd[h * z.w : (h + 1) * z.w, :] = jnp.where(lane == h, do, zero)
            qbd[h * z.w : (h + 1) * z.w, :] = jnp.where(lane == h, q, zero)
        prod = do.astype(F32) * of_ref[...]
        spread_prod = jnp.concatenate([jnp.where(lane == h, prod, 0.0) for h in range(HEADS)], axis=0)
        delta[...] = lax.dot_general(
            jnp.ones((8, d), F32), spread_prod, (((1,), (1,)), ((), ())), precision=HIGH,
            preferred_element_type=F32,
        )
        small[...] = jnp.zeros_like(small)
        small[2:3, :] = colsum(gr.astype(F32))
        acc[...] = jnp.zeros_like(acc)
        gacc[...] = gwq_ref[...]

    p = p_ref[...]
    ds = (p.astype(F32) * (mm_nt(kv_ref[:, d:], dobd[...]) - delta[0:1, :])).astype(BF16)
    dv = mm(p, dobd[...]).astype(BF16)
    dk = (mm(ds, qbd[...]) * scale).astype(BF16)
    dkv = jnp.concatenate([dk, dv], axis=1)
    gacc[:, d:] += mm_tn(nr_ref[...], dkv)
    dn = mm_nt(dkv, w_ref[:, d:])
    acc[...] += mm_tn(ds, kv_ref[:, :d])
    hat, _ = norm_stats(all_ref[...].astype(F32))
    small[0:1, :] += colsum(dn * hat)
    small[1:2, :] += colsum(dn)
    per = kc // z.w
    for j in range(per):
        dev = step * per + j
        at = {"gx": dev // ny, "gy": lax.rem(dev, ny)}
        place = 0
        for axis, b in order_d:
            place = 2 * place + lax.rem(at[axis] // (1 << b), 2)
        dbuf[pl.ds(pl.multiple_of(place * z.w, 16), z.w), :] = dn[j * z.w : (j + 1) * z.w].astype(BF16)

    @pl.when(step == steps - 1)
    def _():
        sums[split].start(0)
        dq = acc[(HEADS - 1) * z.w :, :]
        for h in range(HEADS - 2, -1, -1):
            dq = jnp.where(lane == h, acc[h * z.w : (h + 1) * z.w, :], dq)
        dq = (dq * scale).astype(BF16)
        abuf[:d, :] = (gacc[:, :d] + mm_tn(nown_ref[...], dq)).astype(BF16)
        for f in range(1, 3):
            abuf[f * d : (f + 1) * d, :] = gacc[:, f * d : (f + 1) * d].astype(BF16)
        for x in sums[:split]:
            x.start(0)
        dnown = mm_nt(dq, w_ref[:, :d])
        dnown_ref[...] = dnown
        hat, _ = norm_stats(own_ref[...].astype(F32))
        vbuf[0] = jnp.zeros_like(vbuf[0])
        vbuf[0, 0:1, :] = smalla_ref[0:1, :] + small[0:1, :] + colsum(dnown * hat)
        vbuf[0, 1:2, :] = smalla_ref[1:2, :] + small[1:2, :] + colsum(dnown)
        vbuf[0, 2:3, :] = smallm_ref[3:4, :] + small[2:3, :]
        vbuf[0, 3:6, :] = smallm_ref[0:3, :]
        row = 6
        for f in range(MLP_PARTS):
            for i in range(gbu_ref.shape[2] // d):
                vbuf[0, row : row + 1, :] = gbu_ref[f, :, i * d : (i + 1) * d]
                row += 1
        queue = [(x, 0) for x in sums[split:] + sums[:split]]
        queue += [(x, s) for x, s in zip(rest, done) if s < x.stages]
        vec = None
        for s in range(max(bits, 2 * len(first)) + 1):
            for x, s0 in queue:
                if s and s0 + s - 1 < x.stages:
                    x.finish(s0 + s - 1)
                if s and s0 + s < x.stages:
                    x.start(s0 + s)
            if s <= bits:
                if s:
                    vec.wait()
                    vbuf[2 * s] = vbuf[2 * s - 2] + vbuf[2 * s - 1]
                if s < bits:
                    vec = remote(mesh, vbuf.at[2 * s], vbuf.at[2 * s + 1], asems, s, [order_d[s]])
                    vec.start()
        vec_ref[...] = vbuf[2 * bits]
        dnr_ref[...] = dbuf[pl.ds(pl.multiple_of(sums[split].held(len(first))[0], 16), z.w), :]
        outs = [
            pltpu.make_async_copy(full, mlp_ref, copy_sem.at[0]),
            pltpu.make_async_copy(afull, att_ref, copy_sem.at[1]),
        ]
        for x in outs:
            x.start()
        own_y.wait()
        for o in range(1, nx):
            send(o).wait()
        for x in outs:
            x.wait()


def finish_kernel(
    z, mlp_ref, att_ref, vec_ref, early_ref, late_ref, code_ref, own_ref, dnr_ref, dnown_ref, dt0a_ref, gain_ref,
    out_ref, first_ref, rg_ref, gwu_ref, gwd_ref, gwq_ref, gwo_ref, gbu_ref, *rows,
):
    f = pl.program_id(0)
    fc = gwd_ref.shape[0]
    d = z.d
    gwd_ref[...] = mlp_ref[:fc, :].astype(F32)
    for i in range(fc // d):
        gwu_ref[:, i * d : (i + 1) * d] = mlp_ref[fc + i * d : fc + (i + 1) * d, :].astype(F32)

    @pl.when(f < 3)
    def _():
        gwq_ref[...] = att_ref[...].astype(F32)

    @pl.when(f == 3)
    def _():
        gwo_ref[...] = att_ref[...].astype(F32)

    @pl.when(f == 0)
    def _():
        for i, row in enumerate(rows):
            row[...] = vec_ref[i : i + 1, :]
        gbu_ref[...] = vec_ref[6 : 6 + gbu_ref.shape[0], :]
        hat, rstd = norm_stats(own_ref[...].astype(F32))
        dn = dnr_ref[...].astype(F32) + dnown_ref[...]
        rg_ref[...] = (dt0a_ref[...] + norm_back(hat, rstd, gain_ref[...], dn)).astype(BF16)

    for step in range(MLP_PARTS):

        @pl.when(f == step)
        def _():
            sel_t = one_hot_t(code_ref[...], z.gp * z.w)
            for g in range(z.ng * step // MLP_PARTS, z.ng * (step + 1) // MLP_PARTS):
                rows = z.gp * z.k
                at = z.early // rows
                src, i = (early_ref, g) if g < at else (late_ref, g - at)
                unpack_group(z, g, sel_t, src, out_ref, first_ref, i)


def local(
    patches, regions, send_order, image_windows, attn_gain, attn_shift, w_qkv, w_out, b_out,
    mlp_gain, mlp_shift, w_up, b_up, w_down, b_down, upstream_patches, upstream_regions,
):
    nx, ny = lax.axis_size("gx"), lax.axis_size("gy")
    z = Sizes(patches.shape[0], patches.shape[1], patches.shape[2], nx)
    ff = w_up.shape[1]
    n = z.w * nx * ny
    gx = lax.axis_index("gx")
    dev = gx * ny + lax.axis_index("gy")
    sds = jax.ShapeDtypeStruct

    order = lax.dynamic_slice_in_dim(send_order, dev, 1, 0)[0].reshape(nx, z.k)
    tile = jnp.arange(nx, dtype=jnp.int32)
    order_t = jnp.take(order, (gx - tile) % nx, axis=0)
    place = jnp.arange(z.gp, dtype=jnp.int32) * z.w
    code_x = (order_t[:, None, :] + place[None, :, None]).reshape(-1)
    block = ((gx + tile) % nx)[:, None] * z.k + jnp.arange(z.k, dtype=jnp.int32)[None, :]
    code_e = (block[:, None, :] + place[None, :, None]).reshape(-1)
    order_t = order_t.reshape(-1)
    bounds = jnp.cumsum(image_windows)
    gain, shift = attn_gain[None], attn_shift[None]

    x_t = jnp.transpose(patches, (1, 0, 2))
    e_t = jnp.transpose(upstream_patches, (1, 0, 2))

    bits = n_bits(nx * ny)
    anywhere = pl.BlockSpec(memory_space=pl.ANY)
    vmem = pl.BlockSpec(memory_space=pltpu.VMEM)
    *packed, xp, qkv, regions_all = pl.pallas_call(
        functools.partial(start_kernel, z, nx, ny),
        in_specs=[anywhere, anywhere] + [vmem] * 7,
        out_specs=[vmem] * (z.nb + 1) + [anywhere, vmem],
        out_shape=[sds((z.r, z.d), BF16)] * z.nb + [
            sds((z.nb, z.r, z.d), BF16),
            sds((z.nb, z.r, 3 * z.d), BF16),
            sds((n, z.d), BF16),
        ],
        scratch_shapes=[
            pltpu.VMEM((z.tok, z.w, z.d), BF16),
            pltpu.VMEM((z.tok, z.w, z.d), BF16),
            pltpu.VMEM((z.nb, z.r, 3 * z.d), BF16),
            pltpu.VMEM((z.r, z.d), BF16),
            pltpu.VMEM((n, z.d), BF16),
            pltpu.SemaphoreType.DMA((2, sems_of(routes_of(nx, ny)[0]))),
            pltpu.SemaphoreType.DMA((2,)),
            pltpu.SemaphoreType.DMA((z.nb,)),
        ],
        compiler_params=params(collective_id=0, has_side_effects=True),
        name="start",
    )(x_t, e_t, upstream_regions, code_x[None], code_e[None], gain, shift, w_qkv, regions)

    e_in = [packed[0]]
    for o in range(1, nx):
        e_in.append(lax.ppermute(packed[o], "gx", [(i, (i + o) % nx) for i in range(nx)]))

    kc = 8 * z.w
    nq = HEADS * z.w
    r2, p_r, kv_all, nr_all, q_r, o_r, o_f, n_own = pl.pallas_call(
        functools.partial(region_fwd_kernel, z, kc, ny),
        in_specs=[vmem, vmem, pl.BlockSpec(memory_space=pltpu.SMEM)] + [vmem] * 6,
        out_shape=(
            sds((z.nb, z.kp, z.d), F32),
            sds((n, nq), BF16),
            sds((n, 2 * z.d), BF16),
            sds((n, z.d), BF16),
            sds((z.w, z.d), BF16),
            sds((z.w, z.d), BF16),
            sds((z.w, z.d), F32),
            sds((z.w, z.d), BF16),
        ),
        scratch_shapes=[pltpu.VMEM((n, nq), F32)],
        compiler_params=params(),
        name="region_fwd",
    )(
        regions_all, regions, bounds, order_t[None], gain, shift, w_qkv, w_out, b_out[None],
    )

    def tiled(*shape):
        return pl.BlockSpec((1,) + shape, lambda i: (i,) + (0,) * len(shape))

    def grouped(*shape):
        return pl.BlockSpec((z.k,) + shape, lambda i: (i,) + (0,) * len(shape))

    cols = z.per_group * SEG
    t2, p_w, qw, o_w = pl.pallas_call(
        functools.partial(local_fwd_kernel, z),
        grid=(z.nb,),
        in_specs=[
            tiled(z.r, 3 * z.d), tiled(z.r, z.d), tiled(z.kp, z.d), whole(1, z.d), whole(1, z.d),
            whole(z.d, 3 * z.d), whole(z.d, z.d), whole(1, z.d),
        ],
        out_specs=[
            tiled(z.r, z.d), grouped(z.groups, SEG, cols), grouped(3 * z.groups, SEG, LANES),
            tiled(z.r, z.d),
        ],
        out_shape=(
            sds((z.nb, z.r, z.d), F32),
            sds((z.w, z.groups, SEG, cols), BF16),
            sds((z.w, 3 * z.groups, SEG, LANES), BF16),
            sds((z.nb, z.r, z.d), BF16),
        ),
        scratch_shapes=[
            pltpu.VMEM((3 * z.groups, z.wide, LANES), F32),
            pltpu.VMEM((z.groups, z.wide, LANES), F32),
        ],
        compiler_params=params(),
        name="local_fwd",
    )(qkv, xp, r2, gain, shift, w_qkv, w_out, b_out[None])

    parts = MLP_PARTS
    fc = ff // parts
    total = 2 * ff
    first, other = routes_of(nx, ny)
    stages = 2 * len(first)
    n_sums = mlp_count(nx, ny, total)
    cost = [stage_costs(nx, ny, mlp_route(nx, ny, i, n_sums), total // n_sums * z.d * 2) for i in range(n_sums)]
    n_sems = sum(2 * sems_of(mlp_route(nx, ny, i, n_sums)) for i in range(n_sums))
    head, part_us, tail_us = 11.0, MLP_US / parts, 7.0
    slots = []
    for i in range(parts):
        base = head + part_us * i
        slots += [base + part_us * x for x in (0.0, 0.3, 0.55, 0.8, 0.8, 0.9, 1.0)]
        slots.append(base + part_us + (tail_us if i == parts - 1 else 0.0))
    acts_m, done_m = plan(
        [mlp_ready(i, n_sums, head, part_us) - 0.05 for i in range(n_sums)], [0] * n_sums, stages, cost,
        slots, slots[-1],
    )
    keep = dict(pipeline_mode=pl.Buffered(1))

    def once(*shape):
        return pl.BlockSpec(shape, lambda *_: (0,) * len(shape), **keep)

    y, gt, part_sums, small_m, gbu = pl.pallas_call(
        functools.partial(mlp_kernel, z, nx, ny, acts_m, tuple(done_m)),
        grid=(parts,),
        in_specs=[pl.BlockSpec(memory_space=pl.ANY)] * (1 + z.nb) + [
            once(1, z.d), once(1, z.d), pl.BlockSpec((z.d, fc), lambda f: (0, f)),
            pl.BlockSpec((1, fc), lambda f: (0, f)), pl.BlockSpec((fc, z.d), lambda f: (f, 0)),
            once(1, z.d),
        ],
        out_specs=[
            anywhere, anywhere, anywhere, once(8, z.d),
            pl.BlockSpec((1, 1, fc), lambda f: (f, 0, 0)),
        ],
        out_shape=(
            sds((z.t, z.d), BF16),
            sds((z.t, z.d), BF16),
            sds((total, z.d), BF16),
            sds((8, z.d), F32),
            sds((parts, 1, fc), F32),
        ),
        scratch_shapes=[
            pltpu.VMEM((z.tp, z.d), BF16),
            pltpu.VMEM((z.tp, z.d), BF16),
            pltpu.VMEM((z.d + 16, z.tp), BF16),
            pltpu.VMEM((z.d + 16, z.tp), BF16),
            pltpu.VMEM((z.m, fc), F32),
            pltpu.VMEM((z.m, fc), F32),
            pltpu.VMEM((z.m, fc), F32),
            pltpu.VMEM((z.m, fc), F32),
            pltpu.VMEM((z.tp, fc), BF16),
            pltpu.VMEM((z.tp, fc), BF16),
            pltpu.VMEM((z.t, z.d), F32),
            pltpu.VMEM((z.t, z.d), F32),
            pltpu.VMEM((total, z.d), BF16),
            pltpu.VMEM((total, z.d), BF16),
            pltpu.VMEM((total, z.d), BF16),
            pltpu.SemaphoreType.DMA((2, n_sems)),
            pltpu.SemaphoreType.DMA((24,)),
        ],
        compiler_params=params(collective_id=1, has_side_effects=True),
        name="mlp",
    )(
        t2.reshape(z.t, z.d), *e_in, mlp_gain[None], mlp_shift[None], w_up, b_up[None], w_down,
        b_down[None],
    )
    y, gt = y.reshape(z.nb, z.r, z.d), gt.reshape(z.nb, z.r, z.d)

    head, part_us, tail_us = 2.0, BWD_US / z.nb, 2.0
    slots = []
    for i in range(z.nb):
        base = head + part_us * i
        slots += [base + part_us * x for x in (0.0, 0.3, 0.5, 0.7, 1.0)]
        slots.append(base + part_us + (tail_us if i == z.nb - 1 else 0.0))
    acts_b, done = plan([0.0] * n_sums, done_m, stages, cost, slots, slots[-1], 0.6)
    patch_grad, dt0, gwq, gwo, small_a, part_sums, y_early = pl.pallas_call(
        functools.partial(local_bwd_kernel, z, nx, ny, acts_b, tuple(done_m), tuple(done)),
        grid=(z.nb,),
        in_specs=[
            tiled(z.r, z.d), tiled(z.r, z.d), tiled(z.kp, z.d), tiled(z.r, z.d),
            grouped(z.groups, SEG, cols), grouped(3 * z.groups, SEG, LANES),
            whole(1, z.nb * z.gp * z.k), whole(1, z.d), whole(1, z.d), whole(z.d, 3 * z.d),
            whole(z.d, z.d), anywhere, anywhere,
        ],
        out_specs=[
            once(z.tok, z.w, z.d), tiled(z.kp, z.d), once(z.d, 3 * z.d), once(z.d, z.d),
            once(8, z.d), anywhere, anywhere,
        ],
        out_shape=(
            sds((z.tok, z.w, z.d), BF16),
            sds((z.nb, z.kp, z.d), F32),
            sds((z.d, 3 * z.d), F32),
            sds((z.d, z.d), F32),
            sds((8, z.d), F32),
            sds((total, z.d), BF16),
            sds((z.nb, z.early, z.d), BF16),
        ),
        scratch_shapes=[
            pltpu.VMEM((z.groups, z.wide, LANES), F32),
            pltpu.VMEM((3 * z.groups, z.wide, LANES), F32),
            pltpu.VMEM((z.r, 3 * z.d), BF16),
            pltpu.VMEM((z.nb, z.r, z.d), BF16),
            pltpu.VMEM((total, z.d), BF16),
            pltpu.VMEM((total, z.d), BF16),
            pltpu.VMEM((total, z.d), BF16),
            pltpu.SemaphoreType.DMA((2, n_sems)),
            pltpu.SemaphoreType.DMA((2, nx * z.nb)),
            pltpu.SemaphoreType.DMA((n_sums,)),
        ],
        compiler_params=params(collective_id=2, has_side_effects=True),
        name="local_bwd",
    )(gt, xp, r2, o_w, p_w, qw, code_x[None], gain, shift, w_qkv, w_out, part_sums, y)

    def keys(*shape):
        return pl.BlockSpec((kc,) + shape, lambda i: (i,) + (0,) * len(shape))

    mlp_total, att_total, vec, dnr, dt0a, dn_own, y_late = pl.pallas_call(
        functools.partial(region_bwd_kernel, z, nx, ny, tuple(done)),
        grid=(n // kc,),
        in_specs=[
            once(z.nb, z.kp, z.d), keys(z.d), once(z.w, z.d), once(z.w, z.d), keys(nq), keys(2 * z.d),
            keys(z.d), once(z.w, z.d), once(z.w, z.d), once(z.w, z.d), once(1, z.w), once(1, z.d),
            once(z.d, 3 * z.d), once(z.d, z.d), once(z.d, 3 * z.d), once(z.d, z.d), once(8, z.d),
            once(8, z.d), once(parts, 1, fc), anywhere, anywhere,
        ],
        out_specs=[
            anywhere, anywhere, once(16, z.d), once(z.w, z.d), once(z.w, z.d), once(z.w, z.d), anywhere,
        ],
        out_shape=(
            sds((total, z.d), BF16),
            sds((4 * z.d, z.d), BF16),
            sds((16, z.d), F32),
            sds((z.w, z.d), BF16),
            sds((z.w, z.d), F32),
            sds((z.w, z.d), F32),
            sds((z.nb, z.r - z.early, z.d), BF16),
        ),
        scratch_shapes=[
            pltpu.VMEM((nq, z.d), BF16),
            pltpu.VMEM((nq, z.d), BF16),
            pltpu.VMEM((8, nq), F32),
            pltpu.VMEM((nq, z.d), F32),
            pltpu.VMEM((z.d, 3 * z.d), F32),
            pltpu.VMEM((8, z.d), F32),
            pltpu.VMEM((total, z.d), BF16),
            pltpu.VMEM((total, z.d), BF16),
            pltpu.VMEM((total, z.d), BF16),
            pltpu.VMEM((4 * z.d, z.d), BF16),
            pltpu.VMEM((4 * z.d, z.d), BF16),
            pltpu.VMEM((4 * z.d, z.d), BF16),
            pltpu.VMEM((2 * bits + 1, 16, z.d), F32),
            pltpu.VMEM((n, z.d), BF16),
            pltpu.VMEM((n, z.d), BF16),
            pltpu.SemaphoreType.DMA((2, n_sems)),
            pltpu.SemaphoreType.DMA((2, bits + 9 * sems_of(first))),
            pltpu.SemaphoreType.DMA((2, nx)),
            pltpu.SemaphoreType.DMA((max(n_sums, 2),)),
        ],
        compiler_params=params(collective_id=3, has_side_effects=True),
        name="region_bwd",
    )(
        dt0, regions_all, o_r, o_f, p_r, kv_all, nr_all, q_r, n_own, regions, order_t[None], gain, w_qkv,
        w_out, gwq, gwo, small_a, small_m, gbu, part_sums, y,
    )

    out_p, out_r, region_grad, gwu, gwd, gwq, gwo, gbu, *rows = pl.pallas_call(
        functools.partial(finish_kernel, z),
        grid=(parts,),
        in_specs=[
            pl.BlockSpec((2 * fc, z.d), lambda f: (f, 0)), pl.BlockSpec((z.d, z.d), lambda f: (f, 0)),
            once(16, z.d), once(z.nb, z.early, z.d), once(z.nb, z.r - z.early, z.d), once(1, z.nb * z.gp * z.k), once(z.w, z.d),
            once(z.w, z.d), once(z.w, z.d), once(z.w, z.d), once(1, z.d),
        ],
        out_specs=[
            once(z.tok, z.w, z.d), once(z.w, z.d), once(z.w, z.d),
            pl.BlockSpec((z.d, fc), lambda f: (0, f)), pl.BlockSpec((fc, z.d), lambda f: (f, 0)),
            pl.BlockSpec((z.d, z.d), lambda f: (0, jnp.minimum(f, 2))), once(z.d, z.d),
            once(ff // z.d, z.d),
        ] + [once(1, z.d)] * 6,
        out_shape=[
            sds((z.tok, z.w, z.d), BF16), sds((z.w, z.d), BF16), sds((z.w, z.d), BF16),
            sds((z.d, ff), F32), sds((ff, z.d), F32), sds((z.d, 3 * z.d), F32), sds((z.d, z.d), F32),
            sds((ff // z.d, z.d), F32),
        ] + [sds((1, z.d), F32)] * 6,
        compiler_params=params(),
        name="finish",
    )(mlp_total, att_total, vec, y_early, y_late, code_e[None], regions, dnr, dn_own, dt0a, gain)
    rows = [x[0] for x in rows]
    return (
        jnp.transpose(out_p, (1, 0, 2)),
        out_r,
        jnp.transpose(patch_grad, (1, 0, 2)),
        region_grad,
        rows[0],
        rows[1],
        gwq,
        gwo,
        rows[2],
        rows[3],
        rows[4],
        gwu,
        gbu.reshape(ff),
        gwd,
        rows[5],
    )


def solution(mesh):
    split = ("gx", "gy")
    rows3, rows2, full = P(split, None, None), P(split, None), P()
    in_specs = (rows3, rows2) + (full,) * 13 + (rows3, rows2)
    out_specs = (rows3, rows2, rows3, rows2) + (full,) * 11
    return jax.shard_map(local, mesh=mesh, in_specs=in_specs, out_specs=out_specs, check_vma=False)
```

```python
import functools
import math

import jax
import jax.numpy as jnp
from jax import lax
from jax.experimental import pallas as pl
from jax.experimental.pallas import tpu as pltpu
from jax.sharding import PartitionSpec as P

HEADS = 16
EPS = 1e-05
F32 = jnp.float32
BF16 = jnp.bfloat16
LOG2E = 1.4426950408889634
VMEM_LIMIT = 60 * 1024 * 1024
HIGH = lax.Precision.HIGHEST
LANES = 128
MLP_PARTS = 4
BWD_TICKS = 3
MLP_US = 60.0
BWD_US = 36.0
LATENCY_US = 3.0
SLACK_US = 2.5
SEG = 64


def mm(a, b):
    return lax.dot_general(a, b, (((1,), (0,)), ((), ())), preferred_element_type=F32)


def mm_nt(a, b):
    return lax.dot_general(a, b, (((1,), (1,)), ((), ())), preferred_element_type=F32)


def mm_tn(a, b):
    return lax.dot_general(a, b, (((0,), (0,)), ((), ())), preferred_element_type=F32)


def norm_stats(v):
    average = jnp.mean(v, axis=-1, keepdims=True)
    centered = v - average
    variance = jnp.mean(centered * centered, axis=-1, keepdims=True)
    rstd = lax.rsqrt(variance + EPS)
    return centered * rstd, rstd


def norm_back(hat, rstd, gain, dn):
    dhat = dn * gain
    m1 = jnp.mean(dhat, axis=-1, keepdims=True)
    m2 = jnp.mean(dhat * hat, axis=-1, keepdims=True)
    return rstd * (dhat - m1 - hat * m2)


def colsum(v):
    return jnp.sum(v, axis=0, keepdims=True)


def gelu_both(u):
    a = jnp.abs(u)
    d = 1.0 + (0.3275911 * 0.7071067811865476) * a
    r = pl.reciprocal(d, approx=True)
    t = r * (2.0 - d * r)
    e = jnp.exp2((u * u) * (-0.5 * LOG2E))
    poly = t * (
        0.127414796
        + t * (-0.142248368 + t * (0.7107068705 + t * (-0.7265760135 + t * 0.5307027145)))
    )
    tail = poly * e
    cdf = jnp.where(u >= 0.0, 1.0 - tail, tail)
    return u * cdf, cdf + u * (e * 0.3989422804014327)


def head_masks(rows, head_dim):
    lane = lax.broadcasted_iota(jnp.int32, (rows, LANES), 1)
    return [(lane // head_dim) == h for h in range(LANES // head_dim)]


def spread(v, masks):
    zero = jnp.zeros_like(v)
    return jnp.concatenate([jnp.where(m, v, zero) for m in masks], axis=0)


def unspread(full, rows, stride, masks):
    out = full[(len(masks) - 1) * stride : (len(masks) - 1) * stride + rows]
    for h in range(len(masks) - 2, -1, -1):
        out = jnp.where(masks[h][:rows], full[h * stride : h * stride + rows], out)
    return out


def one_hot(code_col, count):
    rows = code_col.shape[0]
    return (lax.broadcasted_iota(jnp.int32, (rows, count), 1) == code_col).astype(F32).astype(BF16)


def one_hot_t(code_row, count):
    rows = code_row.shape[1]
    return (lax.broadcasted_iota(jnp.int32, (count, rows), 0) == code_row).astype(F32).astype(BF16)


def whole(*shape):
    return pl.BlockSpec(shape, lambda *_: (0,) * len(shape))


class Sizes:
    def __init__(self, per_dev, patch_tokens, width, count_gx):
        self.w = per_dev
        self.tok = patch_tokens
        self.d = width
        self.nb = count_gx
        self.k = per_dev // count_gx
        step = 16 // math.gcd(16, self.k)
        self.pos = -(-(patch_tokens + 1) // step) * step
        self.gp = step
        while (self.gp * self.k) % 16:
            self.gp *= 2
        self.ng = self.pos // self.gp
        self.early = self.ng // 2 * self.gp * self.k
        self.r = self.pos * self.k
        self.wide = 56 * self.k
        self.hd = width // HEADS
        self.groups = width // LANES
        self.per_group = LANES // self.hd
        self.chunk = self.r // 3 if self.r % 48 == 0 else self.r
        self.kp = -(-self.k // 16) * 16
        self.side = max(j for j in range(1, 5) if self.k % j == 0)
        self.t = self.nb * self.r
        self.tp = -(-self.t // 512) * 512
        self.m = max(m for m in range(16, 449, 16) if self.t % (2 * m) == 0)


def params(**kw):
    return pltpu.CompilerParams(vmem_limit_bytes=VMEM_LIMIT, **kw)


def pack_group(z, g, sel_t, x_ref, first_ref, outs):
    pieces = []
    for p in range(g * z.gp, (g + 1) * z.gp):
        if p == 0:
            pieces.append(jnp.zeros((z.w, z.d), BF16) if first_ref is None else first_ref[...])
        elif p <= z.tok:
            pieces.append(x_ref[p - 1])
        else:
            pieces.append(jnp.zeros((z.w, z.d), BF16))
    got = mm_tn(sel_t, jnp.concatenate(pieces, axis=0)).astype(BF16)
    rows = z.gp * z.k
    for c in range(z.nb):
        outs[c][g * rows : (g + 1) * rows, :] = got[c * rows : (c + 1) * rows]


def unpack_group(z, g, sel_t, packed_ref, out_ref, first_ref, at=None):
    rows = z.gp * z.k
    here = slice((g if at is None else at) * rows, ((g if at is None else at) + 1) * rows)
    src = jnp.concatenate([packed_ref[c, here, :] for c in range(z.nb)], axis=0)
    got = mm(sel_t, src).astype(BF16)
    for i in range(z.gp):
        p = g * z.gp + i
        piece = got[i * z.w : (i + 1) * z.w]
        if p == 0:
            if first_ref is not None:
                first_ref[...] = piece
        elif p <= z.tok:
            out_ref[p - 1] = piece


def start_kernel(
    z, nx, ny, x_ref, e_ref, first_ref, codex_ref, codee_ref, gain_ref, shift_ref, w_ref, own_ref, *refs
):
    packed, refs = refs[: z.nb], refs[z.nb :]
    xp_ref, qkv_ref, all_ref, xs, es, qs, nt, buf, sems, load_sems, out_sems = refs
    loads = [
        pltpu.make_async_copy(src, dst, load_sems.at[i])
        for i, (src, dst) in enumerate(((e_ref, es), (x_ref, xs)))
    ]
    for x in loads:
        x.start()
    mesh = Mesh2(nx, ny)
    rounds = routes_of(nx, ny)[0]
    gather = Gather(mesh, buf, z.w, rounds, sems, 0)
    mesh.barrier(rounds)
    buf[pl.ds(*gather.held(0)), :] = own_ref[...]
    gather.start(0)

    def pack(src, code_ref, first, outs):
        sel_t = one_hot_t(code_ref[...], z.gp * z.w)
        for g in range(z.ng):
            pack_group(z, g, sel_t, src, first, outs)

    def out(c):
        return pltpu.make_async_copy(qs.at[c], qkv_ref.at[c], out_sems.at[c])

    def project(c, _):
        hat, _ = norm_stats(xp_ref[c].astype(F32))
        nt[...] = (hat * gain_ref[...] + shift_ref[...]).astype(BF16)
        qs[c] = mm(nt[...], w_ref[...]).astype(BF16)
        out(c).start()
        return 0

    stages = gather.stages
    loads[0].wait()
    pack(es, codee_ref, first_ref, packed)
    loads[1].wait()
    pack(xs, codex_ref, None, [xp_ref.at[c] for c in range(z.nb)])
    for s in range(1, stages + 1):
        gather.finish(s - 1)
        if s < stages:
            gather.start(s)
            lax.fori_loop(z.nb * (s - 1) // (stages - 1), z.nb * s // (stages - 1), project, 0)
    n = nx * ny
    order = flat(rounds)
    for dev in range(n):
        p = place_of(order, nx, ny, dev)
        all_ref[dev * z.w : (dev + 1) * z.w, :] = buf[p * z.w : (p + 1) * z.w, :]
    for c in range(z.nb):
        out(c).wait()


def region_fwd_kernel(
    z, kc, ny, all_ref, own_ref, bounds_ref, ord_ref, gain_ref, shift_ref, w_ref, wo_ref, bo_ref,
    r2_ref, p_ref, kv_ref, nr_ref, q_ref, o_ref, of_ref, nown_ref, s_ref,
):
    n = all_ref.shape[0]
    nq = HEADS * z.w
    hat, _ = norm_stats(own_ref[...].astype(F32))
    nown = (hat * gain_ref[...] + shift_ref[...]).astype(BF16)
    nown_ref[...] = nown
    q = mm(nown, w_ref[:, : z.d]).astype(BF16)
    q_ref[...] = q
    lane = lax.broadcasted_iota(jnp.int32, (z.w, z.d), 1) // z.hd
    zero = jnp.zeros_like(q)
    qbd = jnp.concatenate([jnp.where(lane == h, q, zero) for h in range(HEADS)], axis=0)
    scale = z.hd ** (-0.5) * LOG2E
    dev = lax.axis_index("gx") * ny + lax.axis_index("gy")
    window = dev * z.w + lax.broadcasted_iota(jnp.int32, (1, nq), 1) % z.w

    def image(j, span):
        low, high = span
        bound = bounds_ref[j]
        return jnp.where(bound <= window, bound, low), jnp.where(bound > window, jnp.minimum(high, bound), high)

    low, high = lax.fori_loop(
        0, bounds_ref.shape[0], image,
        (jnp.zeros((1, nq), jnp.int32), jnp.full((1, nq), n, jnp.int32)),
    )
    key = lax.broadcasted_iota(jnp.int32, (kc, nq), 0)

    def reach(j, span):
        bound = bounds_ref[j]
        return (
            jnp.where(bound <= dev * z.w, bound, span[0]),
            jnp.where(bound > dev * z.w + z.w - 1, jnp.minimum(span[1], bound), span[1]),
        )

    begin, end = lax.fori_loop(0, bounds_ref.shape[0], reach, (jnp.int32(0), jnp.int32(n)))
    begin, end = begin // kc, (end + kc - 1) // kc

    def blank(i, _):
        rows = pl.ds(pl.multiple_of(i * kc, kc), kc)
        nr_ref[rows, :] = jnp.zeros((kc, z.d), BF16)
        kv_ref[rows, :] = jnp.zeros((kc, 2 * z.d), BF16)
        p_ref[rows, :] = jnp.zeros((kc, nq), BF16)
        return 0

    lax.fori_loop(0, begin, blank, 0)
    lax.fori_loop(end, n // kc, blank, 0)

    def scores(i, top):
        rows = pl.ds(pl.multiple_of(i * kc, kc), kc)
        hat, _ = norm_stats(all_ref[rows, :].astype(F32))
        nr = (hat * gain_ref[...] + shift_ref[...]).astype(BF16)
        nr_ref[rows, :] = nr
        kv = mm(nr, w_ref[:, z.d :]).astype(BF16)
        kv_ref[rows, :] = kv
        s = mm_nt(kv[:, : z.d], qbd) * scale
        s = jnp.where((key >= low - i * kc) & (key < high - i * kc), s, -1e30)
        s_ref[rows, :] = s
        return jnp.maximum(top, jnp.max(s, axis=0, keepdims=True))

    top = lax.fori_loop(begin, end, scores, jnp.full((1, nq), -1e30, F32))

    def weigh(i, total):
        rows = pl.ds(pl.multiple_of(i * kc, kc), kc)
        p = jnp.exp2(s_ref[rows, :] - top)
        s_ref[rows, :] = p
        return total + jnp.sum(p, axis=0, keepdims=True)

    total = lax.fori_loop(begin, end, weigh, jnp.zeros((1, nq), F32))
    inverse = 1.0 / total

    def attend(i, acc):
        rows = pl.ds(pl.multiple_of(i * kc, kc), kc)
        p = (s_ref[rows, :] * inverse).astype(BF16)
        p_ref[rows, :] = p
        return acc + mm_tn(p, kv_ref[rows, z.d :])

    full = lax.fori_loop(begin, end, attend, jnp.zeros((nq, z.d), F32))
    o = full[(HEADS - 1) * z.w :]
    for h in range(HEADS - 2, -1, -1):
        o = jnp.where(lane == h, full[h * z.w : (h + 1) * z.w], o)
    of_ref[...] = o
    o = o.astype(BF16)
    o_ref[...] = o
    r2 = own_ref[...].astype(F32) + mm(o, wo_ref[...]) + bo_ref[...]
    sel_t = one_hot_t(ord_ref[...], z.w).astype(F32)
    r2 = lax.dot_general(
        sel_t, r2, (((0,), (0,)), ((), ())), precision=HIGH, preferred_element_type=F32
    )
    for c in range(z.nb):
        r2_ref[c, : z.k, :] = r2[c * z.k : (c + 1) * z.k]
        r2_ref[c, z.k :, :] = jnp.zeros((z.kp - z.k, z.d), F32)


def local_fwd_kernel(
    z, qkv_ref, xp_ref, r2_ref, gain_ref, shift_ref, w_ref, wo_ref, bo_ref,
    t2_ref, p_ref, qw_ref, o_ref, qs, os,
):
    tiles = 3 * z.groups
    for j in range(tiles):
        qs[j, : z.r, :] = qkv_ref[0, :, j * LANES : (j + 1) * LANES].astype(F32)
        if z.wide > z.r:
            qs[j, z.r :, :] = jnp.zeros((z.wide - z.r, LANES), F32)
    hat, _ = norm_stats(r2_ref[0])
    nt = (hat * gain_ref[...] + shift_ref[...]).astype(BF16)
    reg = mm(nt, w_ref[...]).astype(BF16).astype(F32)
    for j in range(tiles):
        qs[j, : z.k, :] = reg[: z.k, j * LANES : (j + 1) * LANES]
    masks = head_masks(SEG, z.hd)
    pad = jnp.zeros((SEG - 56, LANES), F32)
    valid = lax.broadcasted_iota(jnp.int32, (56, z.per_group * SEG), 0) < z.tok + 1
    scale = z.hd ** (-0.5) * LOG2E
    tail = jnp.zeros((SEG - 56, z.per_group * SEG), F32)

    def windows(i, _):
        jobs = [(i * z.side + j, g) for j in range(z.side) for g in range(z.groups)]

        def load(w, j):
            rows = qs[j, pl.ds(w, 56, stride=z.k), :]
            got = jnp.concatenate([rows, pad], axis=0).astype(BF16)
            qw_ref[w, j] = got
            return got

        q = [load(w, g) for w, g in jobs]
        k = [load(w, z.groups + g) for w, g in jobs]
        v = [load(w, 2 * z.groups + g) for w, g in jobs]
        s = [mm_nt(kk, spread(qq, masks))[:56] for qq, kk in zip(q, k)]
        s = [jnp.where(valid, x, -1e30) for x in s]
        p = [jnp.exp2((x - jnp.max(x, axis=0, keepdims=True)) * scale) for x in s]
        p = [x * (1.0 / jnp.sum(x, axis=0, keepdims=True)) for x in p]
        p = [jnp.concatenate([x, tail], axis=0).astype(BF16) for x in p]
        for (w, g), x in zip(jobs, p):
            p_ref[w, g] = x
        full = [mm_tn(x, vv) for x, vv in zip(p, v)]
        for (w, g), x in zip(jobs, full):
            os[g, pl.ds(w, 56, stride=z.k), :] = unspread(x, 56, SEG, masks)
        return 0

    lax.fori_loop(0, z.k // z.side, windows, 0)
    for i in range(z.r // z.chunk):
        rows = slice(i * z.chunk, (i + 1) * z.chunk)
        o = jnp.concatenate([os[g, rows, :] for g in range(z.groups)], axis=1).astype(BF16)
        o_ref[0, rows, :] = o
        t2_ref[0, rows, :] = xp_ref[0, rows, :].astype(F32) + mm(o, wo_ref[...]) + bo_ref[...]
    t2_ref[0, : z.k, :] = t2_ref[0, : z.k, :] + r2_ref[0, : z.k, :]


def tiles_dot(lhs, w, acc, transposed=False):
    side = 256
    for k in range(w.shape[0] // side):
        for j in range(len(acc)):
            ks, js = slice(k * side, (k + 1) * side), slice(j * side, (j + 1) * side)
            pltpu.matmul_push_rhs(w[js, ks] if transposed else w[ks, js], k % 2, j, transpose=transposed)
            pltpu.matmul_acc_lhs(acc[j], lhs(k), load_staged_rhs=k % 2)


def mlp_kernel(z, nx, ny, acts, done, *refs):
    (t2_ref, *e_refs), refs = refs[: 1 + z.nb], refs[1 + z.nb :]
    (
        gain_ref, shift_ref, wu_ref, bu_ref, wd_ref, bd_ref,
        y_ref, gt_ref, buf_ref, small_ref, gbu_ref,
        n2, e, n2_t, e_t, h0, h1, d0, d1, active, dh, yacc, dn, buf, recv, full, sems, copy_sem,
    ) = refs
    f = pl.program_id(0)
    parts = pl.num_programs(0)
    mesh = Mesh2(nx, ny)
    sums = mlp_sums(mesh, z, buf, recv, full, sems)
    per = len(acts) // MLP_PARTS
    sub, side = math.gcd(z.m, 32), 256
    fc = wu_ref.shape[1]
    m = h0.shape[0]
    chunks = z.t // m

    def rows_of(c):
        return slice(c * m, (c + 1) * m)

    def tick(p):
        for step in range(len(acts) // per):
            if acts[step * per + p]:

                @pl.when(f == step)
                def _():
                    act(sums, acts[step * per + p])

    @pl.when(f == 0)
    def _():
        fetch = [
            pltpu.make_async_copy(e_refs[c], e.at[c * z.r : (c + 1) * z.r, :], copy_sem.at[c])
            for c in range(z.nb)
        ]
        begin = [
            pltpu.make_async_copy(t2_ref.at[rows_of(c), :], yacc.at[rows_of(c), :], copy_sem.at[8 + c])
            for c in range(chunks)
        ]
        for x in begin + fetch:
            x.start()
        mesh.barrier(all_rounds(nx, ny))

        def prepare(i, _):
            rows = pl.ds(pl.multiple_of(i * sub, 16), sub)
            hat, _ = norm_stats(yacc[rows, :])
            n2[rows, :] = (hat * gain_ref[...] + shift_ref[...]).astype(BF16)
            dn[rows, :] = jnp.zeros((sub, z.d), F32)
            return 0

        for x in begin:
            x.wait()
        lax.fori_loop(0, z.t // sub, prepare, 0, unroll=6)
        for x in fetch:
            x.wait()
        if z.tp > z.t:
            for x in (n2, e, active, dh):
                x[z.t :, :] = jnp.zeros((z.tp - z.t, x.shape[1]), BF16)

        def turn(i, _):
            span = pl.ds(pl.multiple_of(i * side, side), side)
            n2_t[: z.d, span] = n2[span, :].T
            e_t[: z.d, span] = e[span, :].T
            n2_t[z.d :, span] = jnp.ones((16, side), BF16)
            e_t[z.d :, span] = jnp.zeros((16, side), BF16)
            return 0

        lax.fori_loop(0, z.tp // side, turn, 0)

    def result(c):
        rows = pl.ds(pl.multiple_of(c * m, 16), m)
        return (
            pltpu.make_async_copy(n2.at[rows], y_ref.at[rows], copy_sem.at[8 + 2 * c]),
            pltpu.make_async_copy(e.at[rows], gt_ref.at[rows], copy_sem.at[9 + 2 * c]),
        )

    slots = (h0, h1)

    def again(c, slot):
        rows = pl.ds(pl.multiple_of(c * m, 16), m)
        return pltpu.make_async_copy(t2_ref.at[rows], slots[slot], copy_sem.at[slot])

    tick(0)
    bias = bu_ref[...]

    def stream(*accs):
        one, two = accs[:2], accs[2:]
        h, d = (h0, h1), (d0, d1)

        def rows(c):
            return pl.ds(pl.multiple_of(c * m, 16), m)

        def up(c, slot):
            tiles_dot(lambda k: n2[rows(c), k * side : (k + 1) * side], wu_ref, one)
            for j in range(2):
                h[slot][:, j * side : (j + 1) * side] = pltpu.matmul_pop(one[j])
            tiles_dot(lambda k: e[rows(c), k * side : (k + 1) * side], wd_ref, two, True)
            for j in range(2):
                d[slot][:, j * side : (j + 1) * side] = pltpu.matmul_pop(two[j])

        def down(c):
            tiles_dot(lambda k: active[rows(c), k * side : (k + 1) * side], wd_ref, one)
            for j in range(2):
                yacc[rows(c), j * side : (j + 1) * side] += pltpu.matmul_pop(one[j])
            tiles_dot(lambda k: dh[rows(c), k * side : (k + 1) * side], wu_ref, two, True)
            for j in range(2):
                dn[rows(c), j * side : (j + 1) * side] += pltpu.matmul_pop(two[j])

        def middle(c, slot):
            for i in range(m // 16):
                r, o = slice(i * 16, (i + 1) * 16), pl.ds(pl.multiple_of(c * m + i * 16, 16), 16)
                value, slope = gelu_both(h[slot][r, :] + bias)
                active[o, :] = value.astype(BF16)
                dh[o, :] = (d[slot][r, :] * slope).astype(BF16)

        def pair(i, _):
            for slot in range(2):
                c = 2 * i + slot
                up(jnp.minimum(c + 1, chunks - 1), 1 - slot)
                middle(c, slot)
                down(c)
            return 0

        up(0, 0)
        for i in range(3):
            lax.fori_loop(chunks // 2 * i // 3, chunks // 2 * (i + 1) // 3, pair, 0)
            tick(1 + i)

    pl.run_scoped(stream, *[pltpu.ACC(mxu_id=i)((m, side), F32) for i in (0, 1, 0, 1)])
    @pl.when(f == parts - 1)
    def _():
        for slot in range(2):
            again(slot, slot).start()

    tick(4)
    here = pl.multiple_of(f * (2 * fc), 16)

    def gradients(acc0, acc1):
        acc = (acc0, acc1)
        halves = [slice(j * side, (j + 1) * side) for j in range(2)]

        def over_tokens(left, right):
            def two(i, _):
                for k in range(2):
                    span = pl.ds(pl.multiple_of((2 * i + k) * side, side), side)
                    for j in range(2):
                        pltpu.matmul_push_rhs(right[span, halves[j]], k, j)
                        pltpu.matmul_acc_lhs(acc[j], left[:, span], load_staged_rhs=k)
                return 0

            lax.fori_loop(0, z.tp // (2 * side), two, 0)

        over_tokens(e_t, active)
        for j in range(2):
            rows = pl.ds(pl.multiple_of(here + j * side, 16), side)
            buf[rows, :] = pltpu.matmul_pop(acc[j])[: z.d].T.astype(BF16)
        tick(5)
        over_tokens(n2_t, dh)
        for j in range(2):
            got = pltpu.matmul_pop(acc[j])
            buf[pl.ds(pl.multiple_of(here + fc, 16), z.d), halves[j]] = got[: z.d].astype(BF16)
            gbu_ref[0, :, halves[j]] = got[z.d : z.d + 1]

    pl.run_scoped(
        gradients, pltpu.ACC(mxu_id=0)((z.d + 16, side), F32), pltpu.ACC(mxu_id=1)((z.d + 16, side), F32)
    )
    tick(6)

    @pl.when(f == parts - 1)
    def _():
        def pair(i, sums):
            for slot in range(2):
                c = 2 * i + slot
                again(c, slot).wait()

                def close(j, sums):
                    here = pl.ds(pl.multiple_of(j * sub, 16), sub)
                    rows = pl.ds(pl.multiple_of(c * m + j * sub, 16), sub)
                    up = e[rows, :].astype(F32)
                    n2[rows, :] = (yacc[rows, :] + bd_ref[...]).astype(BF16)
                    hat, rstd = norm_stats(slots[slot][here, :])
                    d = dn[rows, :]
                    gt = (up + norm_back(hat, rstd, gain_ref[...], d)).astype(BF16)
                    e[rows, :] = gt
                    return (
                        sums[0] + colsum(d * hat), sums[1] + colsum(d), sums[2] + colsum(up),
                        sums[3] + colsum(gt.astype(F32)),
                    )

                sums = lax.fori_loop(0, m // sub, close, sums, unroll=13)
                for x in result(c):
                    x.start()

                @pl.when(c + 2 < chunks)
                def _():
                    again(c + 2, slot).start()

            return sums

        got = lax.fori_loop(0, chunks // 2, pair, (jnp.zeros((1, z.d), F32),) * 4)
        small_ref[...] = jnp.zeros_like(small_ref)
        for i in range(4):
            small_ref[i : i + 1, :] = got[i]

    tick(7)

    @pl.when(f == parts - 1)
    def _():
        out = carry(sums, done, buf_ref, copy_sem, True)
        for x in out:
            x.start()
        for x in out:
            x.wait()
        for c in range(chunks):
            for x in result(c):
                x.wait()


def mlp_count(nx, ny, rows):
    count = 2 * MLP_PARTS
    while rows // count % (16 * nx * ny):
        count //= 2
    return count


def mlp_ready(i, count, head, part_us):
    unit = (i + 1) * (2 * MLP_PARTS // count) - 1
    return head + part_us * (unit // 2 + (0.9 if unit % 2 == 0 else 1.0))


def mlp_sums(mesh, z, buf, recv, full, sems):
    nx, ny = mesh.n["gx"], mesh.n["gy"]
    count = mlp_count(nx, ny, buf.shape[0])
    rows = buf.shape[0] // count
    sem0, out = 0, []
    for i in range(count):
        rounds = mlp_route(nx, ny, i, count)
        out.append(Sum(mesh, buf, i * rows, rows, rounds, recv, i * rows, sems, sem0, full))
        sem0 += 2 * sems_of(rounds)
    return out


def mlp_route(nx, ny, i, count):
    first, other = routes_of(nx, ny)
    if i == count - 1:
        return other
    return long_first(first) if i in (3, 6) else first


def long_first(rounds):
    return rounds[:1] + rounds[-1:] + rounds[1:-1]


def local_bwd_kernel(
    z, nx, ny, acts, before, done, gt_ref, xp_ref, r2_ref, o_ref, p_ref, qw_ref, code_ref, gain_ref, shift_ref, w_ref,
    wo_ref, part_ref, y_ref,
    pg_ref, dt0_ref, gwq_ref, gwo_ref, small_ref, buf_ref, yin_ref,
    ds_, dq_, dqkv, dtp, buf, recv, full, sems, ysems, copy_sem,
):
    step = pl.program_id(0)
    steps = pl.num_programs(0)
    mesh = Mesh2(nx, ny)
    sums = mlp_sums(mesh, z, buf, recv, full, sems)
    per = len(acts) // z.nb

    def tick(p):
        for i in range(z.nb):
            if acts[i * per + p]:

                @pl.when(step == i)
                def _():
                    act(sums, acts[i * per + p])

    units = z.early // 16

    def send(o, i):
        rows = pl.ds(units * i // z.nb * 16, (units * (i + 1) // z.nb - units * i // z.nb) * 16)
        return pltpu.make_async_remote_copy(
            src_ref=y_ref.at[o, rows], dst_ref=yin_ref.at[o, rows], send_sem=ysems.at[0, o * z.nb + i],
            recv_sem=ysems.at[1, o * z.nb + i], device_id=mesh.beside(nx - o),
            device_id_type=pl.DeviceIdType.MESH,
        )

    own_y = pltpu.make_async_copy(y_ref.at[0, : z.early], yin_ref.at[0], ysems.at[0, 0])

    @pl.when(step == 0)
    def _():
        gwq_ref[...] = jnp.zeros_like(gwq_ref)
        gwo_ref[...] = jnp.zeros_like(gwo_ref)
        small_ref[...] = jnp.zeros_like(small_ref)
        fetch = carry(sums, before, part_ref, copy_sem, False)
        for x in fetch:
            x.start()
        mesh.barrier(all_rounds(nx, ny), row=True)
        own_y.start()
        for x in fetch:
            x.wait()

    tick(0)
    for i in range(z.nb):

        @pl.when(step == i)
        def _(i=i):
            for o in range(1, nx):
                send(o, i).start()

    gt = gt_ref[0]
    dot = mm_nt(gt, wo_ref[...])
    for j in range(z.groups):
        ds_[j, : z.r, :] = dot[:, j * LANES : (j + 1) * LANES]
        if z.wide > z.r:
            ds_[j, z.r :, :] = jnp.zeros((z.wide - z.r, LANES), F32)
    gwo_ref[...] += mm_tn(o_ref[0], gt)
    masks = head_masks(SEG, z.hd)
    pad = jnp.zeros((SEG - 56, LANES), F32)
    scale = z.hd ** (-0.5)

    def windows(i, _):
        jobs = [(i * z.side + j, g) for j in range(z.side) for g in range(z.groups)]
        do = [
            jnp.concatenate([ds_[g, pl.ds(w, 56, stride=z.k), :], pad], axis=0).astype(BF16)
            for w, g in jobs
        ]
        dobd = [spread(x, masks) for x in do]
        dp = [mm_nt(qw_ref[w, 2 * z.groups + g], x) for (w, g), x in zip(jobs, dobd)]
        dv = [mm(p_ref[w, g], x) for (w, g), x in zip(jobs, dobd)]
        for (w, g), x in zip(jobs, dv):
            dq_[2 * z.groups + g, pl.ds(w, 56, stride=z.k), :] = x[:56]
        ds = []
        for (w, g), x in zip(jobs, dp):
            pf = p_ref[w, g].astype(F32)
            t = pf * x
            ds.append((t - pf * jnp.sum(t, axis=0, keepdims=True)).astype(BF16))
        dk = [mm(x, spread(qw_ref[w, g], masks)) for (w, g), x in zip(jobs, ds)]
        for (w, g), x in zip(jobs, dk):
            dq_[z.groups + g, pl.ds(w, 56, stride=z.k), :] = x[:56] * scale
        full = [mm_tn(x, qw_ref[w, z.groups + g]) for (w, g), x in zip(jobs, ds)]
        for (w, g), x in zip(jobs, full):
            dq_[g, pl.ds(w, 56, stride=z.k), :] = unspread(x, 56, SEG, masks) * scale
        return 0

    rounds = z.k // z.side
    for i in range(BWD_TICKS):
        lax.fori_loop(rounds * i // BWD_TICKS, rounds * (i + 1) // BWD_TICKS, windows, 0)
        tick(1 + i)
    for j in range(3 * z.groups):
        dqkv[:, j * LANES : (j + 1) * LANES] = dq_[j, : z.r, :].astype(BF16)
    dn = mm_nt(dqkv[...], w_ref[...])
    t = xp_ref[0].astype(F32)
    t = jnp.concatenate([r2_ref[0, : z.k, :], t[z.k :]], axis=0)
    hat, rstd = norm_stats(t)
    nt = (hat * gain_ref[...] + shift_ref[...]).astype(BF16)
    gwq_ref[...] += mm_tn(nt, dqkv[...])
    dt = gt.astype(F32) + norm_back(hat, rstd, gain_ref[...], dn)
    dt0_ref[0, : z.k, :] = dt[: z.k]
    dt0_ref[0, z.k :, :] = jnp.zeros((z.kp - z.k, z.d), F32)
    dtp[step] = dt.astype(BF16)
    small_ref[0:1, :] += colsum(dn * hat)
    small_ref[1:2, :] += colsum(dn)
    tick(1 + BWD_TICKS)

    @pl.when(step == steps - 1)
    def _():
        sel_t = one_hot_t(code_ref[...], z.gp * z.w)
        for g in range(z.ng):
            unpack_group(z, g, sel_t, dtp, pg_ref, None)

    tick(2 + BWD_TICKS)

    @pl.when(step == steps - 1)
    def _():
        out = carry(sums, done, buf_ref, copy_sem, True)
        for x in out:
            x.start()
        own_y.wait()
        for o in range(1, nx):
            for i in range(z.nb):
                send(o, i).wait()
        for x in out:
            x.wait()


def bit_list(count, axis):
    return [(axis, b) for b in range(count.bit_length() - 1)]


def n_bits(count):
    return count.bit_length() - 1


def stage_costs(nx, ny, rounds, size):
    xs = n_bits(ny) // 2
    costs, share = [], size
    for group in rounds:
        share /= 1 << len(group)
        wire = {}
        if group == (("gx", 0),):
            costs.append((2.5, wire))
            continue
        for axis, b in group:
            name, far = ("y", b > 1) if axis == "gx" else ("x", b > 0) if b < xs else ("z", b > xs)
            wire[name] = max(wire.get(name, 0.0), (8 if far else 4) * share / 85e3)
        costs.append((LATENCY_US, wire))
    return costs + costs[::-1]


class Mesh2:
    def __init__(self, nx, ny):
        self.n = {"gx": nx, "gy": ny}
        self.at = {"gx": lax.axis_index("gx"), "gy": lax.axis_index("gy")}

    def bit(self, which):
        axis, b = which
        return lax.rem(self.at[axis] // (1 << b), 2)

    def flips(self, group):
        return [
            [which for i, which in enumerate(group) if m >> (len(group) - 1 - i) & 1]
            for m in range(1, 1 << len(group))
        ]

    def partner(self, flipped):
        at = dict(self.at)
        for axis, b in flipped:
            at[axis] = at[axis] + (1 - 2 * self.bit((axis, b))) * (1 << b)
        return (at["gx"], at["gy"])

    def share(self, group, flipped=()):
        index = 0
        for which in group:
            bit = self.bit(which)
            index = 2 * index + (1 - bit if which in flipped else bit)
        return index

    def beside(self, o):
        return (lax.rem(self.at["gx"] + o, self.n["gx"]), self.at["gy"])

    def barrier(self, rounds, row=False):
        sem = pltpu.get_barrier_semaphore()
        sets = []
        for group in rounds:
            sets += [x for x in self.flips(group) if sorted(x) not in [sorted(y) for y in sets]]
        if row:
            sets = [x for x in sets if any(axis == "gy" for axis, _ in x)]
        others = [self.partner(x) for x in sets]
        if row:
            others += [self.beside(o) for o in range(1, self.n["gx"])]
        for other in others:
            pl.semaphore_signal(sem, inc=1, device_id=other, device_id_type=pl.DeviceIdType.MESH)
        pl.semaphore_wait(sem, len(others))


def routes_of(nx, ny):
    core, ys, g = [("gx", 0)], bit_list(nx, "gx")[1:], bit_list(ny, "gy")
    xs, zs = g[: len(g) // 2], g[len(g) // 2 :]
    if len(g) == 3:
        xs, zs = g[:1], g[1:]
    plane = [tuple(x) for x in zip(ys, xs)]
    line = [tuple(zs)]
    first = [tuple(core)] + plane + line
    other = [tuple(core)] + [tuple(x) for x in zip(xs, zs)]
    left = [x for x in ys + g if not any(x in group for group in other)]
    while left:
        other.append(tuple(left[:2]))
        left = left[2:]
    return first, other


def all_rounds(nx, ny):
    first, other = routes_of(nx, ny)
    return first + other


def place_of(order, nx, ny, dev):
    gx, gy = dev // ny, dev % ny
    p = 0
    for axis, b in order:
        p = 2 * p + (((gx if axis == "gx" else gy) >> b) & 1)
    return p


def flat(rounds):
    return [which for group in rounds for which in group]


def remote(mesh, src, dst, sems, i, flipped):
    return pltpu.make_async_remote_copy(
        src_ref=src, dst_ref=dst, send_sem=sems.at[0, i], recv_sem=sems.at[1, i],
        device_id=mesh.partner(flipped), device_id_type=pl.DeviceIdType.MESH,
    )


def sems_of(rounds):
    return sum((1 << len(group)) - 1 for group in rounds)


class Sum:
    def __init__(self, mesh, buf, start, rows, rounds, recv, recv_start, sems, sem0, full=None):
        self.mesh, self.buf, self.rounds, self.sems, self.sem0 = mesh, buf, rounds, sems, sem0
        self.recv, self.recv0, self.first, self.total = recv, recv_start, start, rows
        self.full = full
        self.n = len(rounds)
        self.stages = self.n * (2 if full is not None else 1)

    def held(self, s):
        off, rows = self.first, self.total
        for group in self.rounds[:s]:
            rows //= 1 << len(group)
            off = off + self.mesh.share(group) * rows
        return off, rows

    def recv_base(self, s):
        rows, base = self.total, self.recv0
        for group in self.rounds[:s]:
            part = rows >> len(group)
            base += rows - part
            rows = part
        return base

    def copies(self, s):
        back = s >= self.n
        r = 2 * self.n - 1 - s if back else s
        group = self.rounds[r]
        sem = self.sem0 + (sems_of(self.rounds) if back else 0) + sems_of(self.rounds[:r])
        off, rows = self.held(r)
        part = rows >> len(group)
        out = []
        for i, flipped in enumerate(self.mesh.flips(group)):
            if back:
                mine = pl.multiple_of(off + self.mesh.share(group) * part, 16)
                src = dst = self.full.at[pl.ds(mine, part)]
            else:
                theirs = pl.multiple_of(off + self.mesh.share(group, flipped) * part, 16)
                src = self.buf.at[pl.ds(theirs, part)]
                dst = self.recv.at[pl.ds(self.recv_base(r) + i * part, part)]
            out.append(remote(self.mesh, src, dst, self.sems, sem + i, flipped))
        return out

    def start(self, s):
        for x in self.copies(s):
            x.start()

    def finish(self, s):
        for x in self.copies(s):
            x.wait()
        if s < self.n:
            off, part = self.held(s + 1)
            base = self.recv_base(s)
            count = (1 << len(self.rounds[s])) - 1
            step = math.gcd(part, 64)
            into = self.full if s == self.n - 1 and self.full is not None else self.buf

            def add(i, _):
                mine = pl.ds(pl.multiple_of(off + i * step, 16), step)
                total = self.buf[mine, :].astype(F32)
                for j in range(count):
                    theirs = pl.ds(pl.multiple_of(base + j * part + i * step, 16), step)
                    total = total + self.recv[theirs, :].astype(F32)
                into[mine, :] = total.astype(BF16)
                return 0

            lax.fori_loop(0, part // step, add, 0)


def carry(sums, done, where, sem, out):
    copies = []
    for x, s in zip(sums, done):
        off, rows = x.held(min(s, 2 * x.n - s))
        rows = pl.ds(pl.multiple_of(off, 16), rows)
        mine = (x.buf if s < x.n else x.full).at[rows]
        src, dst = (mine, where.at[rows]) if out else (where.at[rows], mine)
        copies.append(pltpu.make_async_copy(src, dst, sem.at[len(copies)]))
    return copies


def plan(ready, done, stages, cost, slots, end, share=1.0):
    acts = [[] for _ in slots]
    done = list(done)
    running = [None] * len(done)
    free = {"x": 0.0, "y": 0.0, "z": 0.0}
    rate = {"x": 1.0, "y": share, "z": 1.0}
    for i, now in enumerate(slots):
        last = i == len(slots) - 1
        for j in range(len(done)):
            if ready[j] > now:
                continue
            stop = None
            if running[j] is not None:
                if now < running[j] and not last:
                    continue
                stop = done[j]
                done[j] += 1
                running[j] = None
            go = None
            if done[j] < stages and not last:
                latency, wire = cost[j][done[j]]
                over = max([now] + [max(free[c], now) + wire[c] / rate[c] for c in wire]) + latency
                if over <= end + SLACK_US:
                    go = done[j]
                    running[j] = over
                    for c in wire:
                        free[c] = max(free[c], now) + wire[c] / rate[c]
            if stop is not None or go is not None:
                acts[i].append((j, stop, go))
    return acts, done


def act(sums, acts):
    for j, stop, go in acts:
        if stop is not None:
            sums[j].finish(stop)
        if go is not None:
            sums[j].start(go)


class Gather:
    def __init__(self, mesh, buf, rows, rounds, sems, sem0):
        self.mesh, self.buf, self.rounds, self.sems, self.sem0 = mesh, buf, rounds, sems, sem0
        self.block = rows
        self.stages = len(rounds)

    def held(self, s):
        off, rows = 0, self.block << len(flat(self.rounds))
        for group in self.rounds[: self.stages - s]:
            rows >>= len(group)
            off = off + self.mesh.share(group) * rows
        return pl.multiple_of(off, 16), rows

    def copies(self, s):
        group = self.rounds[self.stages - 1 - s]
        here = self.buf.at[pl.ds(*self.held(s))]
        sem = self.sem0 + sems_of(self.rounds[: self.stages - 1 - s])
        return [
            remote(self.mesh, here, here, self.sems, sem + i, flipped)
            for i, flipped in enumerate(self.mesh.flips(group))
        ]

    def start(self, s):
        for x in self.copies(s):
            x.start()

    def finish(self, s):
        for x in self.copies(s):
            x.wait()


def region_bwd_kernel(
    z, nx, ny, done,
    dt0_ref, all_ref, o_ref, of_ref, p_ref, kv_ref, nr_ref, q_ref, nown_ref, own_ref, ord_ref, gain_ref,
    w_ref, wo_ref, gwq_ref, gwo_ref, smalla_ref, smallm_ref, gbu_ref, part_ref, y_ref,
    mlp_ref, att_ref, vec_ref, dnr_ref, dt0a_ref, dnown_ref, yin_ref,
    dobd, qbd, delta, acc, gacc, small, buf, recv, full, abuf, arecv, afull, vbuf, dbuf, drecv,
    sems, asems, ysems, copy_sem,
):
    step = pl.program_id(0)
    steps = pl.num_programs(0)
    mesh = Mesh2(nx, ny)
    d = z.d
    kc = all_ref.shape[0]
    nq = HEADS * z.w
    n = nx * ny
    scale = z.hd ** (-0.5)
    rest = mlp_sums(mesh, z, buf, recv, full, sems)
    first, other = routes_of(nx, ny)
    last = long_first(first)
    order_d = flat(first)
    bits = len(order_d)
    lane = lax.broadcasted_iota(jnp.int32, (z.w, d), 1) // z.hd

    late = pl.ds(z.early, z.r - z.early)

    def send(o):
        return pltpu.make_async_remote_copy(
            src_ref=y_ref.at[o, late], dst_ref=yin_ref.at[o], send_sem=ysems.at[0, o],
            recv_sem=ysems.at[1, o], device_id=mesh.beside(nx - o),
            device_id_type=pl.DeviceIdType.MESH,
        )

    own_y = pltpu.make_async_copy(y_ref.at[0, late], yin_ref.at[0], ysems.at[0, 0])

    sums, sem0 = [], bits
    split = max(x for x in (1, 2, 4) if (4 * d // x) % (16 * n) == 0 or x == 1)
    for i in range(split):
        rows = 4 * d // split
        rounds = first if i < 3 else last
        sums.append(Sum(mesh, abuf, i * rows, rows, rounds, arecv, i * rows, asems, sem0, afull))
        sem0 += 2 * sems_of(rounds)
    sums.append(Sum(mesh, dbuf, 0, n * z.w, first, drecv, 0, asems, sem0))

    @pl.when(step == 0)
    def _():
        fetch = carry(rest, done, part_ref, copy_sem, False)
        for x in fetch:
            x.start()
        mesh.barrier(all_rounds(nx, ny), row=True)
        for x in fetch:
            x.wait()
        for x, s in zip(rest, done):
            if s < x.stages:
                x.start(s)
        for o in range(1, nx):
            send(o).start()
        own_y.start()
        dt0 = jnp.concatenate([dt0_ref[c, : z.k, :] for c in range(z.nb)], axis=0)
        sel_t = one_hot_t(ord_ref[...], z.w).astype(F32)
        dt0 = jnp.dot(sel_t, dt0, precision=HIGH, preferred_element_type=F32)
        dt0a_ref[...] = dt0
        gr = dt0.astype(BF16)
        abuf[3 * d :, :] = (gwo_ref[...] + mm_tn(o_ref[...], gr)).astype(BF16)
        do = mm_nt(gr, wo_ref[...]).astype(BF16)
        zero = jnp.zeros_like(do)
        q = q_ref[...]
        for h in range(HEADS):
            dobd[h * z.w : (h + 1) * z.w, :] = jnp.where(lane == h, do, zero)
            qbd[h * z.w : (h + 1) * z.w, :] = jnp.where(lane == h, q, zero)
        prod = do.astype(F32) * of_ref[...]
        spread_prod = jnp.concatenate([jnp.where(lane == h, prod, 0.0) for h in range(HEADS)], axis=0)
        delta[...] = lax.dot_general(
            jnp.ones((8, d), F32), spread_prod, (((1,), (1,)), ((), ())), precision=HIGH,
            preferred_element_type=F32,
        )
        small[...] = jnp.zeros_like(small)
        small[2:3, :] = colsum(gr.astype(F32))
        acc[...] = jnp.zeros_like(acc)
        gacc[...] = gwq_ref[...]

    p = p_ref[...]
    ds = (p.astype(F32) * (mm_nt(kv_ref[:, d:], dobd[...]) - delta[0:1, :])).astype(BF16)
    dv = mm(p, dobd[...]).astype(BF16)
    dk = (mm(ds, qbd[...]) * scale).astype(BF16)
    dkv = jnp.concatenate([dk, dv], axis=1)
    gacc[:, d:] += mm_tn(nr_ref[...], dkv)
    dn = mm_nt(dkv, w_ref[:, d:])
    acc[...] += mm_tn(ds, kv_ref[:, :d])
    hat, _ = norm_stats(all_ref[...].astype(F32))
    small[0:1, :] += colsum(dn * hat)
    small[1:2, :] += colsum(dn)
    per = kc // z.w
    for j in range(per):
        dev = step * per + j
        at = {"gx": dev // ny, "gy": lax.rem(dev, ny)}
        place = 0
        for axis, b in order_d:
            place = 2 * place + lax.rem(at[axis] // (1 << b), 2)
        dbuf[pl.ds(pl.multiple_of(place * z.w, 16), z.w), :] = dn[j * z.w : (j + 1) * z.w].astype(BF16)

    @pl.when(step == steps - 1)
    def _():
        sums[split].start(0)
        dq = acc[(HEADS - 1) * z.w :, :]
        for h in range(HEADS - 2, -1, -1):
            dq = jnp.where(lane == h, acc[h * z.w : (h + 1) * z.w, :], dq)
        dq = (dq * scale).astype(BF16)
        abuf[:d, :] = (gacc[:, :d] + mm_tn(nown_ref[...], dq)).astype(BF16)
        for f in range(1, 3):
            abuf[f * d : (f + 1) * d, :] = gacc[:, f * d : (f + 1) * d].astype(BF16)
        for x in sums[:split]:
            x.start(0)
        dnown = mm_nt(dq, w_ref[:, :d])
        dnown_ref[...] = dnown
        hat, _ = norm_stats(own_ref[...].astype(F32))
        vbuf[0] = jnp.zeros_like(vbuf[0])
        vbuf[0, 0:1, :] = smalla_ref[0:1, :] + small[0:1, :] + colsum(dnown * hat)
        vbuf[0, 1:2, :] = smalla_ref[1:2, :] + small[1:2, :] + colsum(dnown)
        vbuf[0, 2:3, :] = smallm_ref[3:4, :] + small[2:3, :]
        vbuf[0, 3:6, :] = smallm_ref[0:3, :]
        row = 6
        for f in range(MLP_PARTS):
            for i in range(gbu_ref.shape[2] // d):
                vbuf[0, row : row + 1, :] = gbu_ref[f, :, i * d : (i + 1) * d]
                row += 1
        queue = [(x, 0) for x in sums[split:] + sums[:split]]
        queue += [(x, s) for x, s in zip(rest, done) if s < x.stages]
        vec = None
        for s in range(max(bits, 2 * len(first)) + 1):
            for x, s0 in queue:
                if s and s0 + s - 1 < x.stages:
                    x.finish(s0 + s - 1)
                if s and s0 + s < x.stages:
                    x.start(s0 + s)
            if s <= bits:
                if s:
                    vec.wait()
                    vbuf[2 * s] = vbuf[2 * s - 2] + vbuf[2 * s - 1]
                if s < bits:
                    vec = remote(mesh, vbuf.at[2 * s], vbuf.at[2 * s + 1], asems, s, [order_d[s]])
                    vec.start()
        vec_ref[...] = vbuf[2 * bits]
        dnr_ref[...] = dbuf[pl.ds(pl.multiple_of(sums[split].held(len(first))[0], 16), z.w), :]
        outs = [
            pltpu.make_async_copy(full, mlp_ref, copy_sem.at[0]),
            pltpu.make_async_copy(afull, att_ref, copy_sem.at[1]),
        ]
        for x in outs:
            x.start()
        own_y.wait()
        for o in range(1, nx):
            send(o).wait()
        for x in outs:
            x.wait()


def finish_kernel(
    z, mlp_ref, att_ref, vec_ref, early_ref, late_ref, code_ref, own_ref, dnr_ref, dnown_ref, dt0a_ref, gain_ref,
    out_ref, first_ref, rg_ref, gwu_ref, gwd_ref, gwq_ref, gwo_ref, gbu_ref, *rows,
):
    f = pl.program_id(0)
    fc = gwd_ref.shape[0]
    d = z.d
    gwd_ref[...] = mlp_ref[:fc, :].astype(F32)
    for i in range(fc // d):
        gwu_ref[:, i * d : (i + 1) * d] = mlp_ref[fc + i * d : fc + (i + 1) * d, :].astype(F32)

    @pl.when(f < 3)
    def _():
        gwq_ref[...] = att_ref[...].astype(F32)

    @pl.when(f == 3)
    def _():
        gwo_ref[...] = att_ref[...].astype(F32)

    @pl.when(f == 0)
    def _():
        for i, row in enumerate(rows):
            row[...] = vec_ref[i : i + 1, :]
        gbu_ref[...] = vec_ref[6 : 6 + gbu_ref.shape[0], :]
        hat, rstd = norm_stats(own_ref[...].astype(F32))
        dn = dnr_ref[...].astype(F32) + dnown_ref[...]
        rg_ref[...] = (dt0a_ref[...] + norm_back(hat, rstd, gain_ref[...], dn)).astype(BF16)

    for step in range(MLP_PARTS):

        @pl.when(f == step)
        def _():
            sel_t = one_hot_t(code_ref[...], z.gp * z.w)
            for g in range(z.ng * step // MLP_PARTS, z.ng * (step + 1) // MLP_PARTS):
                rows = z.gp * z.k
                at = z.early // rows
                src, i = (early_ref, g) if g < at else (late_ref, g - at)
                unpack_group(z, g, sel_t, src, out_ref, first_ref, i)


def local(
    patches, regions, send_order, image_windows, attn_gain, attn_shift, w_qkv, w_out, b_out,
    mlp_gain, mlp_shift, w_up, b_up, w_down, b_down, upstream_patches, upstream_regions,
):
    nx, ny = lax.axis_size("gx"), lax.axis_size("gy")
    z = Sizes(patches.shape[0], patches.shape[1], patches.shape[2], nx)
    ff = w_up.shape[1]
    n = z.w * nx * ny
    gx = lax.axis_index("gx")
    dev = gx * ny + lax.axis_index("gy")
    sds = jax.ShapeDtypeStruct

    order = lax.dynamic_slice_in_dim(send_order, dev, 1, 0)[0].reshape(nx, z.k)
    tile = jnp.arange(nx, dtype=jnp.int32)
    order_t = jnp.take(order, (gx - tile) % nx, axis=0)
    place = jnp.arange(z.gp, dtype=jnp.int32) * z.w
    code_x = (order_t[:, None, :] + place[None, :, None]).reshape(-1)
    block = ((gx + tile) % nx)[:, None] * z.k + jnp.arange(z.k, dtype=jnp.int32)[None, :]
    code_e = (block[:, None, :] + place[None, :, None]).reshape(-1)
    order_t = order_t.reshape(-1)
    bounds = jnp.cumsum(image_windows)
    gain, shift = attn_gain[None], attn_shift[None]

    x_t = jnp.transpose(patches, (1, 0, 2))
    e_t = jnp.transpose(upstream_patches, (1, 0, 2))

    bits = n_bits(nx * ny)
    anywhere = pl.BlockSpec(memory_space=pl.ANY)
    vmem = pl.BlockSpec(memory_space=pltpu.VMEM)
    *packed, xp, qkv, regions_all = pl.pallas_call(
        functools.partial(start_kernel, z, nx, ny),
        in_specs=[anywhere, anywhere] + [vmem] * 7,
        out_specs=[vmem] * (z.nb + 1) + [anywhere, vmem],
        out_shape=[sds((z.r, z.d), BF16)] * z.nb + [
            sds((z.nb, z.r, z.d), BF16),
            sds((z.nb, z.r, 3 * z.d), BF16),
            sds((n, z.d), BF16),
        ],
        scratch_shapes=[
            pltpu.VMEM((z.tok, z.w, z.d), BF16),
            pltpu.VMEM((z.tok, z.w, z.d), BF16),
            pltpu.VMEM((z.nb, z.r, 3 * z.d), BF16),
            pltpu.VMEM((z.r, z.d), BF16),
            pltpu.VMEM((n, z.d), BF16),
            pltpu.SemaphoreType.DMA((2, sems_of(routes_of(nx, ny)[0]))),
            pltpu.SemaphoreType.DMA((2,)),
            pltpu.SemaphoreType.DMA((z.nb,)),
        ],
        compiler_params=params(collective_id=0, has_side_effects=True),
        name="start",
    )(x_t, e_t, upstream_regions, code_x[None], code_e[None], gain, shift, w_qkv, regions)

    e_in = [packed[0]]
    for o in range(1, nx):
        e_in.append(lax.ppermute(packed[o], "gx", [(i, (i + o) % nx) for i in range(nx)]))

    kc = 8 * z.w
    nq = HEADS * z.w
    r2, p_r, kv_all, nr_all, q_r, o_r, o_f, n_own = pl.pallas_call(
        functools.partial(region_fwd_kernel, z, kc, ny),
        in_specs=[vmem, vmem, pl.BlockSpec(memory_space=pltpu.SMEM)] + [vmem] * 6,
        out_shape=(
            sds((z.nb, z.kp, z.d), F32),
            sds((n, nq), BF16),
            sds((n, 2 * z.d), BF16),
            sds((n, z.d), BF16),
            sds((z.w, z.d), BF16),
            sds((z.w, z.d), BF16),
            sds((z.w, z.d), F32),
            sds((z.w, z.d), BF16),
        ),
        scratch_shapes=[pltpu.VMEM((n, nq), F32)],
        compiler_params=params(),
        name="region_fwd",
    )(
        regions_all, regions, bounds, order_t[None], gain, shift, w_qkv, w_out, b_out[None],
    )

    def tiled(*shape):
        return pl.BlockSpec((1,) + shape, lambda i: (i,) + (0,) * len(shape))

    def grouped(*shape):
        return pl.BlockSpec((z.k,) + shape, lambda i: (i,) + (0,) * len(shape))

    cols = z.per_group * SEG
    t2, p_w, qw, o_w = pl.pallas_call(
        functools.partial(local_fwd_kernel, z),
        grid=(z.nb,),
        in_specs=[
            tiled(z.r, 3 * z.d), tiled(z.r, z.d), tiled(z.kp, z.d), whole(1, z.d), whole(1, z.d),
            whole(z.d, 3 * z.d), whole(z.d, z.d), whole(1, z.d),
        ],
        out_specs=[
            tiled(z.r, z.d), grouped(z.groups, SEG, cols), grouped(3 * z.groups, SEG, LANES),
            tiled(z.r, z.d),
        ],
        out_shape=(
            sds((z.nb, z.r, z.d), F32),
            sds((z.w, z.groups, SEG, cols), BF16),
            sds((z.w, 3 * z.groups, SEG, LANES), BF16),
            sds((z.nb, z.r, z.d), BF16),
        ),
        scratch_shapes=[
            pltpu.VMEM((3 * z.groups, z.wide, LANES), F32),
            pltpu.VMEM((z.groups, z.wide, LANES), F32),
        ],
        compiler_params=params(),
        name="local_fwd",
    )(qkv, xp, r2, gain, shift, w_qkv, w_out, b_out[None])

    parts = MLP_PARTS
    fc = ff // parts
    total = 2 * ff
    first, other = routes_of(nx, ny)
    stages = 2 * len(first)
    n_sums = mlp_count(nx, ny, total)
    cost = [stage_costs(nx, ny, mlp_route(nx, ny, i, n_sums), total // n_sums * z.d * 2) for i in range(n_sums)]
    n_sems = sum(2 * sems_of(mlp_route(nx, ny, i, n_sums)) for i in range(n_sums))
    head, part_us, tail_us = 11.0, MLP_US / parts, 7.0
    slots = []
    for i in range(parts):
        base = head + part_us * i
        slots += [base + part_us * x for x in (0.0, 0.3, 0.55, 0.8, 0.8, 0.9, 1.0)]
        slots.append(base + part_us + (tail_us if i == parts - 1 else 0.0))
    acts_m, done_m = plan(
        [mlp_ready(i, n_sums, head, part_us) - 0.05 for i in range(n_sums)], [0] * n_sums, stages, cost,
        slots, slots[-1],
    )
    keep = dict(pipeline_mode=pl.Buffered(1))

    def once(*shape):
        return pl.BlockSpec(shape, lambda *_: (0,) * len(shape), **keep)

    y, gt, part_sums, small_m, gbu = pl.pallas_call(
        functools.partial(mlp_kernel, z, nx, ny, acts_m, tuple(done_m)),
        grid=(parts,),
        in_specs=[pl.BlockSpec(memory_space=pl.ANY)] * (1 + z.nb) + [
            once(1, z.d), once(1, z.d), pl.BlockSpec((z.d, fc), lambda f: (0, f)),
            pl.BlockSpec((1, fc), lambda f: (0, f)), pl.BlockSpec((fc, z.d), lambda f: (f, 0)),
            once(1, z.d),
        ],
        out_specs=[
            anywhere, anywhere, anywhere, once(8, z.d),
            pl.BlockSpec((1, 1, fc), lambda f: (f, 0, 0)),
        ],
        out_shape=(
            sds((z.t, z.d), BF16),
            sds((z.t, z.d), BF16),
            sds((total, z.d), BF16),
            sds((8, z.d), F32),
            sds((parts, 1, fc), F32),
        ),
        scratch_shapes=[
            pltpu.VMEM((z.tp, z.d), BF16),
            pltpu.VMEM((z.tp, z.d), BF16),
            pltpu.VMEM((z.d + 16, z.tp), BF16),
            pltpu.VMEM((z.d + 16, z.tp), BF16),
            pltpu.VMEM((z.m, fc), F32),
            pltpu.VMEM((z.m, fc), F32),
            pltpu.VMEM((z.m, fc), F32),
            pltpu.VMEM((z.m, fc), F32),
            pltpu.VMEM((z.tp, fc), BF16),
            pltpu.VMEM((z.tp, fc), BF16),
            pltpu.VMEM((z.t, z.d), F32),
            pltpu.VMEM((z.t, z.d), F32),
            pltpu.VMEM((total, z.d), BF16),
            pltpu.VMEM((total, z.d), BF16),
            pltpu.VMEM((total, z.d), BF16),
            pltpu.SemaphoreType.DMA((2, n_sems)),
            pltpu.SemaphoreType.DMA((24,)),
        ],
        compiler_params=params(collective_id=1, has_side_effects=True),
        name="mlp",
    )(
        t2.reshape(z.t, z.d), *e_in, mlp_gain[None], mlp_shift[None], w_up, b_up[None], w_down,
        b_down[None],
    )
    y, gt = y.reshape(z.nb, z.r, z.d), gt.reshape(z.nb, z.r, z.d)

    head, part_us, tail_us = 2.0, BWD_US / z.nb, 2.0
    slots = []
    for i in range(z.nb):
        base = head + part_us * i
        slots += [base + part_us * x for x in (0.0, 0.3, 0.5, 0.7, 1.0)]
        slots.append(base + part_us + (tail_us if i == z.nb - 1 else 0.0))
    acts_b, done = plan([0.0] * n_sums, done_m, stages, cost, slots, slots[-1], 0.6)
    patch_grad, dt0, gwq, gwo, small_a, part_sums, y_early = pl.pallas_call(
        functools.partial(local_bwd_kernel, z, nx, ny, acts_b, tuple(done_m), tuple(done)),
        grid=(z.nb,),
        in_specs=[
            tiled(z.r, z.d), tiled(z.r, z.d), tiled(z.kp, z.d), tiled(z.r, z.d),
            grouped(z.groups, SEG, cols), grouped(3 * z.groups, SEG, LANES),
            whole(1, z.nb * z.gp * z.k), whole(1, z.d), whole(1, z.d), whole(z.d, 3 * z.d),
            whole(z.d, z.d), anywhere, anywhere,
        ],
        out_specs=[
            once(z.tok, z.w, z.d), tiled(z.kp, z.d), once(z.d, 3 * z.d), once(z.d, z.d),
            once(8, z.d), anywhere, anywhere,
        ],
        out_shape=(
            sds((z.tok, z.w, z.d), BF16),
            sds((z.nb, z.kp, z.d), F32),
            sds((z.d, 3 * z.d), F32),
            sds((z.d, z.d), F32),
            sds((8, z.d), F32),
            sds((total, z.d), BF16),
            sds((z.nb, z.early, z.d), BF16),
        ),
        scratch_shapes=[
            pltpu.VMEM((z.groups, z.wide, LANES), F32),
            pltpu.VMEM((3 * z.groups, z.wide, LANES), F32),
            pltpu.VMEM((z.r, 3 * z.d), BF16),
            pltpu.VMEM((z.nb, z.r, z.d), BF16),
            pltpu.VMEM((total, z.d), BF16),
            pltpu.VMEM((total, z.d), BF16),
            pltpu.VMEM((total, z.d), BF16),
            pltpu.SemaphoreType.DMA((2, n_sems)),
            pltpu.SemaphoreType.DMA((2, nx * z.nb)),
            pltpu.SemaphoreType.DMA((n_sums,)),
        ],
        compiler_params=params(collective_id=2, has_side_effects=True),
        name="local_bwd",
    )(gt, xp, r2, o_w, p_w, qw, code_x[None], gain, shift, w_qkv, w_out, part_sums, y)

    def keys(*shape):
        return pl.BlockSpec((kc,) + shape, lambda i: (i,) + (0,) * len(shape))

    mlp_total, att_total, vec, dnr, dt0a, dn_own, y_late = pl.pallas_call(
        functools.partial(region_bwd_kernel, z, nx, ny, tuple(done)),
        grid=(n // kc,),
        in_specs=[
            once(z.nb, z.kp, z.d), keys(z.d), once(z.w, z.d), once(z.w, z.d), keys(nq), keys(2 * z.d),
            keys(z.d), once(z.w, z.d), once(z.w, z.d), once(z.w, z.d), once(1, z.w), once(1, z.d),
            once(z.d, 3 * z.d), once(z.d, z.d), once(z.d, 3 * z.d), once(z.d, z.d), once(8, z.d),
            once(8, z.d), once(parts, 1, fc), anywhere, anywhere,
        ],
        out_specs=[
            anywhere, anywhere, once(16, z.d), once(z.w, z.d), once(z.w, z.d), once(z.w, z.d), anywhere,
        ],
        out_shape=(
            sds((total, z.d), BF16),
            sds((4 * z.d, z.d), BF16),
            sds((16, z.d), F32),
            sds((z.w, z.d), BF16),
            sds((z.w, z.d), F32),
            sds((z.w, z.d), F32),
            sds((z.nb, z.r - z.early, z.d), BF16),
        ),
        scratch_shapes=[
            pltpu.VMEM((nq, z.d), BF16),
            pltpu.VMEM((nq, z.d), BF16),
            pltpu.VMEM((8, nq), F32),
            pltpu.VMEM((nq, z.d), F32),
            pltpu.VMEM((z.d, 3 * z.d), F32),
            pltpu.VMEM((8, z.d), F32),
            pltpu.VMEM((total, z.d), BF16),
            pltpu.VMEM((total, z.d), BF16),
            pltpu.VMEM((total, z.d), BF16),
            pltpu.VMEM((4 * z.d, z.d), BF16),
            pltpu.VMEM((4 * z.d, z.d), BF16),
            pltpu.VMEM((4 * z.d, z.d), BF16),
            pltpu.VMEM((2 * bits + 1, 16, z.d), F32),
            pltpu.VMEM((n, z.d), BF16),
            pltpu.VMEM((n, z.d), BF16),
            pltpu.SemaphoreType.DMA((2, n_sems)),
            pltpu.SemaphoreType.DMA((2, bits + 9 * sems_of(first))),
            pltpu.SemaphoreType.DMA((2, nx)),
            pltpu.SemaphoreType.DMA((max(n_sums, 2),)),
        ],
        compiler_params=params(collective_id=3, has_side_effects=True),
        name="region_bwd",
    )(
        dt0, regions_all, o_r, o_f, p_r, kv_all, nr_all, q_r, n_own, regions, order_t[None], gain, w_qkv,
        w_out, gwq, gwo, small_a, small_m, gbu, part_sums, y,
    )

    out_p, out_r, region_grad, gwu, gwd, gwq, gwo, gbu, *rows = pl.pallas_call(
        functools.partial(finish_kernel, z),
        grid=(parts,),
        in_specs=[
            pl.BlockSpec((2 * fc, z.d), lambda f: (f, 0)), pl.BlockSpec((z.d, z.d), lambda f: (f, 0)),
            once(16, z.d), once(z.nb, z.early, z.d), once(z.nb, z.r - z.early, z.d), once(1, z.nb * z.gp * z.k), once(z.w, z.d),
            once(z.w, z.d), once(z.w, z.d), once(z.w, z.d), once(1, z.d),
        ],
        out_specs=[
            once(z.tok, z.w, z.d), once(z.w, z.d), once(z.w, z.d),
            pl.BlockSpec((z.d, fc), lambda f: (0, f)), pl.BlockSpec((fc, z.d), lambda f: (f, 0)),
            pl.BlockSpec((z.d, z.d), lambda f: (0, jnp.minimum(f, 2))), once(z.d, z.d),
            once(ff // z.d, z.d),
        ] + [once(1, z.d)] * 6,
        out_shape=[
            sds((z.tok, z.w, z.d), BF16), sds((z.w, z.d), BF16), sds((z.w, z.d), BF16),
            sds((z.d, ff), F32), sds((ff, z.d), F32), sds((z.d, 3 * z.d), F32), sds((z.d, z.d), F32),
            sds((ff // z.d, z.d), F32),
        ] + [sds((1, z.d), F32)] * 6,
        compiler_params=params(),
        name="finish",
    )(mlp_total, att_total, vec, y_early, y_late, code_e[None], regions, dnr, dn_own, dt0a, gain)
    rows = [x[0] for x in rows]
    return (
        jnp.transpose(out_p, (1, 0, 2)),
        out_r,
        jnp.transpose(patch_grad, (1, 0, 2)),
        region_grad,
        rows[0],
        rows[1],
        gwq,
        gwo,
        rows[2],
        rows[3],
        rows[4],
        gwu,
        gbu.reshape(ff),
        gwd,
        rows[5],
    )


def solution(mesh):
    split = ("gx", "gy")
    rows3, rows2, full = P(split, None, None), P(split, None), P()
    in_specs = (rows3, rows2) + (full,) * 13 + (rows3, rows2)
    out_specs = (rows3, rows2, rows3, rows2) + (full,) * 11
    return jax.shard_map(local, mesh=mesh, in_specs=in_specs, out_specs=out_specs, check_vma=False)
```

```python
import functools
import math

import jax
import jax.numpy as jnp
from jax import lax
from jax.experimental import pallas as pl
from jax.experimental.pallas import tpu as pltpu
from jax.sharding import PartitionSpec as P

HEADS = 16
EPS = 1e-05
F32 = jnp.float32
BF16 = jnp.bfloat16
LOG2E = 1.4426950408889634
VMEM_LIMIT = 60 * 1024 * 1024
HIGH = lax.Precision.HIGHEST
LANES = 128
MLP_PARTS = 4
BWD_TICKS = 3
MLP_US = 60.0
BWD_US = 36.0
LATENCY_US = 3.0
SLACK_US = 2.5
SEG = 64


def mm(a, b):
    return lax.dot_general(a, b, (((1,), (0,)), ((), ())), preferred_element_type=F32)


def mm_nt(a, b):
    return lax.dot_general(a, b, (((1,), (1,)), ((), ())), preferred_element_type=F32)


def mm_tn(a, b):
    return lax.dot_general(a, b, (((0,), (0,)), ((), ())), preferred_element_type=F32)


def norm_stats(v):
    average = jnp.mean(v, axis=-1, keepdims=True)
    centered = v - average
    variance = jnp.mean(centered * centered, axis=-1, keepdims=True)
    rstd = lax.rsqrt(variance + EPS)
    return centered * rstd, rstd


def norm_back(hat, rstd, gain, dn):
    dhat = dn * gain
    m1 = jnp.mean(dhat, axis=-1, keepdims=True)
    m2 = jnp.mean(dhat * hat, axis=-1, keepdims=True)
    return rstd * (dhat - m1 - hat * m2)


def colsum(v):
    return jnp.sum(v, axis=0, keepdims=True)


def gelu_both(u):
    a = jnp.abs(u)
    d = 1.0 + (0.3275911 * 0.7071067811865476) * a
    r = pl.reciprocal(d, approx=True)
    t = r * (2.0 - d * r)
    e = jnp.exp2((u * u) * (-0.5 * LOG2E))
    poly = t * (
        0.127414796
        + t * (-0.142248368 + t * (0.7107068705 + t * (-0.7265760135 + t * 0.5307027145)))
    )
    tail = poly * e
    cdf = jnp.where(u >= 0.0, 1.0 - tail, tail)
    return u * cdf, cdf + u * (e * 0.3989422804014327)


def head_masks(rows, head_dim):
    lane = lax.broadcasted_iota(jnp.int32, (rows, LANES), 1)
    return [(lane // head_dim) == h for h in range(LANES // head_dim)]


def spread(v, masks):
    zero = jnp.zeros_like(v)
    return jnp.concatenate([jnp.where(m, v, zero) for m in masks], axis=0)


def unspread(full, rows, stride, masks):
    out = full[(len(masks) - 1) * stride : (len(masks) - 1) * stride + rows]
    for h in range(len(masks) - 2, -1, -1):
        out = jnp.where(masks[h][:rows], full[h * stride : h * stride + rows], out)
    return out


def one_hot(code_col, count):
    rows = code_col.shape[0]
    return (lax.broadcasted_iota(jnp.int32, (rows, count), 1) == code_col).astype(F32).astype(BF16)


def one_hot_t(code_row, count):
    rows = code_row.shape[1]
    return (lax.broadcasted_iota(jnp.int32, (count, rows), 0) == code_row).astype(F32).astype(BF16)


def whole(*shape):
    return pl.BlockSpec(shape, lambda *_: (0,) * len(shape))


class Sizes:
    def __init__(self, per_dev, patch_tokens, width, count_gx):
        self.w = per_dev
        self.tok = patch_tokens
        self.d = width
        self.nb = count_gx
        self.k = per_dev // count_gx
        step = 16 // math.gcd(16, self.k)
        self.pos = -(-(patch_tokens + 1) // step) * step
        self.gp = step
        while (self.gp * self.k) % 16:
            self.gp *= 2
        self.ng = self.pos // self.gp
        self.early = self.ng // 2 * self.gp * self.k
        self.r = self.pos * self.k
        self.wide = 56 * self.k
        self.hd = width // HEADS
        self.groups = width // LANES
        self.per_group = LANES // self.hd
        self.chunk = self.r // 3 if self.r % 48 == 0 else self.r
        self.kp = -(-self.k // 16) * 16
        self.side = max(j for j in range(1, 5) if self.k % j == 0)
        self.t = self.nb * self.r
        self.tp = -(-self.t // 512) * 512
        self.m = max(m for m in range(16, 449, 16) if self.t % (2 * m) == 0)


def params(**kw):
    return pltpu.CompilerParams(vmem_limit_bytes=VMEM_LIMIT, **kw)


def pack_group(z, g, sel_t, x_ref, first_ref, outs):
    pieces = []
    for p in range(g * z.gp, (g + 1) * z.gp):
        if p == 0:
            pieces.append(jnp.zeros((z.w, z.d), BF16) if first_ref is None else first_ref[...])
        elif p <= z.tok:
            pieces.append(x_ref[p - 1])
        else:
            pieces.append(jnp.zeros((z.w, z.d), BF16))
    got = mm_tn(sel_t, jnp.concatenate(pieces, axis=0)).astype(BF16)
    rows = z.gp * z.k
    for c in range(z.nb):
        outs[c][g * rows : (g + 1) * rows, :] = got[c * rows : (c + 1) * rows]


def unpack_group(z, g, sel_t, packed_ref, out_ref, first_ref, at=None):
    rows = z.gp * z.k
    here = slice((g if at is None else at) * rows, ((g if at is None else at) + 1) * rows)
    src = jnp.concatenate([packed_ref[c, here, :] for c in range(z.nb)], axis=0)
    got = mm(sel_t, src).astype(BF16)
    for i in range(z.gp):
        p = g * z.gp + i
        piece = got[i * z.w : (i + 1) * z.w]
        if p == 0:
            if first_ref is not None:
                first_ref[...] = piece
        elif p <= z.tok:
            out_ref[p - 1] = piece


def start_kernel(
    z, nx, ny, x_ref, e_ref, first_ref, codex_ref, codee_ref, gain_ref, shift_ref, w_ref, own_ref, *refs
):
    packed, refs = refs[: z.nb], refs[z.nb :]
    xp_ref, qkv_ref, all_ref, xs, es, qs, nt, buf, sems, load_sems, out_sems = refs
    loads = [
        pltpu.make_async_copy(src, dst, load_sems.at[i])
        for i, (src, dst) in enumerate(((e_ref, es), (x_ref, xs)))
    ]
    for x in loads:
        x.start()
    mesh = Mesh2(nx, ny)
    rounds = routes_of(nx, ny)[0]
    gather = Gather(mesh, buf, z.w, rounds, sems, 0)
    mesh.barrier(rounds)
    buf[pl.ds(*gather.held(0)), :] = own_ref[...]
    gather.start(0)

    def pack(src, code_ref, first, outs):
        sel_t = one_hot_t(code_ref[...], z.gp * z.w)
        for g in range(z.ng):
            pack_group(z, g, sel_t, src, first, outs)

    def out(c):
        return pltpu.make_async_copy(qs.at[c], qkv_ref.at[c], out_sems.at[c])

    def project(c, _):
        hat, _ = norm_stats(xp_ref[c].astype(F32))
        nt[...] = (hat * gain_ref[...] + shift_ref[...]).astype(BF16)
        qs[c] = mm(nt[...], w_ref[...]).astype(BF16)
        out(c).start()
        return 0

    stages = gather.stages
    loads[0].wait()
    pack(es, codee_ref, first_ref, packed)
    loads[1].wait()
    pack(xs, codex_ref, None, [xp_ref.at[c] for c in range(z.nb)])
    for s in range(1, stages + 1):
        gather.finish(s - 1)
        if s < stages:
            gather.start(s)
            lax.fori_loop(z.nb * (s - 1) // (stages - 1), z.nb * s // (stages - 1), project, 0)
    n = nx * ny
    order = flat(rounds)
    for dev in range(n):
        p = place_of(order, nx, ny, dev)
        all_ref[dev * z.w : (dev + 1) * z.w, :] = buf[p * z.w : (p + 1) * z.w, :]
    for c in range(z.nb):
        out(c).wait()


def region_fwd_kernel(
    z, kc, ny, all_ref, own_ref, bounds_ref, ord_ref, gain_ref, shift_ref, w_ref, wo_ref, bo_ref,
    r2_ref, p_ref, kv_ref, nr_ref, q_ref, o_ref, of_ref, nown_ref, s_ref,
):
    n = all_ref.shape[0]
    nq = HEADS * z.w
    hat, _ = norm_stats(own_ref[...].astype(F32))
    nown = (hat * gain_ref[...] + shift_ref[...]).astype(BF16)
    nown_ref[...] = nown
    q = mm(nown, w_ref[:, : z.d]).astype(BF16)
    q_ref[...] = q
    lane = lax.broadcasted_iota(jnp.int32, (z.w, z.d), 1) // z.hd
    zero = jnp.zeros_like(q)
    qbd = jnp.concatenate([jnp.where(lane == h, q, zero) for h in range(HEADS)], axis=0)
    scale = z.hd ** (-0.5) * LOG2E
    dev = lax.axis_index("gx") * ny + lax.axis_index("gy")
    window = dev * z.w + lax.broadcasted_iota(jnp.int32, (1, nq), 1) % z.w

    def image(j, span):
        low, high = span
        bound = bounds_ref[j]
        return jnp.where(bound <= window, bound, low), jnp.where(bound > window, jnp.minimum(high, bound), high)

    low, high = lax.fori_loop(
        0, bounds_ref.shape[0], image,
        (jnp.zeros((1, nq), jnp.int32), jnp.full((1, nq), n, jnp.int32)),
    )
    key = lax.broadcasted_iota(jnp.int32, (kc, nq), 0)

    def reach(j, span):
        bound = bounds_ref[j]
        return (
            jnp.where(bound <= dev * z.w, bound, span[0]),
            jnp.where(bound > dev * z.w + z.w - 1, jnp.minimum(span[1], bound), span[1]),
        )

    begin, end = lax.fori_loop(0, bounds_ref.shape[0], reach, (jnp.int32(0), jnp.int32(n)))
    begin, end = begin // kc, (end + kc - 1) // kc

    def blank(i, _):
        rows = pl.ds(pl.multiple_of(i * kc, kc), kc)
        nr_ref[rows, :] = jnp.zeros((kc, z.d), BF16)
        kv_ref[rows, :] = jnp.zeros((kc, 2 * z.d), BF16)
        p_ref[rows, :] = jnp.zeros((kc, nq), BF16)
        return 0

    lax.fori_loop(0, begin, blank, 0)
    lax.fori_loop(end, n // kc, blank, 0)

    def scores(i, top):
        rows = pl.ds(pl.multiple_of(i * kc, kc), kc)
        hat, _ = norm_stats(all_ref[rows, :].astype(F32))
        nr = (hat * gain_ref[...] + shift_ref[...]).astype(BF16)
        nr_ref[rows, :] = nr
        kv = mm(nr, w_ref[:, z.d :]).astype(BF16)
        kv_ref[rows, :] = kv
        s = mm_nt(kv[:, : z.d], qbd) * scale
        s = jnp.where((key >= low - i * kc) & (key < high - i * kc), s, -1e30)
        s_ref[rows, :] = s
        return jnp.maximum(top, jnp.max(s, axis=0, keepdims=True))

    top = lax.fori_loop(begin, end, scores, jnp.full((1, nq), -1e30, F32))

    def weigh(i, total):
        rows = pl.ds(pl.multiple_of(i * kc, kc), kc)
        p = jnp.exp2(s_ref[rows, :] - top)
        s_ref[rows, :] = p
        return total + jnp.sum(p, axis=0, keepdims=True)

    total = lax.fori_loop(begin, end, weigh, jnp.zeros((1, nq), F32))
    inverse = 1.0 / total

    def attend(i, acc):
        rows = pl.ds(pl.multiple_of(i * kc, kc), kc)
        p = (s_ref[rows, :] * inverse).astype(BF16)
        p_ref[rows, :] = p
        return acc + mm_tn(p, kv_ref[rows, z.d :])

    full = lax.fori_loop(begin, end, attend, jnp.zeros((nq, z.d), F32))
    o = full[(HEADS - 1) * z.w :]
    for h in range(HEADS - 2, -1, -1):
        o = jnp.where(lane == h, full[h * z.w : (h + 1) * z.w], o)
    of_ref[...] = o
    o = o.astype(BF16)
    o_ref[...] = o
    r2 = own_ref[...].astype(F32) + mm(o, wo_ref[...]) + bo_ref[...]
    sel_t = one_hot_t(ord_ref[...], z.w).astype(F32)
    r2 = lax.dot_general(
        sel_t, r2, (((0,), (0,)), ((), ())), precision=HIGH, preferred_element_type=F32
    )
    for c in range(z.nb):
        r2_ref[c, : z.k, :] = r2[c * z.k : (c + 1) * z.k]
        r2_ref[c, z.k :, :] = jnp.zeros((z.kp - z.k, z.d), F32)


def local_fwd_kernel(
    z, qkv_ref, xp_ref, r2_ref, gain_ref, shift_ref, w_ref, wo_ref, bo_ref,
    t2_ref, p_ref, qw_ref, o_ref, qs, os,
):
    tiles = 3 * z.groups
    for j in range(tiles):
        qs[j, : z.r, :] = qkv_ref[0, :, j * LANES : (j + 1) * LANES].astype(F32)
        if z.wide > z.r:
            qs[j, z.r :, :] = jnp.zeros((z.wide - z.r, LANES), F32)
    hat, _ = norm_stats(r2_ref[0])
    nt = (hat * gain_ref[...] + shift_ref[...]).astype(BF16)
    reg = mm(nt, w_ref[...]).astype(BF16).astype(F32)
    for j in range(tiles):
        qs[j, : z.k, :] = reg[: z.k, j * LANES : (j + 1) * LANES]
    masks = head_masks(SEG, z.hd)
    pad = jnp.zeros((SEG - 56, LANES), F32)
    valid = lax.broadcasted_iota(jnp.int32, (56, z.per_group * SEG), 0) < z.tok + 1
    scale = z.hd ** (-0.5) * LOG2E
    tail = jnp.zeros((SEG - 56, z.per_group * SEG), F32)

    def windows(i, _):
        jobs = [(i * z.side + j, g) for j in range(z.side) for g in range(z.groups)]

        def load(w, j):
            rows = qs[j, pl.ds(w, 56, stride=z.k), :]
            got = jnp.concatenate([rows, pad], axis=0).astype(BF16)
            qw_ref[w, j] = got
            return got

        q = [load(w, g) for w, g in jobs]
        k = [load(w, z.groups + g) for w, g in jobs]
        v = [load(w, 2 * z.groups + g) for w, g in jobs]
        s = [mm_nt(kk, spread(qq, masks))[:56] for qq, kk in zip(q, k)]
        s = [jnp.where(valid, x, -1e30) for x in s]
        p = [jnp.exp2((x - jnp.max(x, axis=0, keepdims=True)) * scale) for x in s]
        p = [x * (1.0 / jnp.sum(x, axis=0, keepdims=True)) for x in p]
        p = [jnp.concatenate([x, tail], axis=0).astype(BF16) for x in p]
        for (w, g), x in zip(jobs, p):
            p_ref[w, g] = x
        full = [mm_tn(x, vv) for x, vv in zip(p, v)]
        for (w, g), x in zip(jobs, full):
            os[g, pl.ds(w, 56, stride=z.k), :] = unspread(x, 56, SEG, masks)
        return 0

    lax.fori_loop(0, z.k // z.side, windows, 0)
    for i in range(z.r // z.chunk):
        rows = slice(i * z.chunk, (i + 1) * z.chunk)
        o = jnp.concatenate([os[g, rows, :] for g in range(z.groups)], axis=1).astype(BF16)
        o_ref[0, rows, :] = o
        t2_ref[0, rows, :] = xp_ref[0, rows, :].astype(F32) + mm(o, wo_ref[...]) + bo_ref[...]
    t2_ref[0, : z.k, :] = t2_ref[0, : z.k, :] + r2_ref[0, : z.k, :]


def tiles_dot(lhs, w, acc, transposed=False):
    side = 256
    for k in range(w.shape[0] // side):
        for j in range(len(acc)):
            ks, js = slice(k * side, (k + 1) * side), slice(j * side, (j + 1) * side)
            pltpu.matmul_push_rhs(w[js, ks] if transposed else w[ks, js], k % 2, j, transpose=transposed)
            pltpu.matmul_acc_lhs(acc[j], lhs(k), load_staged_rhs=k % 2)


def mlp_kernel(z, nx, ny, acts, done, *refs):
    (t2_ref, *e_refs), refs = refs[: 1 + z.nb], refs[1 + z.nb :]
    (
        gain_ref, shift_ref, wu_ref, bu_ref, wd_ref, bd_ref,
        y_ref, gt_ref, buf_ref, small_ref, gbu_ref,
        n2, e, n2_t, e_t, h0, h1, d0, d1, active, dh, yacc, dn, buf, recv, full, sems, copy_sem,
    ) = refs
    f = pl.program_id(0)
    parts = pl.num_programs(0)
    mesh = Mesh2(nx, ny)
    sums = mlp_sums(mesh, z, buf, recv, full, sems)
    per = len(acts) // MLP_PARTS
    sub, side = math.gcd(z.m, 32), 256
    fc = wu_ref.shape[1]
    m = h0.shape[0]
    chunks = z.t // m

    def rows_of(c):
        return slice(c * m, (c + 1) * m)

    def tick(p, also=True):
        for step in range(len(acts) // per):
            if acts[step * per + p]:

                @pl.when((f == step) & also)
                def _():
                    act(sums, acts[step * per + p])

    @pl.when(f == 0)
    def _():
        fetch = [
            pltpu.make_async_copy(e_refs[c], e.at[c * z.r : (c + 1) * z.r, :], copy_sem.at[c])
            for c in range(z.nb)
        ]
        begin = [
            pltpu.make_async_copy(t2_ref.at[rows_of(c), :], yacc.at[rows_of(c), :], copy_sem.at[8 + c])
            for c in range(chunks)
        ]
        for x in begin + fetch:
            x.start()
        mesh.barrier(all_rounds(nx, ny))

        def prepare(i, _):
            rows = pl.ds(pl.multiple_of(i * sub, 16), sub)
            hat, _ = norm_stats(yacc[rows, :])
            n2[rows, :] = (hat * gain_ref[...] + shift_ref[...]).astype(BF16)
            dn[rows, :] = jnp.zeros((sub, z.d), F32)
            return 0

        for x in begin:
            x.wait()
        lax.fori_loop(0, z.t // sub, prepare, 0, unroll=6)
        for x in fetch:
            x.wait()
        if z.tp > z.t:
            for x in (n2, e, active, dh):
                x[z.t :, :] = jnp.zeros((z.tp - z.t, x.shape[1]), BF16)

        def turn(i, _):
            span = pl.ds(pl.multiple_of(i * side, side), side)
            n2_t[: z.d, span] = n2[span, :].T
            e_t[: z.d, span] = e[span, :].T
            n2_t[z.d :, span] = jnp.ones((16, side), BF16)
            e_t[z.d :, span] = jnp.zeros((16, side), BF16)
            return 0

        lax.fori_loop(0, z.tp // side, turn, 0)

    def result(c):
        rows = pl.ds(pl.multiple_of(c * m, 16), m)
        return (
            pltpu.make_async_copy(n2.at[rows], y_ref.at[rows], copy_sem.at[8 + 2 * c]),
            pltpu.make_async_copy(e.at[rows], gt_ref.at[rows], copy_sem.at[9 + 2 * c]),
        )

    slots = (h0, h1)

    def again(c, slot):
        rows = pl.ds(pl.multiple_of(c * m, 16), m)
        return pltpu.make_async_copy(t2_ref.at[rows], slots[slot], copy_sem.at[slot])

    tick(0)
    bias = bu_ref[...]

    def stream(*accs):
        one, two = accs[:2], accs[2:]
        h, d = (h0, h1), (d0, d1)

        def rows(c):
            return pl.ds(pl.multiple_of(c * m, 16), m)

        def up(c, slot):
            tiles_dot(lambda k: n2[rows(c), k * side : (k + 1) * side], wu_ref, one)
            for j in range(2):
                h[slot][:, j * side : (j + 1) * side] = pltpu.matmul_pop(one[j])
            tiles_dot(lambda k: e[rows(c), k * side : (k + 1) * side], wd_ref, two, True)
            for j in range(2):
                d[slot][:, j * side : (j + 1) * side] = pltpu.matmul_pop(two[j])

        def down(c):
            tiles_dot(lambda k: active[rows(c), k * side : (k + 1) * side], wd_ref, one)
            for j in range(2):
                yacc[rows(c), j * side : (j + 1) * side] += pltpu.matmul_pop(one[j])
            tiles_dot(lambda k: dh[rows(c), k * side : (k + 1) * side], wu_ref, two, True)
            for j in range(2):
                dn[rows(c), j * side : (j + 1) * side] += pltpu.matmul_pop(two[j])

        def middle(c, slot):
            for i in range(m // 16):
                r, o = slice(i * 16, (i + 1) * 16), pl.ds(pl.multiple_of(c * m + i * 16, 16), 16)
                value, slope = gelu_both(h[slot][r, :] + bias)
                active[o, :] = value.astype(BF16)
                dh[o, :] = (d[slot][r, :] * slope).astype(BF16)

        def pair(i, _):
            for slot in range(2):
                c = 2 * i + slot
                up(jnp.minimum(c + 1, chunks - 1), 1 - slot)
                middle(c, slot)
                down(c)
            for p in range(1, 4):
                tick(p, i + 1 == chunks // 2 * p // 3)
            return 0

        up(0, 0)
        lax.fori_loop(0, chunks // 2, pair, 0)

    pl.run_scoped(stream, *[pltpu.ACC(mxu_id=i)((m, side), F32) for i in (0, 1, 0, 1)])
    @pl.when(f == parts - 1)
    def _():
        for slot in range(2):
            again(slot, slot).start()

    tick(4)
    here = pl.multiple_of(f * (2 * fc), 16)

    def gradients(acc0, acc1):
        acc = (acc0, acc1)
        halves = [slice(j * side, (j + 1) * side) for j in range(2)]

        def over_tokens(left, right):
            def two(i, _):
                for k in range(2):
                    span = pl.ds(pl.multiple_of((2 * i + k) * side, side), side)
                    for j in range(2):
                        pltpu.matmul_push_rhs(right[span, halves[j]], k, j)
                        pltpu.matmul_acc_lhs(acc[j], left[:, span], load_staged_rhs=k)
                return 0

            lax.fori_loop(0, z.tp // (2 * side), two, 0)

        over_tokens(e_t, active)
        for j in range(2):
            rows = pl.ds(pl.multiple_of(here + j * side, 16), side)
            buf[rows, :] = pltpu.matmul_pop(acc[j])[: z.d].T.astype(BF16)
        tick(5)
        over_tokens(n2_t, dh)
        for j in range(2):
            got = pltpu.matmul_pop(acc[j])
            buf[pl.ds(pl.multiple_of(here + fc, 16), z.d), halves[j]] = got[: z.d].astype(BF16)
            gbu_ref[0, :, halves[j]] = got[z.d : z.d + 1]

    pl.run_scoped(
        gradients, pltpu.ACC(mxu_id=0)((z.d + 16, side), F32), pltpu.ACC(mxu_id=1)((z.d + 16, side), F32)
    )
    tick(6)

    @pl.when(f == parts - 1)
    def _():
        def pair(i, sums):
            for slot in range(2):
                c = 2 * i + slot
                again(c, slot).wait()

                def close(j, sums):
                    here = pl.ds(pl.multiple_of(j * sub, 16), sub)
                    rows = pl.ds(pl.multiple_of(c * m + j * sub, 16), sub)
                    up = e[rows, :].astype(F32)
                    n2[rows, :] = (yacc[rows, :] + bd_ref[...]).astype(BF16)
                    hat, rstd = norm_stats(slots[slot][here, :])
                    d = dn[rows, :]
                    gt = (up + norm_back(hat, rstd, gain_ref[...], d)).astype(BF16)
                    e[rows, :] = gt
                    return (
                        sums[0] + colsum(d * hat), sums[1] + colsum(d), sums[2] + colsum(up),
                        sums[3] + colsum(gt.astype(F32)),
                    )

                sums = lax.fori_loop(0, m // sub, close, sums, unroll=13)
                for x in result(c):
                    x.start()

                @pl.when(c + 2 < chunks)
                def _():
                    again(c + 2, slot).start()

            return sums

        got = lax.fori_loop(0, chunks // 2, pair, (jnp.zeros((1, z.d), F32),) * 4)
        small_ref[...] = jnp.zeros_like(small_ref)
        for i in range(4):
            small_ref[i : i + 1, :] = got[i]

    tick(7)

    @pl.when(f == parts - 1)
    def _():
        out = carry(sums, done, buf_ref, copy_sem, True)
        for x in out:
            x.start()
        for x in out:
            x.wait()
        for c in range(chunks):
            for x in result(c):
                x.wait()


def mlp_count(nx, ny, rows):
    count = 2 * MLP_PARTS
    while rows // count % (16 * nx * ny):
        count //= 2
    return count


def mlp_ready(i, count, head, part_us):
    unit = (i + 1) * (2 * MLP_PARTS // count) - 1
    return head + part_us * (unit // 2 + (0.9 if unit % 2 == 0 else 1.0))


def mlp_sums(mesh, z, buf, recv, full, sems):
    nx, ny = mesh.n["gx"], mesh.n["gy"]
    count = mlp_count(nx, ny, buf.shape[0])
    rows = buf.shape[0] // count
    sem0, out = 0, []
    for i in range(count):
        rounds = mlp_route(nx, ny, i, count)
        out.append(Sum(mesh, buf, i * rows, rows, rounds, recv, i * rows, sems, sem0, full))
        sem0 += 2 * sems_of(rounds)
    return out


def mlp_route(nx, ny, i, count):
    first, other = routes_of(nx, ny)
    if i == count - 1:
        return other
    return long_first(first) if i in (3, 6) else first


def long_first(rounds):
    return rounds[:1] + rounds[-1:] + rounds[1:-1]


def local_bwd_kernel(
    z, nx, ny, acts, before, done, gt_ref, xp_ref, r2_ref, o_ref, p_ref, qw_ref, code_ref, gain_ref, shift_ref, w_ref,
    wo_ref, part_ref, y_ref,
    pg_ref, dt0_ref, gwq_ref, gwo_ref, small_ref, buf_ref, yin_ref,
    ds_, dq_, dqkv, dtp, buf, recv, full, sems, ysems, copy_sem,
):
    step = pl.program_id(0)
    steps = pl.num_programs(0)
    mesh = Mesh2(nx, ny)
    sums = mlp_sums(mesh, z, buf, recv, full, sems)
    per = len(acts) // z.nb

    def tick(p, also=True):
        for i in range(z.nb):
            if acts[i * per + p]:

                @pl.when((step == i) & also)
                def _():
                    act(sums, acts[i * per + p])

    units = z.early // 16

    def send(o, i):
        rows = pl.ds(units * i // z.nb * 16, (units * (i + 1) // z.nb - units * i // z.nb) * 16)
        return pltpu.make_async_remote_copy(
            src_ref=y_ref.at[o, rows], dst_ref=yin_ref.at[o, rows], send_sem=ysems.at[0, o * z.nb + i],
            recv_sem=ysems.at[1, o * z.nb + i], device_id=mesh.beside(nx - o),
            device_id_type=pl.DeviceIdType.MESH,
        )

    own_y = pltpu.make_async_copy(y_ref.at[0, : z.early], yin_ref.at[0], ysems.at[0, 0])

    @pl.when(step == 0)
    def _():
        gwq_ref[...] = jnp.zeros_like(gwq_ref)
        gwo_ref[...] = jnp.zeros_like(gwo_ref)
        small_ref[...] = jnp.zeros_like(small_ref)
        fetch = carry(sums, before, part_ref, copy_sem, False)
        for x in fetch:
            x.start()
        mesh.barrier(all_rounds(nx, ny), row=True)
        own_y.start()
        for x in fetch:
            x.wait()

    tick(0)
    for i in range(z.nb):

        @pl.when(step == i)
        def _(i=i):
            for o in range(1, nx):
                send(o, i).start()

    gt = gt_ref[0]
    dot = mm_nt(gt, wo_ref[...])
    for j in range(z.groups):
        ds_[j, : z.r, :] = dot[:, j * LANES : (j + 1) * LANES]
        if z.wide > z.r:
            ds_[j, z.r :, :] = jnp.zeros((z.wide - z.r, LANES), F32)
    gwo_ref[...] += mm_tn(o_ref[0], gt)
    masks = head_masks(SEG, z.hd)
    pad = jnp.zeros((SEG - 56, LANES), F32)
    scale = z.hd ** (-0.5)

    def windows(i, _):
        jobs = [(i * z.side + j, g) for j in range(z.side) for g in range(z.groups)]
        do = [
            jnp.concatenate([ds_[g, pl.ds(w, 56, stride=z.k), :], pad], axis=0).astype(BF16)
            for w, g in jobs
        ]
        dobd = [spread(x, masks) for x in do]
        dp = [mm_nt(qw_ref[w, 2 * z.groups + g], x) for (w, g), x in zip(jobs, dobd)]
        dv = [mm(p_ref[w, g], x) for (w, g), x in zip(jobs, dobd)]
        for (w, g), x in zip(jobs, dv):
            dq_[2 * z.groups + g, pl.ds(w, 56, stride=z.k), :] = x[:56]
        ds = []
        for (w, g), x in zip(jobs, dp):
            pf = p_ref[w, g].astype(F32)
            t = pf * x
            ds.append((t - pf * jnp.sum(t, axis=0, keepdims=True)).astype(BF16))
        dk = [mm(x, spread(qw_ref[w, g], masks)) for (w, g), x in zip(jobs, ds)]
        for (w, g), x in zip(jobs, dk):
            dq_[z.groups + g, pl.ds(w, 56, stride=z.k), :] = x[:56] * scale
        full = [mm_tn(x, qw_ref[w, z.groups + g]) for (w, g), x in zip(jobs, ds)]
        for (w, g), x in zip(jobs, full):
            dq_[g, pl.ds(w, 56, stride=z.k), :] = unspread(x, 56, SEG, masks) * scale
        return 0

    rounds = z.k // z.side

    def turn(i, _):
        windows(i, 0)
        for p in range(1, 1 + BWD_TICKS):
            tick(p, i + 1 == max(1, rounds * p // BWD_TICKS))
        return 0

    lax.fori_loop(0, rounds, turn, 0)
    for j in range(3 * z.groups):
        dqkv[:, j * LANES : (j + 1) * LANES] = dq_[j, : z.r, :].astype(BF16)
    dn = mm_nt(dqkv[...], w_ref[...])
    t = xp_ref[0].astype(F32)
    t = jnp.concatenate([r2_ref[0, : z.k, :], t[z.k :]], axis=0)
    hat, rstd = norm_stats(t)
    nt = (hat * gain_ref[...] + shift_ref[...]).astype(BF16)
    gwq_ref[...] += mm_tn(nt, dqkv[...])
    dt = gt.astype(F32) + norm_back(hat, rstd, gain_ref[...], dn)
    dt0_ref[0, : z.k, :] = dt[: z.k]
    dt0_ref[0, z.k :, :] = jnp.zeros((z.kp - z.k, z.d), F32)
    dtp[step] = dt.astype(BF16)
    small_ref[0:1, :] += colsum(dn * hat)
    small_ref[1:2, :] += colsum(dn)
    tick(1 + BWD_TICKS)

    @pl.when(step == steps - 1)
    def _():
        sel_t = one_hot_t(code_ref[...], z.gp * z.w)
        for g in range(z.ng):
            unpack_group(z, g, sel_t, dtp, pg_ref, None)

    tick(2 + BWD_TICKS)

    @pl.when(step == steps - 1)
    def _():
        out = carry(sums, done, buf_ref, copy_sem, True)
        for x in out:
            x.start()
        own_y.wait()
        for o in range(1, nx):
            for i in range(z.nb):
                send(o, i).wait()
        for x in out:
            x.wait()


def bit_list(count, axis):
    return [(axis, b) for b in range(count.bit_length() - 1)]


def n_bits(count):
    return count.bit_length() - 1


def stage_costs(nx, ny, rounds, size):
    xs = n_bits(ny) // 2
    costs, share = [], size
    for group in rounds:
        share /= 1 << len(group)
        wire = {}
        if group == (("gx", 0),):
            costs.append((2.5, wire))
            continue
        for axis, b in group:
            name, far = ("y", b > 1) if axis == "gx" else ("x", b > 0) if b < xs else ("z", b > xs)
            wire[name] = max(wire.get(name, 0.0), (8 if far else 4) * share / 85e3)
        costs.append((LATENCY_US, wire))
    return costs + costs[::-1]


class Mesh2:
    def __init__(self, nx, ny):
        self.n = {"gx": nx, "gy": ny}
        self.at = {"gx": lax.axis_index("gx"), "gy": lax.axis_index("gy")}

    def bit(self, which):
        axis, b = which
        return lax.rem(self.at[axis] // (1 << b), 2)

    def flips(self, group):
        return [
            [which for i, which in enumerate(group) if m >> (len(group) - 1 - i) & 1]
            for m in range(1, 1 << len(group))
        ]

    def partner(self, flipped):
        at = dict(self.at)
        for axis, b in flipped:
            at[axis] = at[axis] + (1 - 2 * self.bit((axis, b))) * (1 << b)
        return (at["gx"], at["gy"])

    def share(self, group, flipped=()):
        index = 0
        for which in group:
            bit = self.bit(which)
            index = 2 * index + (1 - bit if which in flipped else bit)
        return index

    def beside(self, o):
        return (lax.rem(self.at["gx"] + o, self.n["gx"]), self.at["gy"])

    def barrier(self, rounds, row=False):
        sem = pltpu.get_barrier_semaphore()
        sets = []
        for group in rounds:
            sets += [x for x in self.flips(group) if sorted(x) not in [sorted(y) for y in sets]]
        if row:
            sets = [x for x in sets if any(axis == "gy" for axis, _ in x)]
        others = [self.partner(x) for x in sets]
        if row:
            others += [self.beside(o) for o in range(1, self.n["gx"])]
        for other in others:
            pl.semaphore_signal(sem, inc=1, device_id=other, device_id_type=pl.DeviceIdType.MESH)
        pl.semaphore_wait(sem, len(others))


def routes_of(nx, ny):
    core, ys, g = [("gx", 0)], bit_list(nx, "gx")[1:], bit_list(ny, "gy")
    xs, zs = g[: len(g) // 2], g[len(g) // 2 :]
    if len(g) == 3:
        xs, zs = g[:1], g[1:]
    plane = [tuple(x) for x in zip(ys, xs)]
    line = [tuple(zs)]
    first = [tuple(core)] + plane + line
    other = [tuple(core)] + [tuple(x) for x in zip(xs, zs)]
    left = [x for x in ys + g if not any(x in group for group in other)]
    while left:
        other.append(tuple(left[:2]))
        left = left[2:]
    return first, other


def all_rounds(nx, ny):
    first, other = routes_of(nx, ny)
    return first + other


def place_of(order, nx, ny, dev):
    gx, gy = dev // ny, dev % ny
    p = 0
    for axis, b in order:
        p = 2 * p + (((gx if axis == "gx" else gy) >> b) & 1)
    return p


def flat(rounds):
    return [which for group in rounds for which in group]


def remote(mesh, src, dst, sems, i, flipped):
    return pltpu.make_async_remote_copy(
        src_ref=src, dst_ref=dst, send_sem=sems.at[0, i], recv_sem=sems.at[1, i],
        device_id=mesh.partner(flipped), device_id_type=pl.DeviceIdType.MESH,
    )


def sems_of(rounds):
    return sum((1 << len(group)) - 1 for group in rounds)


class Sum:
    def __init__(self, mesh, buf, start, rows, rounds, recv, recv_start, sems, sem0, full=None):
        self.mesh, self.buf, self.rounds, self.sems, self.sem0 = mesh, buf, rounds, sems, sem0
        self.recv, self.recv0, self.first, self.total = recv, recv_start, start, rows
        self.full = full
        self.n = len(rounds)
        self.stages = self.n * (2 if full is not None else 1)

    def held(self, s):
        off, rows = self.first, self.total
        for group in self.rounds[:s]:
            rows //= 1 << len(group)
            off = off + self.mesh.share(group) * rows
        return off, rows

    def recv_base(self, s):
        rows, base = self.total, self.recv0
        for group in self.rounds[:s]:
            part = rows >> len(group)
            base += rows - part
            rows = part
        return base

    def copies(self, s):
        back = s >= self.n
        r = 2 * self.n - 1 - s if back else s
        group = self.rounds[r]
        sem = self.sem0 + (sems_of(self.rounds) if back else 0) + sems_of(self.rounds[:r])
        off, rows = self.held(r)
        part = rows >> len(group)
        out = []
        for i, flipped in enumerate(self.mesh.flips(group)):
            if back:
                mine = pl.multiple_of(off + self.mesh.share(group) * part, 16)
                src = dst = self.full.at[pl.ds(mine, part)]
            else:
                theirs = pl.multiple_of(off + self.mesh.share(group, flipped) * part, 16)
                src = self.buf.at[pl.ds(theirs, part)]
                dst = self.recv.at[pl.ds(self.recv_base(r) + i * part, part)]
            out.append(remote(self.mesh, src, dst, self.sems, sem + i, flipped))
        return out

    def start(self, s):
        for x in self.copies(s):
            x.start()

    def finish(self, s):
        for x in self.copies(s):
            x.wait()
        if s < self.n:
            off, part = self.held(s + 1)
            base = self.recv_base(s)
            count = (1 << len(self.rounds[s])) - 1
            step = math.gcd(part, 64)
            into = self.full if s == self.n - 1 and self.full is not None else self.buf

            def add(i, _):
                mine = pl.ds(pl.multiple_of(off + i * step, 16), step)
                total = self.buf[mine, :].astype(F32)
                for j in range(count):
                    theirs = pl.ds(pl.multiple_of(base + j * part + i * step, 16), step)
                    total = total + self.recv[theirs, :].astype(F32)
                into[mine, :] = total.astype(BF16)
                return 0

            lax.fori_loop(0, part // step, add, 0)


def carry(sums, done, where, sem, out):
    copies = []
    for x, s in zip(sums, done):
        off, rows = x.held(min(s, 2 * x.n - s))
        rows = pl.ds(pl.multiple_of(off, 16), rows)
        mine = (x.buf if s < x.n else x.full).at[rows]
        src, dst = (mine, where.at[rows]) if out else (where.at[rows], mine)
        copies.append(pltpu.make_async_copy(src, dst, sem.at[len(copies)]))
    return copies


def plan(ready, done, stages, cost, slots, end, share=1.0):
    acts = [[] for _ in slots]
    done = list(done)
    running = [None] * len(done)
    free = {"x": 0.0, "y": 0.0, "z": 0.0}
    rate = {"x": 1.0, "y": share, "z": 1.0}
    for i, now in enumerate(slots):
        last = i == len(slots) - 1
        for j in range(len(done)):
            if ready[j] > now:
                continue
            stop = None
            if running[j] is not None:
                if now < running[j] and not last:
                    continue
                stop = done[j]
                done[j] += 1
                running[j] = None
            go = None
            if done[j] < stages and not last:
                latency, wire = cost[j][done[j]]
                over = max([now] + [max(free[c], now) + wire[c] / rate[c] for c in wire]) + latency
                if over <= end + SLACK_US:
                    go = done[j]
                    running[j] = over
                    for c in wire:
                        free[c] = max(free[c], now) + wire[c] / rate[c]
            if stop is not None or go is not None:
                acts[i].append((j, stop, go))
    return acts, done


def act(sums, acts):
    for j, stop, go in acts:
        if stop is not None:
            sums[j].finish(stop)
        if go is not None:
            sums[j].start(go)


class Gather:
    def __init__(self, mesh, buf, rows, rounds, sems, sem0):
        self.mesh, self.buf, self.rounds, self.sems, self.sem0 = mesh, buf, rounds, sems, sem0
        self.block = rows
        self.stages = len(rounds)

    def held(self, s):
        off, rows = 0, self.block << len(flat(self.rounds))
        for group in self.rounds[: self.stages - s]:
            rows >>= len(group)
            off = off + self.mesh.share(group) * rows
        return pl.multiple_of(off, 16), rows

    def copies(self, s):
        group = self.rounds[self.stages - 1 - s]
        here = self.buf.at[pl.ds(*self.held(s))]
        sem = self.sem0 + sems_of(self.rounds[: self.stages - 1 - s])
        return [
            remote(self.mesh, here, here, self.sems, sem + i, flipped)
            for i, flipped in enumerate(self.mesh.flips(group))
        ]

    def start(self, s):
        for x in self.copies(s):
            x.start()

    def finish(self, s):
        for x in self.copies(s):
            x.wait()


def region_bwd_kernel(
    z, nx, ny, done,
    dt0_ref, all_ref, o_ref, of_ref, p_ref, kv_ref, nr_ref, q_ref, nown_ref, own_ref, ord_ref, gain_ref,
    w_ref, wo_ref, gwq_ref, gwo_ref, smalla_ref, smallm_ref, gbu_ref, part_ref, y_ref,
    mlp_ref, att_ref, vec_ref, dnr_ref, dt0a_ref, dnown_ref, yin_ref,
    dobd, qbd, delta, acc, gacc, small, buf, recv, full, abuf, arecv, afull, vbuf, dbuf, drecv,
    sems, asems, ysems, copy_sem,
):
    step = pl.program_id(0)
    steps = pl.num_programs(0)
    mesh = Mesh2(nx, ny)
    d = z.d
    kc = all_ref.shape[0]
    nq = HEADS * z.w
    n = nx * ny
    scale = z.hd ** (-0.5)
    rest = mlp_sums(mesh, z, buf, recv, full, sems)
    first, other = routes_of(nx, ny)
    last = long_first(first)
    order_d = flat(first)
    bits = len(order_d)
    lane = lax.broadcasted_iota(jnp.int32, (z.w, d), 1) // z.hd

    late = pl.ds(z.early, z.r - z.early)

    def send(o):
        return pltpu.make_async_remote_copy(
            src_ref=y_ref.at[o, late], dst_ref=yin_ref.at[o], send_sem=ysems.at[0, o],
            recv_sem=ysems.at[1, o], device_id=mesh.beside(nx - o),
            device_id_type=pl.DeviceIdType.MESH,
        )

    own_y = pltpu.make_async_copy(y_ref.at[0, late], yin_ref.at[0], ysems.at[0, 0])

    sums, sem0 = [], bits
    split = max(x for x in (1, 2, 4) if (4 * d // x) % (16 * n) == 0 or x == 1)
    for i in range(split):
        rows = 4 * d // split
        rounds = first if i < 3 else last
        sums.append(Sum(mesh, abuf, i * rows, rows, rounds, arecv, i * rows, asems, sem0, afull))
        sem0 += 2 * sems_of(rounds)
    sums.append(Sum(mesh, dbuf, 0, n * z.w, first, drecv, 0, asems, sem0))

    @pl.when(step == 0)
    def _():
        fetch = carry(rest, done, part_ref, copy_sem, False)
        for x in fetch:
            x.start()
        mesh.barrier(all_rounds(nx, ny), row=True)
        for x in fetch:
            x.wait()
        for x, s in zip(rest, done):
            if s < x.stages:
                x.start(s)
        for o in range(1, nx):
            send(o).start()
        own_y.start()
        dt0 = jnp.concatenate([dt0_ref[c, : z.k, :] for c in range(z.nb)], axis=0)
        sel_t = one_hot_t(ord_ref[...], z.w).astype(F32)
        dt0 = jnp.dot(sel_t, dt0, precision=HIGH, preferred_element_type=F32)
        dt0a_ref[...] = dt0
        gr = dt0.astype(BF16)
        abuf[3 * d :, :] = (gwo_ref[...] + mm_tn(o_ref[...], gr)).astype(BF16)
        do = mm_nt(gr, wo_ref[...]).astype(BF16)
        zero = jnp.zeros_like(do)
        q = q_ref[...]
        for h in range(HEADS):
            dobd[h * z.w : (h + 1) * z.w, :] = jnp.where(lane == h, do, zero)
            qbd[h * z.w : (h + 1) * z.w, :] = jnp.where(lane == h, q, zero)
        prod = do.astype(F32) * of_ref[...]
        spread_prod = jnp.concatenate([jnp.where(lane == h, prod, 0.0) for h in range(HEADS)], axis=0)
        delta[...] = lax.dot_general(
            jnp.ones((8, d), F32), spread_prod, (((1,), (1,)), ((), ())), precision=HIGH,
            preferred_element_type=F32,
        )
        small[...] = jnp.zeros_like(small)
        small[2:3, :] = colsum(gr.astype(F32))
        acc[...] = jnp.zeros_like(acc)
        gacc[...] = gwq_ref[...]

    p = p_ref[...]
    ds = (p.astype(F32) * (mm_nt(kv_ref[:, d:], dobd[...]) - delta[0:1, :])).astype(BF16)
    dv = mm(p, dobd[...]).astype(BF16)
    dk = (mm(ds, qbd[...]) * scale).astype(BF16)
    dkv = jnp.concatenate([dk, dv], axis=1)
    gacc[:, d:] += mm_tn(nr_ref[...], dkv)
    dn = mm_nt(dkv, w_ref[:, d:])
    acc[...] += mm_tn(ds, kv_ref[:, :d])
    hat, _ = norm_stats(all_ref[...].astype(F32))
    small[0:1, :] += colsum(dn * hat)
    small[1:2, :] += colsum(dn)
    per = kc // z.w
    for j in range(per):
        dev = step * per + j
        at = {"gx": dev // ny, "gy": lax.rem(dev, ny)}
        place = 0
        for axis, b in order_d:
            place = 2 * place + lax.rem(at[axis] // (1 << b), 2)
        dbuf[pl.ds(pl.multiple_of(place * z.w, 16), z.w), :] = dn[j * z.w : (j + 1) * z.w].astype(BF16)

    @pl.when(step == steps - 1)
    def _():
        sums[split].start(0)
        dq = acc[(HEADS - 1) * z.w :, :]
        for h in range(HEADS - 2, -1, -1):
            dq = jnp.where(lane == h, acc[h * z.w : (h + 1) * z.w, :], dq)
        dq = (dq * scale).astype(BF16)
        abuf[:d, :] = (gacc[:, :d] + mm_tn(nown_ref[...], dq)).astype(BF16)
        for f in range(1, 3):
            abuf[f * d : (f + 1) * d, :] = gacc[:, f * d : (f + 1) * d].astype(BF16)
        for x in sums[:split]:
            x.start(0)
        dnown = mm_nt(dq, w_ref[:, :d])
        dnown_ref[...] = dnown
        hat, _ = norm_stats(own_ref[...].astype(F32))
        vbuf[0] = jnp.zeros_like(vbuf[0])
        vbuf[0, 0:1, :] = smalla_ref[0:1, :] + small[0:1, :] + colsum(dnown * hat)
        vbuf[0, 1:2, :] = smalla_ref[1:2, :] + small[1:2, :] + colsum(dnown)
        vbuf[0, 2:3, :] = smallm_ref[3:4, :] + small[2:3, :]
        vbuf[0, 3:6, :] = smallm_ref[0:3, :]
        row = 6
        for f in range(MLP_PARTS):
            for i in range(gbu_ref.shape[2] // d):
                vbuf[0, row : row + 1, :] = gbu_ref[f, :, i * d : (i + 1) * d]
                row += 1
        queue = [(x, 0) for x in sums[split:] + sums[:split]]
        queue += [(x, s) for x, s in zip(rest, done) if s < x.stages]
        vec = None
        for s in range(max(bits, 2 * len(first)) + 1):
            for x, s0 in queue:
                if s and s0 + s - 1 < x.stages:
                    x.finish(s0 + s - 1)
                if s and s0 + s < x.stages:
                    x.start(s0 + s)
            if s <= bits:
                if s:
                    vec.wait()
                    vbuf[2 * s] = vbuf[2 * s - 2] + vbuf[2 * s - 1]
                if s < bits:
                    vec = remote(mesh, vbuf.at[2 * s], vbuf.at[2 * s + 1], asems, s, [order_d[s]])
                    vec.start()
        vec_ref[...] = vbuf[2 * bits]
        dnr_ref[...] = dbuf[pl.ds(pl.multiple_of(sums[split].held(len(first))[0], 16), z.w), :]
        outs = [
            pltpu.make_async_copy(full, mlp_ref, copy_sem.at[0]),
            pltpu.make_async_copy(afull, att_ref, copy_sem.at[1]),
        ]
        for x in outs:
            x.start()
        own_y.wait()
        for o in range(1, nx):
            send(o).wait()
        for x in outs:
            x.wait()


def finish_kernel(
    z, mlp_ref, att_ref, vec_ref, early_ref, late_ref, code_ref, own_ref, dnr_ref, dnown_ref, dt0a_ref, gain_ref,
    out_ref, first_ref, rg_ref, gwu_ref, gwd_ref, gwq_ref, gwo_ref, gbu_ref, *rows,
):
    f = pl.program_id(0)
    fc = gwd_ref.shape[0]
    d = z.d
    gwd_ref[...] = mlp_ref[:fc, :].astype(F32)
    for i in range(fc // d):
        gwu_ref[:, i * d : (i + 1) * d] = mlp_ref[fc + i * d : fc + (i + 1) * d, :].astype(F32)

    @pl.when(f < 3)
    def _():
        gwq_ref[...] = att_ref[...].astype(F32)

    @pl.when(f == 3)
    def _():
        gwo_ref[...] = att_ref[...].astype(F32)

    @pl.when(f == 0)
    def _():
        for i, row in enumerate(rows):
            row[...] = vec_ref[i : i + 1, :]
        gbu_ref[...] = vec_ref[6 : 6 + gbu_ref.shape[0], :]
        hat, rstd = norm_stats(own_ref[...].astype(F32))
        dn = dnr_ref[...].astype(F32) + dnown_ref[...]
        rg_ref[...] = (dt0a_ref[...] + norm_back(hat, rstd, gain_ref[...], dn)).astype(BF16)

    for step in range(MLP_PARTS):

        @pl.when(f == step)
        def _():
            sel_t = one_hot_t(code_ref[...], z.gp * z.w)
            for g in range(z.ng * step // MLP_PARTS, z.ng * (step + 1) // MLP_PARTS):
                rows = z.gp * z.k
                at = z.early // rows
                src, i = (early_ref, g) if g < at else (late_ref, g - at)
                unpack_group(z, g, sel_t, src, out_ref, first_ref, i)


def local(
    patches, regions, send_order, image_windows, attn_gain, attn_shift, w_qkv, w_out, b_out,
    mlp_gain, mlp_shift, w_up, b_up, w_down, b_down, upstream_patches, upstream_regions,
):
    nx, ny = lax.axis_size("gx"), lax.axis_size("gy")
    z = Sizes(patches.shape[0], patches.shape[1], patches.shape[2], nx)
    ff = w_up.shape[1]
    n = z.w * nx * ny
    gx = lax.axis_index("gx")
    dev = gx * ny + lax.axis_index("gy")
    sds = jax.ShapeDtypeStruct

    order = lax.dynamic_slice_in_dim(send_order, dev, 1, 0)[0].reshape(nx, z.k)
    tile = jnp.arange(nx, dtype=jnp.int32)
    order_t = jnp.take(order, (gx - tile) % nx, axis=0)
    place = jnp.arange(z.gp, dtype=jnp.int32) * z.w
    code_x = (order_t[:, None, :] + place[None, :, None]).reshape(-1)
    block = ((gx + tile) % nx)[:, None] * z.k + jnp.arange(z.k, dtype=jnp.int32)[None, :]
    code_e = (block[:, None, :] + place[None, :, None]).reshape(-1)
    order_t = order_t.reshape(-1)
    bounds = jnp.cumsum(image_windows)
    gain, shift = attn_gain[None], attn_shift[None]

    x_t = jnp.transpose(patches, (1, 0, 2))
    e_t = jnp.transpose(upstream_patches, (1, 0, 2))

    bits = n_bits(nx * ny)
    anywhere = pl.BlockSpec(memory_space=pl.ANY)
    vmem = pl.BlockSpec(memory_space=pltpu.VMEM)
    *packed, xp, qkv, regions_all = pl.pallas_call(
        functools.partial(start_kernel, z, nx, ny),
        in_specs=[anywhere, anywhere] + [vmem] * 7,
        out_specs=[vmem] * (z.nb + 1) + [anywhere, vmem],
        out_shape=[sds((z.r, z.d), BF16)] * z.nb + [
            sds((z.nb, z.r, z.d), BF16),
            sds((z.nb, z.r, 3 * z.d), BF16),
            sds((n, z.d), BF16),
        ],
        scratch_shapes=[
            pltpu.VMEM((z.tok, z.w, z.d), BF16),
            pltpu.VMEM((z.tok, z.w, z.d), BF16),
            pltpu.VMEM((z.nb, z.r, 3 * z.d), BF16),
            pltpu.VMEM((z.r, z.d), BF16),
            pltpu.VMEM((n, z.d), BF16),
            pltpu.SemaphoreType.DMA((2, sems_of(routes_of(nx, ny)[0]))),
            pltpu.SemaphoreType.DMA((2,)),
            pltpu.SemaphoreType.DMA((z.nb,)),
        ],
        compiler_params=params(collective_id=0, has_side_effects=True),
        name="start",
    )(x_t, e_t, upstream_regions, code_x[None], code_e[None], gain, shift, w_qkv, regions)

    e_in = [packed[0]]
    for o in range(1, nx):
        e_in.append(lax.ppermute(packed[o], "gx", [(i, (i + o) % nx) for i in range(nx)]))

    kc = 8 * z.w
    nq = HEADS * z.w
    r2, p_r, kv_all, nr_all, q_r, o_r, o_f, n_own = pl.pallas_call(
        functools.partial(region_fwd_kernel, z, kc, ny),
        in_specs=[vmem, vmem, pl.BlockSpec(memory_space=pltpu.SMEM)] + [vmem] * 6,
        out_shape=(
            sds((z.nb, z.kp, z.d), F32),
            sds((n, nq), BF16),
            sds((n, 2 * z.d), BF16),
            sds((n, z.d), BF16),
            sds((z.w, z.d), BF16),
            sds((z.w, z.d), BF16),
            sds((z.w, z.d), F32),
            sds((z.w, z.d), BF16),
        ),
        scratch_shapes=[pltpu.VMEM((n, nq), F32)],
        compiler_params=params(),
        name="region_fwd",
    )(
        regions_all, regions, bounds, order_t[None], gain, shift, w_qkv, w_out, b_out[None],
    )

    def tiled(*shape):
        return pl.BlockSpec((1,) + shape, lambda i: (i,) + (0,) * len(shape))

    def grouped(*shape):
        return pl.BlockSpec((z.k,) + shape, lambda i: (i,) + (0,) * len(shape))

    cols = z.per_group * SEG
    t2, p_w, qw, o_w = pl.pallas_call(
        functools.partial(local_fwd_kernel, z),
        grid=(z.nb,),
        in_specs=[
            tiled(z.r, 3 * z.d), tiled(z.r, z.d), tiled(z.kp, z.d), whole(1, z.d), whole(1, z.d),
            whole(z.d, 3 * z.d), whole(z.d, z.d), whole(1, z.d),
        ],
        out_specs=[
            tiled(z.r, z.d), grouped(z.groups, SEG, cols), grouped(3 * z.groups, SEG, LANES),
            tiled(z.r, z.d),
        ],
        out_shape=(
            sds((z.nb, z.r, z.d), F32),
            sds((z.w, z.groups, SEG, cols), BF16),
            sds((z.w, 3 * z.groups, SEG, LANES), BF16),
            sds((z.nb, z.r, z.d), BF16),
        ),
        scratch_shapes=[
            pltpu.VMEM((3 * z.groups, z.wide, LANES), F32),
            pltpu.VMEM((z.groups, z.wide, LANES), F32),
        ],
        compiler_params=params(),
        name="local_fwd",
    )(qkv, xp, r2, gain, shift, w_qkv, w_out, b_out[None])

    parts = MLP_PARTS
    fc = ff // parts
    total = 2 * ff
    first, other = routes_of(nx, ny)
    stages = 2 * len(first)
    n_sums = mlp_count(nx, ny, total)
    cost = [stage_costs(nx, ny, mlp_route(nx, ny, i, n_sums), total // n_sums * z.d * 2) for i in range(n_sums)]
    n_sems = sum(2 * sems_of(mlp_route(nx, ny, i, n_sums)) for i in range(n_sums))
    head, part_us, tail_us = 11.0, MLP_US / parts, 7.0
    slots = []
    for i in range(parts):
        base = head + part_us * i
        slots += [base + part_us * x for x in (0.0, 0.3, 0.55, 0.8, 0.8, 0.9, 1.0)]
        slots.append(base + part_us + (tail_us if i == parts - 1 else 0.0))
    acts_m, done_m = plan(
        [mlp_ready(i, n_sums, head, part_us) - 0.05 for i in range(n_sums)], [0] * n_sums, stages, cost,
        slots, slots[-1],
    )
    keep = dict(pipeline_mode=pl.Buffered(1))

    def once(*shape):
        return pl.BlockSpec(shape, lambda *_: (0,) * len(shape), **keep)

    y, gt, part_sums, small_m, gbu = pl.pallas_call(
        functools.partial(mlp_kernel, z, nx, ny, acts_m, tuple(done_m)),
        grid=(parts,),
        in_specs=[pl.BlockSpec(memory_space=pl.ANY)] * (1 + z.nb) + [
            once(1, z.d), once(1, z.d), pl.BlockSpec((z.d, fc), lambda f: (0, f)),
            pl.BlockSpec((1, fc), lambda f: (0, f)), pl.BlockSpec((fc, z.d), lambda f: (f, 0)),
            once(1, z.d),
        ],
        out_specs=[
            anywhere, anywhere, anywhere, once(8, z.d),
            pl.BlockSpec((1, 1, fc), lambda f: (f, 0, 0)),
        ],
        out_shape=(
            sds((z.t, z.d), BF16),
            sds((z.t, z.d), BF16),
            sds((total, z.d), BF16),
            sds((8, z.d), F32),
            sds((parts, 1, fc), F32),
        ),
        scratch_shapes=[
            pltpu.VMEM((z.tp, z.d), BF16),
            pltpu.VMEM((z.tp, z.d), BF16),
            pltpu.VMEM((z.d + 16, z.tp), BF16),
            pltpu.VMEM((z.d + 16, z.tp), BF16),
            pltpu.VMEM((z.m, fc), F32),
            pltpu.VMEM((z.m, fc), F32),
            pltpu.VMEM((z.m, fc), F32),
            pltpu.VMEM((z.m, fc), F32),
            pltpu.VMEM((z.tp, fc), BF16),
            pltpu.VMEM((z.tp, fc), BF16),
            pltpu.VMEM((z.t, z.d), F32),
            pltpu.VMEM((z.t, z.d), F32),
            pltpu.VMEM((total, z.d), BF16),
            pltpu.VMEM((total, z.d), BF16),
            pltpu.VMEM((total, z.d), BF16),
            pltpu.SemaphoreType.DMA((2, n_sems)),
            pltpu.SemaphoreType.DMA((24,)),
        ],
        compiler_params=params(collective_id=1, has_side_effects=True),
        name="mlp",
    )(
        t2.reshape(z.t, z.d), *e_in, mlp_gain[None], mlp_shift[None], w_up, b_up[None], w_down,
        b_down[None],
    )
    y, gt = y.reshape(z.nb, z.r, z.d), gt.reshape(z.nb, z.r, z.d)

    head, part_us, tail_us = 2.0, BWD_US / z.nb, 2.0
    slots = []
    for i in range(z.nb):
        base = head + part_us * i
        slots += [base + part_us * x for x in (0.0, 0.3, 0.5, 0.7, 1.0)]
        slots.append(base + part_us + (tail_us if i == z.nb - 1 else 0.0))
    acts_b, done = plan([0.0] * n_sums, done_m, stages, cost, slots, slots[-1], 0.6)
    patch_grad, dt0, gwq, gwo, small_a, part_sums, y_early = pl.pallas_call(
        functools.partial(local_bwd_kernel, z, nx, ny, acts_b, tuple(done_m), tuple(done)),
        grid=(z.nb,),
        in_specs=[
            tiled(z.r, z.d), tiled(z.r, z.d), tiled(z.kp, z.d), tiled(z.r, z.d),
            grouped(z.groups, SEG, cols), grouped(3 * z.groups, SEG, LANES),
            whole(1, z.nb * z.gp * z.k), whole(1, z.d), whole(1, z.d), whole(z.d, 3 * z.d),
            whole(z.d, z.d), anywhere, anywhere,
        ],
        out_specs=[
            once(z.tok, z.w, z.d), tiled(z.kp, z.d), once(z.d, 3 * z.d), once(z.d, z.d),
            once(8, z.d), anywhere, anywhere,
        ],
        out_shape=(
            sds((z.tok, z.w, z.d), BF16),
            sds((z.nb, z.kp, z.d), F32),
            sds((z.d, 3 * z.d), F32),
            sds((z.d, z.d), F32),
            sds((8, z.d), F32),
            sds((total, z.d), BF16),
            sds((z.nb, z.early, z.d), BF16),
        ),
        scratch_shapes=[
            pltpu.VMEM((z.groups, z.wide, LANES), F32),
            pltpu.VMEM((3 * z.groups, z.wide, LANES), F32),
            pltpu.VMEM((z.r, 3 * z.d), BF16),
            pltpu.VMEM((z.nb, z.r, z.d), BF16),
            pltpu.VMEM((total, z.d), BF16),
            pltpu.VMEM((total, z.d), BF16),
            pltpu.VMEM((total, z.d), BF16),
            pltpu.SemaphoreType.DMA((2, n_sems)),
            pltpu.SemaphoreType.DMA((2, nx * z.nb)),
            pltpu.SemaphoreType.DMA((n_sums,)),
        ],
        compiler_params=params(collective_id=2, has_side_effects=True),
        name="local_bwd",
    )(gt, xp, r2, o_w, p_w, qw, code_x[None], gain, shift, w_qkv, w_out, part_sums, y)

    def keys(*shape):
        return pl.BlockSpec((kc,) + shape, lambda i: (i,) + (0,) * len(shape))

    mlp_total, att_total, vec, dnr, dt0a, dn_own, y_late = pl.pallas_call(
        functools.partial(region_bwd_kernel, z, nx, ny, tuple(done)),
        grid=(n // kc,),
        in_specs=[
            once(z.nb, z.kp, z.d), keys(z.d), once(z.w, z.d), once(z.w, z.d), keys(nq), keys(2 * z.d),
            keys(z.d), once(z.w, z.d), once(z.w, z.d), once(z.w, z.d), once(1, z.w), once(1, z.d),
            once(z.d, 3 * z.d), once(z.d, z.d), once(z.d, 3 * z.d), once(z.d, z.d), once(8, z.d),
            once(8, z.d), once(parts, 1, fc), anywhere, anywhere,
        ],
        out_specs=[
            anywhere, anywhere, once(16, z.d), once(z.w, z.d), once(z.w, z.d), once(z.w, z.d), anywhere,
        ],
        out_shape=(
            sds((total, z.d), BF16),
            sds((4 * z.d, z.d), BF16),
            sds((16, z.d), F32),
            sds((z.w, z.d), BF16),
            sds((z.w, z.d), F32),
            sds((z.w, z.d), F32),
            sds((z.nb, z.r - z.early, z.d), BF16),
        ),
        scratch_shapes=[
            pltpu.VMEM((nq, z.d), BF16),
            pltpu.VMEM((nq, z.d), BF16),
            pltpu.VMEM((8, nq), F32),
            pltpu.VMEM((nq, z.d), F32),
            pltpu.VMEM((z.d, 3 * z.d), F32),
            pltpu.VMEM((8, z.d), F32),
            pltpu.VMEM((total, z.d), BF16),
            pltpu.VMEM((total, z.d), BF16),
            pltpu.VMEM((total, z.d), BF16),
            pltpu.VMEM((4 * z.d, z.d), BF16),
            pltpu.VMEM((4 * z.d, z.d), BF16),
            pltpu.VMEM((4 * z.d, z.d), BF16),
            pltpu.VMEM((2 * bits + 1, 16, z.d), F32),
            pltpu.VMEM((n, z.d), BF16),
            pltpu.VMEM((n, z.d), BF16),
            pltpu.SemaphoreType.DMA((2, n_sems)),
            pltpu.SemaphoreType.DMA((2, bits + 9 * sems_of(first))),
            pltpu.SemaphoreType.DMA((2, nx)),
            pltpu.SemaphoreType.DMA((max(n_sums, 2),)),
        ],
        compiler_params=params(collective_id=3, has_side_effects=True),
        name="region_bwd",
    )(
        dt0, regions_all, o_r, o_f, p_r, kv_all, nr_all, q_r, n_own, regions, order_t[None], gain, w_qkv,
        w_out, gwq, gwo, small_a, small_m, gbu, part_sums, y,
    )

    out_p, out_r, region_grad, gwu, gwd, gwq, gwo, gbu, *rows = pl.pallas_call(
        functools.partial(finish_kernel, z),
        grid=(parts,),
        in_specs=[
            pl.BlockSpec((2 * fc, z.d), lambda f: (f, 0)), pl.BlockSpec((z.d, z.d), lambda f: (f, 0)),
            once(16, z.d), once(z.nb, z.early, z.d), once(z.nb, z.r - z.early, z.d), once(1, z.nb * z.gp * z.k), once(z.w, z.d),
            once(z.w, z.d), once(z.w, z.d), once(z.w, z.d), once(1, z.d),
        ],
        out_specs=[
            once(z.tok, z.w, z.d), once(z.w, z.d), once(z.w, z.d),
            pl.BlockSpec((z.d, fc), lambda f: (0, f)), pl.BlockSpec((fc, z.d), lambda f: (f, 0)),
            pl.BlockSpec((z.d, z.d), lambda f: (0, jnp.minimum(f, 2))), once(z.d, z.d),
            once(ff // z.d, z.d),
        ] + [once(1, z.d)] * 6,
        out_shape=[
            sds((z.tok, z.w, z.d), BF16), sds((z.w, z.d), BF16), sds((z.w, z.d), BF16),
            sds((z.d, ff), F32), sds((ff, z.d), F32), sds((z.d, 3 * z.d), F32), sds((z.d, z.d), F32),
            sds((ff // z.d, z.d), F32),
        ] + [sds((1, z.d), F32)] * 6,
        compiler_params=params(),
        name="finish",
    )(mlp_total, att_total, vec, y_early, y_late, code_e[None], regions, dnr, dn_own, dt0a, gain)
    rows = [x[0] for x in rows]
    return (
        jnp.transpose(out_p, (1, 0, 2)),
        out_r,
        jnp.transpose(patch_grad, (1, 0, 2)),
        region_grad,
        rows[0],
        rows[1],
        gwq,
        gwo,
        rows[2],
        rows[3],
        rows[4],
        gwu,
        gbu.reshape(ff),
        gwd,
        rows[5],
    )


def solution(mesh):
    split = ("gx", "gy")
    rows3, rows2, full = P(split, None, None), P(split, None), P()
    in_specs = (rows3, rows2) + (full,) * 13 + (rows3, rows2)
    out_specs = (rows3, rows2, rows3, rows2) + (full,) * 11
    return jax.shard_map(local, mesh=mesh, in_specs=in_specs, out_specs=out_specs, check_vma=False)
```
